32 devices in a mesh: dp: 4 (over y, x), fsdp: 8 (over z, core).
Axes of the slice: x: 2, y: 2, z: 4, core: 2. Of those that a mesh axis runs over, the one named last changes fastest.
Arguments:
- tokens: bfloat16 [32, 416, 1024], P(('dp', 'fsdp')), may hold values from -6 to 6
- heads_weight: bfloat16 [1024, 3072], P(('dp', 'fsdp')), may hold values from -0.1875 to 0.1875
- merge_weight: bfloat16 [1024, 1024], P(('dp', 'fsdp')), may hold values from -1.5 to 1.5
- up_weight: bfloat16 [1024, 4096], P(('dp', 'fsdp')), may hold values from -0.1875 to 0.1875
- up_bias: bfloat16 [4096], P(('dp', 'fsdp')), may hold values from -3 to 3
- down_weight: bfloat16 [4096, 1024], P(('dp', 'fsdp')), may hold values from -0.09375 to 0.09375
- down_bias: bfloat16 [1024], P(('dp', 'fsdp')), may hold values from -3 to 3
- norm_gain: bfloat16 [1024], P(('dp', 'fsdp')), may hold values from 0.099609375 to 1.8984375
- norm_bias: bfloat16 [1024], P(('dp', 'fsdp')), may hold values from -3 to 3
- offsets: int32 [32], P(('dp', 'fsdp')), may hold values from 1 to 103
- terminal: int32 [32], P(('dp', 'fsdp')), may hold values from 208 to 415, as said below
- cotangent: bfloat16 [32, 416, 1024], P(('dp', 'fsdp')), may hold values from -6 to 6
Outputs:
- block_output: bfloat16 [32, 416, 1024], P(('dp', 'fsdp'))
- grad_tokens: bfloat16 [32, 416, 1024], P(('dp', 'fsdp'))
- grad_heads: float32 [1024, 3072], P(('dp', 'fsdp'))
- grad_merge: float32 [1024, 1024], P(('dp', 'fsdp'))
- grad_up: float32 [1024, 4096], P(('dp', 'fsdp'))
- grad_up_bias: float32 [4096], P(('dp', 'fsdp'))
- grad_down: float32 [4096, 1024], P(('dp', 'fsdp'))
- grad_down_bias: float32 [1024], P(('dp', 'fsdp'))
- grad_gain: float32 [1024], P(('dp', 'fsdp'))
- grad_bias: float32 [1024], P(('dp', 'fsdp'))
The draws below stay inside these ranges and needn't reach their ends.
Inputs may be any that keep to these rules, and one draw needn't show every extreme that they name: Window w holds a protein from offsets[w] to terminal[w]; positions after terminal[w] are padding.
All inputs are finite; a program needn't handle non-finite values.
Results may differ from the reference program's by a relative error of at most 0.011.
Values may be sent and summed in bfloat16 or wider, within the bound.
No kernel may reach another device: no remote copies, remote signals or barrier semaphores. Data moves between devices by JAX's collectives and lax.ppermute only.
A program may use at most 256 MiB of HBM per device.

```python
import jax
import jax.numpy as jnp
from jax import lax

D = 1024
HEADS = 16
HEAD = 64
ROT = 32
FF = 4096
LEN = 416
WINDOWS = 32


def draw_terminal(key, part):
    key = jax.random.fold_in(key, 7)
    first_key, second_key, third_key = jax.random.split(key, 3)
    drawn = jax.random.randint(first_key, (WINDOWS,), LEN // 2, LEN, dtype=jnp.int32)
    highest_slot = jax.random.randint(second_key, (), 0, WINDOWS, dtype=jnp.int32)
    step_ahead = jax.random.randint(third_key, (), 1, WINDOWS, dtype=jnp.int32)
    lowest_slot = (highest_slot + step_ahead) % WINDOWS
    drawn = drawn.at[highest_slot].set(LEN - 1)
    drawn = drawn.at[lowest_slot].set(LEN // 2)
    return drawn


def set_ends(values, rng, smallest, high):
    longest = values.shape.index(max(values.shape))
    spots = []
    for shift in (0, 1):
        where = [jax.random.randint(jax.random.fold_in(rng, axis), (), 0, length) for axis, length in enumerate(values.shape)]
        where[longest] = (where[longest] + shift) % values.shape[longest]
        spots.append(tuple(where))
    return values.at[spots[0]].set(smallest).at[spots[1]].set(high)


def block_scale(key, extent, cuts, low, top_value):
    level, own = 1.0, jax.random.fold_in(key, 6)
    for dim, blocks in cuts:
        steps = jnp.exp(jax.random.uniform(jax.random.fold_in(own, dim), (blocks,), jnp.float32, low / len(cuts), top_value / len(cuts)))
        level = level * jnp.repeat(steps, extent[dim] // blocks).reshape([-1 if axis == dim else 1 for axis in range(len(extent))])
    return level


def bell_draw(rng, shape, scale, limit, pieces=(), kind=jnp.bfloat16):
    level = block_scale(rng, shape, pieces, -0.22, 0.18) if pieces else 1.0
    array = jax.random.normal(rng, shape, jnp.float32) * scale * level
    return jnp.minimum(jnp.maximum(array, -limit), limit).astype(kind)


def setup_inputs(seed: int = 0) -> dict:
    arg_keys = jax.random.split(jax.random.key(seed), 13)
    tokens = bell_draw(arg_keys[0], (WINDOWS, LEN, D), 1.0, 6.0, ((0, 32),))
    heads_weight = bell_draw(arg_keys[1], (D, 3 * D), D ** -0.5, 0.1875, ((0, 32),))
    merge_weight = bell_draw(arg_keys[2], (D, D), (D // 64) ** -0.5, 1.5, ((0, 32),))
    up_weight = bell_draw(arg_keys[3], (D, FF), D ** -0.5, 0.1875, ((0, 32),))
    up_bias = bell_draw(arg_keys[4], (FF,), 0.5, 3.0, ((0, 32),))
    down_weight = bell_draw(arg_keys[5], (FF, D), FF ** -0.5, 0.09375, ((0, 32),))
    down_bias = bell_draw(arg_keys[6], (D,), 0.5, 3.0, ((0, 32),))
    norm_gain = jnp.clip(1.0 + 0.18 * jax.random.normal(arg_keys[7], (D,), jnp.float32), 0.099609375, 1.8984375).astype(jnp.bfloat16)
    norm_bias = bell_draw(arg_keys[8], (D,), 0.5, 3.0, ((0, 32),))
    offsets = set_ends(jax.random.randint(arg_keys[9], (WINDOWS,), 1, LEN // 4), jax.random.fold_in(arg_keys[9], 1), 1, (LEN // 4) - 1).astype(jnp.int32)
    terminal = draw_terminal(jax.random.fold_in(arg_keys[12], 71), 0)
    cotangent = bell_draw(arg_keys[11], (WINDOWS, LEN, D), 1.0, 6.0, ((0, 32),))
    return {"tokens": tokens, "heads_weight": heads_weight, "merge_weight": merge_weight, "up_weight": up_weight, "up_bias": up_bias, "down_weight": down_weight, "down_bias": down_bias, "norm_gain": norm_gain, "norm_bias": norm_bias, "offsets": offsets, "terminal": terminal, "cotangent": cotangent}


@jax.custom_vjp
def low(v):
    return lax.optimization_barrier(v.astype(jnp.bfloat16)).astype(jnp.float32)

@jax.custom_vjp
def low_back(v):
    return v

def low_keep(v):
    return (low(v), None)

def low_pass(kept, grad):
    return (grad,)

def back_keep(v):
    return (v, None)

def back_low(kept, grad):
    return (low(grad),)
low.defvjp(low_keep, low_pass)
low_back.defvjp(back_keep, back_low)
eps = 1e-05
big_negative = -1e+30
gelu_scale = 0.7978845608028654
gelu_cubic = 0.044715
highest = lax.Precision.HIGHEST

def angles(length, rotary):
    position = jnp.arange(length, dtype=jnp.float32)
    exponent = jnp.arange(0, rotary, 2, dtype=jnp.float32) / rotary
    phase = position[:, None] * (1.0 / 10000.0 ** exponent)[None, :]
    return (jnp.cos(phase)[:, None, :], jnp.sin(phase)[:, None, :])

def turn_pairs(values, cosine_table, sine_table, rotary, direction):
    paired = values[..., :rotary].reshape(values.shape[:-1] + (rotary // 2, 2))
    first_half = paired[..., 0]
    second_half = paired[..., 1]
    signed_sine = direction * sine_table
    new_first = first_half * cosine_table - second_half * signed_sine
    new_second = second_half * cosine_table + first_half * signed_sine
    turned = jnp.stack([new_first, new_second], axis=-1).reshape(values.shape[:-1] + (rotary,))
    return jnp.concatenate([turned, values[..., rotary:]], axis=-1)

def allowed_keys(offsets, terminal, length):
    position = jnp.arange(length, dtype=jnp.int32)
    segment = (position[None, :] >= offsets[:, None]).astype(jnp.int32) + (position[None, :] > terminal[:, None]).astype(jnp.int32)
    same_segment = segment[:, :, None] == segment[:, None, :]
    causal = position[:, None] >= position[None, :]
    return (same_segment & causal[None])[:, None, :, :]

def gelu_tanh(values):
    inner = gelu_scale * (values + gelu_cubic * values * values * values)
    return 0.5 * values * (1.0 + jnp.tanh(inner))

def block_forward(residual, heads_weight, merge_weight, up_weight, up_bias, down_weight, down_bias, norm_gain, norm_bias, offsets, terminal):
    windows = residual.shape[0]
    length = residual.shape[1]
    mean_value = lax.optimization_barrier(jnp.mean(residual, axis=-1, keepdims=True))
    centered = residual - mean_value
    inverse_std = lax.rsqrt(lax.optimization_barrier(jnp.mean(centered * centered, axis=-1, keepdims=True)) + eps)
    acts = low(centered * inverse_std * norm_gain + norm_bias)
    mixed = low_back(jnp.einsum('gld,de->gle', acts, heads_weight, precision=highest))
    split_shape = (windows, length, HEADS, HEAD)
    cosine_table, sine_table = angles(length, ROT)
    query = low(turn_pairs(mixed[..., :D].reshape(split_shape), cosine_table, sine_table, ROT, 1.0) * HEAD ** (-0.5))
    keys = low(turn_pairs(mixed[..., D:2 * D].reshape(split_shape), cosine_table, sine_table, ROT, 1.0))
    values = low(mixed[..., 2 * D:].reshape(split_shape))
    scores = low_back(jnp.einsum('gqhe,gkhe->ghqk', query, keys, precision=highest))
    scores = jnp.where(allowed_keys(offsets, terminal, length), scores, big_negative)
    maxes = lax.optimization_barrier(jnp.max(scores, axis=-1, keepdims=True))
    expo = jnp.exp(scores - maxes)
    probs = expo / lax.optimization_barrier(jnp.sum(expo, axis=-1, keepdims=True))
    attended = jnp.einsum('ghqk,gkhe->gqhe', low(probs), values, precision=highest)
    attended = low(low_back(attended.reshape(windows, length, D)))
    attn_out = jnp.einsum('gld,de->gle', attended, merge_weight, precision=highest)
    hidden = low_back(jnp.einsum('gld,df->glf', acts, up_weight, precision=highest) + up_bias)
    activated = low(gelu_tanh(hidden))
    mlp_out = jnp.einsum('glf,fd->gld', activated, down_weight, precision=highest) + down_bias
    return residual + attn_out + mlp_out

def reference(tokens, heads_weight, merge_weight, up_weight, up_bias, down_weight, down_bias, norm_gain, norm_bias, offsets, terminal, cotangent):
    weights = tuple((weight.astype(jnp.float32) for weight in (heads_weight, merge_weight, up_weight, up_bias, down_weight, down_bias, norm_gain, norm_bias)))
    group_size = 8
    group_count = tokens.shape[0] // group_size
    length = tokens.shape[1]

    def scan_step(totals, inputs):
        tok_group, cot_group, off_group, term_group = inputs

        def forward_fn(residual, *params):
            return block_forward(residual, *params, off_group, term_group)
        result, pullback = jax.vjp(forward_fn, tok_group.astype(jnp.float32), *weights)
        gradients = pullback(cot_group.astype(jnp.float32))
        totals = tuple((total + gradient for total, gradient in zip(totals, gradients[1:])))
        return (totals, (result.astype(jnp.bfloat16), gradients[0].astype(jnp.bfloat16)))
    initial = tuple((jnp.zeros_like(weight) for weight in weights))
    totals, (outputs, input_grads) = lax.scan(scan_step, initial, (tokens.reshape(group_count, group_size, length, D), cotangent.reshape(group_count, group_size, length, D), offsets.reshape(group_count, group_size), terminal.reshape(group_count, group_size)))
    block_output = outputs.reshape(tokens.shape)
    grad_tokens = input_grads.reshape(tokens.shape)
    return (block_output, grad_tokens, totals[0], totals[1], totals[2], totals[3], totals[4], totals[5], totals[6], totals[7])
```

```python
import functools

import jax
import jax.numpy as jnp
import numpy as np
from jax import lax
from jax.experimental import pallas as pl
from jax.experimental.pallas import tpu as pltpu
from jax.sharding import PartitionSpec as P

HEADS = 16
ROT = 32
CORES = 2
GROUP = 4
AXES = ("dp", "fsdp")

eps = 1e-05
big_negative = -1e30
gelu_scale = 0.7978845608028654
gelu_cubic = 0.044715

bf16 = jnp.bfloat16
f32 = jnp.float32


def turn_tables(length, head, lanes):
    position = np.arange(length, dtype=np.float32)
    exponent = np.arange(0, ROT, 2, dtype=np.float32) / np.float32(ROT)
    rate = (np.float32(1.0) / np.power(np.float32(10000.0), exponent)).astype(np.float32)
    phase = (position[:, None] * rate[None, :]).astype(np.float32)
    cosine = np.ones((length, head), np.float32)
    sine = np.zeros((length, head), np.float32)
    cosine[:, :ROT] = np.repeat(np.cos(phase), 2, axis=1)
    sine[:, :ROT] = np.repeat(np.sin(phase), 2, axis=1)
    sine[:, 0:ROT:2] *= -1.0
    copies = lanes // head
    return np.tile(cosine, (1, copies)), np.tile(sine, (1, copies))


def turned(values, cosine, sine):
    lanes = values.shape[1]
    even = lax.broadcasted_iota(jnp.int32, values.shape, 1) % 2 == 0
    other = jnp.where(even, pltpu.roll(values, lanes - 1, 1), pltpu.roll(values, 1, 1))
    return values * cosine + other * sine


def dot(a, b, dims=((1,), (0,))):
    return lax.dot_general(a, b, (dims, ((), ())), preferred_element_type=f32)


def allowed_pairs(offset, end, length):
    key = lax.broadcasted_iota(jnp.int32, (length, 1), 0)
    query = lax.broadcasted_iota(jnp.int32, (1, length), 1)
    key_part = (key >= offset).astype(jnp.int32) + (key > end).astype(jnp.int32)
    query_part = (query >= offset).astype(jnp.int32) + (query > end).astype(jnp.int32)
    return (key_part == query_part) & (query >= key)


def attend_kernel(head, ends_ref, mixed_ref, cos_ref, sin_ref, qkv_ref, att_ref, lse_ref):
    window = pl.program_id(0)
    length, width = mixed_ref.shape
    width = width // 3
    lanes = cos_ref.shape[1]
    allowed = allowed_pairs(ends_ref[window, 0], ends_ref[window, 1], length)
    cosine, sine = cos_ref[...], sin_ref[...]
    lane = lax.broadcasted_iota(jnp.int32, (1, lanes), 1)
    for group in range(width // lanes):
        at = group * lanes
        query = (
            turned(mixed_ref[:, at : at + lanes], cosine, sine) * head ** (-0.5)
        ).astype(bf16)
        keys = turned(mixed_ref[:, width + at : width + at + lanes], cosine, sine).astype(bf16)
        values = mixed_ref[:, 2 * width + at : 2 * width + at + lanes]
        qkv_ref[:, at : at + lanes] = query
        qkv_ref[:, width + at : width + at + lanes] = keys
        qkv_ref[:, 2 * width + at : 2 * width + at + lanes] = values.astype(bf16)
        values_turned = values.T.astype(bf16)
        outs = []
        for sub in range(lanes // head):
            mine = (lane >= sub * head) & (lane < (sub + 1) * head)
            scores = dot(jnp.where(mine, keys, 0), query, ((1,), (1,)))
            scores = jnp.where(allowed, scores, big_negative)
            top = jnp.max(scores, axis=0, keepdims=True)
            expo = jnp.exp(scores - top)
            total = jnp.sum(expo, axis=0, keepdims=True)
            probs = (expo / total).astype(bf16)
            number = group * (lanes // head) + sub
            lse_ref[0, number : number + 1, :] = top + jnp.log(total)
            outs.append(dot(values_turned[sub * head : (sub + 1) * head, :], probs))
        att_ref[:, at : at + lanes] = jnp.concatenate(outs, axis=0).T.astype(bf16)


def attend_back_kernel(
    head, ends_ref, qkv_ref, grad_ref, lse_ref, cos_ref, sin_ref, out_ref
):
    window = pl.program_id(0)
    length, width = qkv_ref.shape
    width = width // 3
    lanes = cos_ref.shape[1]
    allowed = allowed_pairs(ends_ref[window, 0], ends_ref[window, 1], length)
    cosine, sine = cos_ref[...], -sin_ref[...]
    lane = lax.broadcasted_iota(jnp.int32, (1, lanes), 1)
    for group in range(width // lanes):
        at = group * lanes
        query = qkv_ref[:, at : at + lanes]
        keys = qkv_ref[:, width + at : width + at + lanes]
        values = qkv_ref[:, 2 * width + at : 2 * width + at + lanes]
        grad = grad_ref[:, at : at + lanes]
        keys_turned = keys.astype(f32).T.astype(bf16)
        values_grad = jnp.zeros((length, lanes), f32)
        keys_grad = jnp.zeros((length, lanes), f32)
        query_grads = []
        for sub in range(lanes // head):
            mine = (lane >= sub * head) & (lane < (sub + 1) * head)
            number = group * (lanes // head) + sub
            scores = dot(jnp.where(mine, keys, 0), query, ((1,), (1,)))
            probs = jnp.exp(
                jnp.where(allowed, scores, big_negative) - lse_ref[0, number : number + 1, :]
            )
            probs_grad = dot(jnp.where(mine, values, 0), grad, ((1,), (1,)))
            weighted = jnp.sum(probs * probs_grad, axis=0, keepdims=True)
            scores_grad = (probs * (probs_grad - weighted)).astype(bf16)
            values_grad += dot(probs.astype(bf16), jnp.where(mine, grad, 0))
            keys_grad += dot(scores_grad, jnp.where(mine, query, 0))
            query_grads.append(dot(keys_turned[sub * head : (sub + 1) * head, :], scores_grad))
        query_grad = jnp.concatenate(query_grads, axis=0).T * head ** (-0.5)
        out_ref[:, at : at + lanes] = turned(query_grad, cosine, sine).astype(bf16)
        out_ref[:, width + at : width + at + lanes] = turned(keys_grad, cosine, sine).astype(bf16)
        out_ref[:, 2 * width + at : 2 * width + at + lanes] = values_grad.astype(bf16)


def attend(ends, mixed, width, head, length):
    windows = mixed.shape[0] // length
    if (3 * width) % 128:
        mixed = mixed[:, : 3 * width]
    lanes = min(width, 128)
    cosine, sine = turn_tables(length, head, lanes)
    count = max(8, width // head)
    smem = pl.BlockSpec(memory_space=pltpu.SMEM)
    table = pl.BlockSpec((length, lanes), lambda w: (0, 0))
    return pl.pallas_call(
        functools.partial(attend_kernel, head),
        grid=(windows,),
        in_specs=[smem, pl.BlockSpec((length, 3 * width), lambda w: (w, 0)), table, table],
        out_specs=[
            pl.BlockSpec((length, 3 * width), lambda w: (w, 0)),
            pl.BlockSpec((length, width), lambda w: (w, 0)),
            pl.BlockSpec((1, count, length), lambda w: (w, 0, 0)),
        ],
        out_shape=[
            jax.ShapeDtypeStruct((windows * length, 3 * width), bf16),
            jax.ShapeDtypeStruct((windows * length, width), bf16),
            jax.ShapeDtypeStruct((windows, count, length), f32),
        ],
        compiler_params=pltpu.CompilerParams(vmem_limit_bytes=40 * 2**20),
        cost_estimate=pl.CostEstimate(
            flops=windows * 4 * length * length * width,
            bytes_accessed=windows * length * width * 20,
            transcendentals=windows * length * length * (width // head),
        ),
    )(ends, mixed, cosine, sine)


def attend_back(ends, qkv, grad, lse, width, head, length):
    windows = qkv.shape[0] // length
    lanes = min(width, 128)
    cosine, sine = turn_tables(length, head, lanes)
    smem = pl.BlockSpec(memory_space=pltpu.SMEM)
    table = pl.BlockSpec((length, lanes), lambda w: (0, 0))
    return pl.pallas_call(
        functools.partial(attend_back_kernel, head),
        grid=(windows,),
        in_specs=[
            smem,
            pl.BlockSpec((length, 3 * width), lambda w: (w, 0)),
            pl.BlockSpec((length, width), lambda w: (w, 0)),
            pl.BlockSpec((1, lse.shape[1], length), lambda w: (w, 0, 0)),
            table,
            table,
        ],
        out_specs=pl.BlockSpec((length, 3 * width), lambda w: (w, 0)),
        out_shape=jax.ShapeDtypeStruct((windows * length, 3 * width), bf16),
        compiler_params=pltpu.CompilerParams(vmem_limit_bytes=40 * 2**20),
        cost_estimate=pl.CostEstimate(
            flops=windows * 10 * length * length * width,
            bytes_accessed=windows * length * width * 14,
            transcendentals=windows * length * length * (width // head),
        ),
    )(ends, qkv, grad, lse, cosine, sine)


def gelu_tanh(values):
    inner = gelu_scale * (values + gelu_cubic * values * values * values)
    return 0.5 * values * (1.0 + jnp.tanh(inner))


def gelu_slope(values):
    tanh_value = jnp.tanh(gelu_scale * (values + gelu_cubic * values * values * values))
    return 0.5 * (1.0 + tanh_value) + 0.5 * values * (
        1.0 - tanh_value * tanh_value
    ) * gelu_scale * (1.0 + 3.0 * gelu_cubic * values * values)


class Place:
    def __init__(self, sizes):
        self.ndp = sizes["dp"]
        self.no = self.ndp // GROUP
        self.nf = sizes["fsdp"]
        self.nz = self.nf // CORES
        fsdp = lax.axis_index("fsdp")
        self.dp = lax.axis_index("dp")
        self.t = self.dp % GROUP
        self.z = fsdp // CORES
        self.c = fsdp % CORES
        self.outer_groups = [[o * GROUP + t for o in range(self.no)] for t in range(GROUP)]

    def send(self, x, to):
        pairs = []
        for d in range(self.ndp):
            for z in range(self.nz):
                for c in range(CORES):
                    d2, z2, c2 = to(d, z, c)
                    pairs.append(
                        (d * self.nf + z * CORES + c, d2 * self.nf + z2 * CORES + c2)
                    )
        return lax.ppermute(x, AXES, pairs)

    def swap_t(self, x, mask):
        return self.send(x, lambda d, z, c: (d ^ mask, z, c))

    def shift_z(self, x, step=1):
        return self.send(x, lambda d, z, c: (d, (z + step) % self.nz, c))

    def swap_core(self, x):
        return self.send(x, lambda d, z, c: (d, z, CORES - 1 - c))


def later(x, *after):
    return lax.optimization_barrier((x,) + after)[0]


def gather_t(place, x):
    half = x.shape[0] // 2
    one = place.swap_t(x, 1)
    two = place.swap_t(x, 2)
    low = place.swap_t(one[:half], 2)
    high = place.swap_t(two[half:], 1)
    return [x, one, two, low, high]


def sum_t(place, parts):
    half = parts[0].shape[0] // 2
    low = place.swap_t(parts[3][:half], 2)
    high = place.swap_t(parts[3][half:], 1)
    first = jnp.concatenate(
        [(parts[1][:half].astype(f32) + low.astype(f32)).astype(bf16), parts[1][half:]]
    )
    second = jnp.concatenate(
        [parts[2][:half], (parts[2][half:].astype(f32) + high.astype(f32)).astype(bf16)]
    )
    first = place.swap_t(first, 1)
    second = place.swap_t(second, 2)
    return parts[0], first, second


def ring_gather(place, block):
    if place.no > 1:
        block = lax.all_gather(block, "dp", axis_index_groups=place.outer_groups, tiled=True)
    blocks = [block]
    for _ in range(place.nz - 1):
        blocks.append(place.shift_z(blocks[-1]))
    return [[b, place.swap_core(b)] for b in blocks]


def ring_sum(place, parts):
    def add(a, b):
        return a.astype(f32) + b.astype(f32)

    if place.no > 1:
        parts = lax.psum_scatter(
            parts, "dp", scatter_dimension=0, axis_index_groups=place.outer_groups
        )
    else:
        parts = parts[0]
    theirs = lax.dynamic_index_in_dim(parts, 1 - place.c, 1, keepdims=False)
    mine = lax.dynamic_index_in_dim(parts, place.c, 1, keepdims=False)
    chip = add(mine, place.swap_core(theirs)).astype(bf16)

    def at(step):
        return lax.dynamic_index_in_dim(chip, (place.z - step) % place.nz, 0, keepdims=False)

    moving = at(1)
    for step in range(1, place.nz):
        moving = add(place.shift_z(moving), at(step + 1))
        if step < place.nz - 1:
            moving = moving.astype(bf16)
    return moving


def assemble_kernel(layout, steps, place_ref, *refs):
    pieces, out, sem = refs[:-2], refs[-2], refs[-1]
    copies = []
    for number, piece in enumerate(pieces):
        step, flip = number // CORES, number % CORES
        z = place_ref[1] - step
        z = jnp.where(z < 0, z + steps, z)
        c = jnp.bitwise_xor(place_ref[2], flip)
        row, base = 0, 0
        for rows, masks in layout:
            for mask in range(masks):
                d = jnp.bitwise_xor(place_ref[0], mask) if masks > 1 else 0
                to = pl.multiple_of(base + ((d * steps + z) * CORES + c) * rows, rows)
                copies.append(
                    pltpu.make_async_copy(
                        piece.at[pl.ds(row, rows)], out.at[pl.ds(to, rows)], sem.at[len(copies)]
                    )
                )
                row += rows
            base += rows * masks * steps * CORES
    for copy in copies:
        copy.start()
    for copy in copies:
        copy.wait()


def assemble(place, pieces, layout):
    steps = place.nz
    flat = [piece for pair in pieces for piece in pair]
    width = flat[0].shape[1]
    if place.no > 1 or any(r % 16 for r, _ in layout):
        stacked = jnp.stack(flat).reshape(steps, CORES, place.no, -1, width)
        stacked = jnp.take(stacked, (place.z - np.arange(steps)) % steps, axis=0)
        stacked = jnp.take(stacked, np.arange(CORES) ^ place.c, axis=1)
        outs, row = [], 0
        for r, masks in layout:
            part = stacked[:, :, :, row : row + r * masks]
            part = part.reshape(steps, CORES, place.no, masks, r, width)
            if masks > 1:
                part = jnp.take(part, np.arange(masks) ^ place.t, axis=3)
            outs.append(part.transpose(2, 3, 0, 1, 4, 5).reshape(-1, width))
            row += r * masks
        return jnp.concatenate(outs)
    rows = flat[0].shape[0]
    anywhere = pl.BlockSpec(memory_space=pl.ANY)
    count = len(flat) * sum(masks for _, masks in layout)
    return pl.pallas_call(
        functools.partial(assemble_kernel, layout, steps),
        in_specs=[pl.BlockSpec(memory_space=pltpu.SMEM)] + [anywhere] * len(flat),
        out_specs=pl.BlockSpec(memory_space=pltpu.VMEM),
        out_shape=jax.ShapeDtypeStruct((rows * len(flat), width), flat[0].dtype),
        scratch_shapes=[pltpu.SemaphoreType.DMA((count,))],
        compiler_params=pltpu.CompilerParams(vmem_limit_bytes=16 * 2**20),
        cost_estimate=pl.CostEstimate(
            flops=0, bytes_accessed=2 * rows * len(flat) * width * 2, transcendentals=0
        ),
    )(jnp.stack([place.t, place.z, place.c]).astype(jnp.int32), *flat)


def columns(place, heads_weight, up_weight, mask):
    rows, width3 = heads_weight.shape
    part = width3 // 3 // GROUP
    hidden_part = up_weight.shape[1] // GROUP
    to = place.t ^ mask
    joint = [
        lax.dynamic_slice_in_dim(heads_weight, (k * GROUP + to) * part, part, axis=1)
        for k in range(3)
    ]
    up = lax.dynamic_slice_in_dim(up_weight, to * hidden_part, hidden_part, axis=1)
    return jnp.concatenate(joint + [up], axis=1)


def spread(vector, at, count):
    n = vector.shape[0]
    row = jnp.tile(vector.astype(f32).reshape(1, n), (1, count))
    lane = lax.broadcasted_iota(jnp.int32, row.shape, 1)
    return jnp.where(lane // n == at, row, 0.0)


def small_gather(place, norm_gain, norm_bias, down_bias, up_bias, offsets, terminal):
    here = ((place.dp * place.nz) + place.z) * CORES + place.c
    count = place.ndp * place.nf
    rows = jnp.concatenate([spread(v, here, count) for v in (norm_gain, norm_bias, down_bias)])
    fsdp = (place.dp // GROUP * place.nz + place.z) * CORES + place.c
    own = spread(up_bias, fsdp, place.no * place.nf)
    lanes = rows.shape[1]
    both = jnp.concatenate([rows, jnp.pad(own, ((0, 0), (0, lanes - own.shape[1])))])
    if place.no > 1:
        both = lax.psum(both, "dp", axis_index_groups=place.outer_groups)
    shifted = [place.shift_z(both, s) for s in range(1, place.nz)]
    both = sum(shifted, both)
    both = both + place.swap_core(both)
    ends = jnp.concatenate([offsets, terminal]).astype(f32).reshape(1, -1)
    ends = jnp.pad(ends, ((0, 0), (0, lanes - ends.shape[1])))
    group = jnp.concatenate([both[:3], ends])
    others = [place.swap_t(group, m) for m in range(1, GROUP)]
    rows = sum((o[:3] for o in others), group[:3])
    windows = offsets.shape[0]
    ends = jnp.concatenate([g[3:4, : 2 * windows] for g in [group] + others])
    return rows, both[3:4, : own.shape[1]], ends


def shards(
    sizes,
    tokens,
    heads_weight,
    merge_weight,
    up_weight,
    up_bias,
    down_weight,
    down_bias,
    norm_gain,
    norm_bias,
    offsets,
    terminal,
    cotangent,
):
    place = Place(sizes)
    nz, no = place.nz, place.no
    windows, length, width = tokens.shape
    head = width // HEADS
    rows = heads_weight.shape[0]
    hidden_rows = down_weight.shape[0]
    part = width // GROUP
    hidden_part = up_weight.shape[1] // GROUP
    own_rows = windows * length

    own_tokens = tokens.reshape(own_rows, width)
    token_pieces = gather_t(place, own_tokens)
    own_grad = cotangent.reshape(own_rows, width)
    grad_pieces = gather_t(place, later(own_grad, token_pieces[1], token_pieces[2]))

    pieces = [
        columns(place, heads_weight, up_weight, m) for m in range(GROUP)
    ]
    pieces = [pieces[0]] + [place.swap_t(pieces[m], m) for m in range(1, GROUP)]
    heads_up = assemble(place, ring_gather(place, jnp.concatenate(pieces)), [(rows, GROUP)])
    down_merge = assemble(
        place,
        ring_gather(place, jnp.concatenate([down_weight, merge_weight])),
        [(hidden_rows, 1), (rows, 1)],
    )

    small, up_shift, ends = small_gather(
        place, norm_gain, norm_bias, down_bias, up_bias, offsets, terminal
    )
    gain_full, shift_full, down_shift = small[0:1], small[1:2], small[2:3]
    ends = ends.reshape(GROUP, 2, windows).swapaxes(1, 2).reshape(GROUP * windows, 2)
    ends = ends.astype(jnp.int32)

    all_tokens = jnp.concatenate(token_pieces)
    grad = jnp.concatenate(grad_pieces)

    def normalised(values):
        values = values.astype(f32)
        centered = values - jnp.mean(values, axis=-1, keepdims=True)
        inverse_std = lax.rsqrt(jnp.mean(centered * centered, axis=-1, keepdims=True) + eps)
        return centered * inverse_std, inverse_std

    normed, _ = normalised(all_tokens)
    acts = (normed * gain_full + shift_full).astype(bf16)
    mixed_hidden = dot(acts, heads_up)
    qkv, attended, lse = attend(ends, mixed_hidden, part, head, length)
    hidden = mixed_hidden[:, 3 * part :] + up_shift
    activated = gelu_tanh(hidden).astype(bf16)
    joined = jnp.concatenate([activated, attended], axis=1)
    out_terms = dot(joined, down_merge).astype(bf16).reshape(GROUP, own_rows, width)
    out_sum = sum((t.astype(f32) for t in sum_t(place, [out_terms[m] for m in range(GROUP)])), 0.0)
    block_output = (own_tokens.astype(f32) + out_sum + down_shift).astype(bf16)

    joined_grad = dot(grad, down_merge, ((1,), (1,)))
    hidden_grad = (joined_grad[:, :hidden_part] * gelu_slope(hidden)).astype(bf16)
    attended_grad = joined_grad[:, hidden_part:].astype(bf16)
    grad_down_merge = dot(joined, grad, ((0,), (0,))).astype(bf16)
    mixed_grad = attend_back(ends, qkv, attended_grad, lse, part, head, length)
    both_grad = jnp.concatenate([mixed_grad, hidden_grad], axis=1)
    acts_grad = dot(both_grad, heads_up, ((1,), (1,)))
    grad_heads_up = dot(acts, both_grad, ((0,), (0,))).astype(bf16)

    grad_gain = jnp.sum(acts_grad * normed, axis=0)
    grad_bias = jnp.sum(acts_grad, axis=0)
    grad_down_bias = jnp.sum(grad.astype(f32), axis=0)
    grad_up_bias = jnp.sum(hidden_grad.astype(f32), axis=0)
    per_row = hidden_rows // rows
    up_rows = grad_up_bias.reshape(no, 1, nz, CORES, rows, per_row)
    up_rows = jnp.broadcast_to(up_rows, (no, GROUP, nz, CORES, rows, per_row))
    up_rows = up_rows.reshape(width, per_row)
    extra = jnp.concatenate(
        [grad_gain[:, None], grad_bias[:, None], grad_down_bias[:, None], up_rows], axis=1
    ).astype(bf16)
    extra = jnp.pad(extra, ((0, 0), (0, 128 - extra.shape[1])))

    acts_terms = acts_grad.astype(bf16).reshape(GROUP, own_rows, width)
    acts_sum = sum((t.astype(f32) for t in sum_t(place, [acts_terms[m] for m in range(GROUP)])), 0.0)
    own_normed, inverse_std = normalised(own_tokens)
    normed_grad = acts_sum * gain_full
    grad_tokens = (
        own_grad.astype(f32)
        + inverse_std
        * (
            normed_grad
            - jnp.mean(normed_grad, axis=-1, keepdims=True)
            - own_normed * jnp.mean(normed_grad * own_normed, axis=-1, keepdims=True)
        )
    ).astype(bf16)

    down_terms = grad_down_merge[:hidden_part].reshape(no, nz, CORES, hidden_rows, width)
    merge_terms = grad_down_merge[hidden_part:].reshape(no, nz, CORES, rows, width)
    down_merge_sum = ring_sum(place, jnp.concatenate([down_terms, merge_terms], axis=3))
    grad_down, grad_merge = down_merge_sum[:hidden_rows], down_merge_sum[hidden_rows:]

    terms = jnp.concatenate([grad_heads_up, extra], axis=1)
    terms = terms.reshape(no, GROUP, nz, CORES, rows, terms.shape[1]).transpose(0, 2, 3, 1, 4, 5)
    summed = ring_sum(place, terms).astype(bf16)

    def block(mask):
        return lax.dynamic_index_in_dim(summed, place.t ^ mask, 0, keepdims=False)

    arrived = [block(0)] + [place.swap_t(block(m), m) for m in range(1, GROUP)]
    by_t = []
    for t in range(GROUP):
        mask = t ^ place.t
        by_t.append(lax.select_n(mask, *arrived).astype(f32))
    grad_heads = jnp.concatenate(
        [b[:, k * part : (k + 1) * part] for k in range(3) for b in by_t], axis=1
    )
    grad_up = jnp.concatenate([b[:, 3 * part : 3 * part + hidden_part] for b in by_t], axis=1)
    last = [a[:, 3 * part + hidden_part :].astype(f32) for a in arrived]
    return (
        block_output.reshape(tokens.shape),
        grad_tokens.reshape(tokens.shape),
        grad_heads,
        grad_merge,
        grad_up,
        last[0][:, 3 : 3 + per_row].reshape(-1),
        grad_down,
        last[0][:, 2],
        sum(a[:, 0] for a in last),
        sum(a[:, 1] for a in last),
    )


def solution(mesh):
    whole = P(AXES)
    return jax.shard_map(
        functools.partial(shards, dict(mesh.shape)),
        mesh=mesh,
        in_specs=(whole,) * 12,
        out_specs=(whole,) * 10,
        check_vma=False,
    )
```

```python
import functools

import jax
import jax.numpy as jnp
import numpy as np
from jax import lax
from jax.experimental import pallas as pl
from jax.experimental.pallas import tpu as pltpu
from jax.sharding import PartitionSpec as P

HEADS = 16
ROT = 32
CORES = 2
GROUP = 4
AXES = ("dp", "fsdp")

eps = 1e-05
big_negative = -1e30
gelu_scale = 0.7978845608028654
gelu_cubic = 0.044715

bf16 = jnp.bfloat16
f32 = jnp.float32


def turn_tables(length, head, lanes):
    position = np.arange(length, dtype=np.float32)
    exponent = np.arange(0, ROT, 2, dtype=np.float32) / np.float32(ROT)
    rate = (np.float32(1.0) / np.power(np.float32(10000.0), exponent)).astype(np.float32)
    phase = (position[:, None] * rate[None, :]).astype(np.float32)
    cosine = np.ones((length, head), np.float32)
    sine = np.zeros((length, head), np.float32)
    cosine[:, :ROT] = np.repeat(np.cos(phase), 2, axis=1)
    sine[:, :ROT] = np.repeat(np.sin(phase), 2, axis=1)
    sine[:, 0:ROT:2] *= -1.0
    copies = lanes // head
    return np.tile(cosine, (1, copies)), np.tile(sine, (1, copies))


def turned(values, cosine, sine):
    lanes = values.shape[1]
    even = lax.broadcasted_iota(jnp.int32, values.shape, 1) % 2 == 0
    other = jnp.where(even, pltpu.roll(values, lanes - 1, 1), pltpu.roll(values, 1, 1))
    return values * cosine + other * sine


def dot(a, b, dims=((1,), (0,))):
    return lax.dot_general(a, b, (dims, ((), ())), preferred_element_type=f32)


def allowed_pairs(ends, length):
    offset = (16.0 * ends[:, 0:1] + ends[:, 1:2]).astype(jnp.int32)
    end = (16.0 * ends[:, 2:3] + ends[:, 3:4]).astype(jnp.int32)
    key = lax.broadcasted_iota(jnp.int32, (length, 1), 0)
    query = lax.broadcasted_iota(jnp.int32, (1, length), 1)
    key_part = (key >= offset).astype(jnp.int32) + (key > end).astype(jnp.int32)
    query_part = (query >= offset).astype(jnp.int32) + (query > end).astype(jnp.int32)
    return (key_part == query_part) & (query >= key)


def spec(space):
    return pl.BlockSpec(memory_space=space)


def settings(mebibytes):
    return {
        "compiler_params": pltpu.CompilerParams(vmem_limit_bytes=mebibytes * 2**20),
        "cost_estimate": pl.CostEstimate(flops=1, bytes_accessed=1, transcendentals=0),
    }


TICK = jax.ShapeDtypeStruct((8, 128), jnp.float32)


def tick(ref):
    ref[...] = jnp.zeros_like(ref)


def call(kernel, ins, outs, mebibytes, after=(), scratch=()):
    many = len(ins)

    def body(*refs):
        rest = refs[many + len(after) :]
        tick(rest[len(outs)])
        kernel(*refs[:many], *rest[: len(outs)], *rest[len(outs) + 1 :])

    result = pl.pallas_call(
        body,
        in_specs=[spec(pltpu.SMEM if x.dtype == jnp.int32 else pltpu.VMEM) for x in ins]
        + [spec(pl.ANY)] * len(after),
        out_specs=[spec(pltpu.VMEM)] * (len(outs) + 1),
        out_shape=[*outs, TICK],
        scratch_shapes=list(scratch),
        **settings(mebibytes),
    )(*ins, *after)
    return result[:-1], result[-1]


def shape16(*dims):
    return jax.ShapeDtypeStruct(dims, bf16)


def stacked(refs):
    return jnp.concatenate([r[...] for r in refs])


def normalised(values):
    mean = jnp.mean(values, axis=-1, keepdims=True)
    centered = values - mean
    inverse_std = lax.rsqrt(jnp.mean(centered * centered, axis=-1, keepdims=True) + eps)
    return centered * inverse_std, inverse_std


def gelu_and_slope(h):
    square = h * h
    tanh_value = jnp.tanh(h * (gelu_scale + gelu_scale * gelu_cubic * square))
    half = 0.5 * (1.0 + tanh_value)
    slope = half + (0.5 * h) * (1.0 - tanh_value * tanh_value) * (
        gelu_scale + 3.0 * gelu_scale * gelu_cubic * square
    )
    return h * half, slope


def ends_of(window, ends_ref):
    rows, width = ends_ref.shape
    at = rows // GROUP * window
    return ends_ref[at : at + 16, width - 128 :].astype(f32)[4:5]


def attend_kernel(head, window, ends_ref, heads_ref, small_ref, cos_ref, sin_ref, *refs):
    tokens = refs[:2]
    acts_ref, normed_ref, attended_ref, qkv_ref, lse_ref = refs[2:]
    length, part = attended_ref.shape
    lanes = cos_ref.shape[1]
    normed, _ = normalised(stacked(tokens).astype(f32))
    normed_ref[...] = normed.astype(bf16)
    acts_ref[...] = (normed * small_ref[0:1, :] + small_ref[1:2, :]).astype(bf16)
    acts = acts_ref[...]
    query_all, keys_all, values_all = (
        dot(acts, heads_ref[:, k * part : (k + 1) * part]) for k in range(3)
    )
    allowed = allowed_pairs(ends_of(window, ends_ref), length)
    cosine, sine = cos_ref[...], sin_ref[...]
    lane = lax.broadcasted_iota(jnp.int32, (1, lanes), 1)
    for group in range(part // lanes):
        at = group * lanes
        query = (turned(query_all[:, at : at + lanes], cosine, sine) * head ** (-0.5)).astype(bf16)
        keys = turned(keys_all[:, at : at + lanes], cosine, sine).astype(bf16)
        values = values_all[:, at : at + lanes]
        qkv_ref[:, at : at + lanes] = query
        qkv_ref[:, part + at : part + at + lanes] = keys
        qkv_ref[:, 2 * part + at : 2 * part + at + lanes] = values.astype(bf16)
        values_turned = values.T.astype(bf16)
        outs = []
        for sub in range(lanes // head):
            mine = (lane >= sub * head) & (lane < (sub + 1) * head)
            scores = dot(jnp.where(mine, keys, 0), query, ((1,), (1,)))
            scores = jnp.where(allowed, scores, big_negative)
            top = jnp.max(scores, axis=0, keepdims=True)
            expo = jnp.exp(scores - top)
            total = jnp.sum(expo, axis=0, keepdims=True)
            probs = (expo * (1.0 / total)).astype(bf16)
            number = group * (lanes // head) + sub
            lse_ref[number : number + 1, :] = top + jnp.log(total)
            outs.append(dot(values_turned[sub * head : (sub + 1) * head, :], probs))
        attended_ref[:, at : at + lanes] = jnp.concatenate(outs, axis=0).T.astype(bf16)


def attend(window, ends, tokens, heads, small, tables, head, after=()):
    length, width = 2 * tokens[0].shape[0], tokens[0].shape[1]
    part = heads.shape[1] // 3
    outs = [shape16(length, w) for w in (width, width, part, 3 * part)]
    outs.append(jax.ShapeDtypeStruct((max(8, part // head), length), f32))
    kernel = functools.partial(attend_kernel, head, window)
    return call(kernel, [ends, heads, small, *tables, *tokens], outs, 6, after)


def hidden_kernel(up_ref, small_ref, acts_ref, activated_ref, slope_ref):
    acts = acts_ref[...]
    hidden_part = up_ref.shape[1]
    step = min(256, hidden_part)
    for at in range(0, hidden_part, step):
        hidden = dot(acts, up_ref[:, at : at + step])
        value, slope = gelu_and_slope(hidden + small_ref[3:4, at : at + step])
        activated_ref[:, at : at + step] = value.astype(bf16)
        slope_ref[:, at : at + step] = slope.astype(bf16)


def hidden_units(acts, up, small, after=()):
    outs = [shape16(acts.shape[0], up.shape[1])] * 2
    return call(hidden_kernel, [up, small, acts], outs, 4, after)


def out_kernel(down_ref, merge_ref, activated_ref, attended_ref, low_ref, high_ref):
    half, width = low_ref.shape
    activated, attended = activated_ref[...], attended_ref[...]
    step = min(256, width)
    for at in range(0, width, step):
        term = dot(activated, down_ref[:, at : at + step])
        term = (term + dot(attended, merge_ref[:, at : at + step])).astype(bf16)
        low_ref[:, at : at + step] = term[:half]
        high_ref[:, at : at + step] = term[half:]


def out_terms(activated, attended, down, merge, after=()):
    outs = [shape16(activated.shape[0] // 2, down.shape[1])] * 2
    return call(out_kernel, [down, merge, activated, attended], outs, 4, after)


def joined_grad_kernel(
    down_ref, merge_ref, slope_ref, low_ref, high_ref, hidden_ref, attended_ref, sums_ref
):
    hidden_part = hidden_ref.shape[1]
    grad = stacked([low_ref, high_ref])
    sums_ref[...] = jnp.zeros_like(sums_ref)
    sums_ref[0:1, :] = jnp.sum(grad.astype(f32), axis=0, keepdims=True)
    step = min(256, hidden_part)
    for at in range(0, hidden_part, step):
        term = dot(grad, down_ref[at : at + step, :], ((1,), (1,)))
        term = (term * slope_ref[:, at : at + step].astype(f32)).astype(bf16)
        hidden_ref[:, at : at + step] = term
        sums_ref[1:2, at : at + step] = jnp.sum(term.astype(f32), axis=0, keepdims=True)
    attended_ref[...] = dot(grad, merge_ref[...], ((1,), (1,))).astype(bf16)


def joined_grad(grad, down, merge, slope, after=()):
    length, hidden_part = slope.shape
    outs = [shape16(length, hidden_part), shape16(length, merge.shape[0])]
    outs.append(jax.ShapeDtypeStruct((8, max(down.shape)), f32))
    return call(joined_grad_kernel, [down, merge, slope, *grad], outs, 5, after)


def attend_back_kernel(
    head, window, ends_ref, cos_ref, sin_ref, qkv_ref, grad_ref, lse_ref, mixed_ref
):
    length = qkv_ref.shape[0]
    part = qkv_ref.shape[1] // 3
    lanes = cos_ref.shape[1]
    allowed = allowed_pairs(ends_of(window, ends_ref), length)
    cosine, sine = cos_ref[...], -sin_ref[...]
    lane = lax.broadcasted_iota(jnp.int32, (1, lanes), 1)
    for group in range(part // lanes):
        at = group * lanes
        query = qkv_ref[:, at : at + lanes]
        keys = qkv_ref[:, part + at : part + at + lanes]
        values = qkv_ref[:, 2 * part + at : 2 * part + at + lanes]
        grad = grad_ref[:, at : at + lanes]
        keys_turned = keys.astype(f32).T.astype(bf16)
        values_grad = jnp.zeros((length, lanes), f32)
        keys_grad = jnp.zeros((length, lanes), f32)
        query_grads = []
        for sub in range(lanes // head):
            mine = (lane >= sub * head) & (lane < (sub + 1) * head)
            number = group * (lanes // head) + sub
            scores = dot(jnp.where(mine, keys, 0), query, ((1,), (1,)))
            probs = jnp.exp(
                jnp.where(allowed, scores, big_negative) - lse_ref[number : number + 1, :]
            )
            probs_grad = dot(jnp.where(mine, values, 0), grad, ((1,), (1,)))
            weighted = jnp.sum(probs * probs_grad, axis=0, keepdims=True)
            scores_grad = (probs * (probs_grad - weighted)).astype(bf16)
            values_grad += dot(probs.astype(bf16), jnp.where(mine, grad, 0))
            keys_grad += dot(scores_grad, jnp.where(mine, query, 0))
            query_grads.append(dot(keys_turned[sub * head : (sub + 1) * head, :], scores_grad))
        query_grad = jnp.concatenate(query_grads, axis=0).T * head ** (-0.5)
        mixed_ref[:, at : at + lanes] = turned(query_grad, cosine, sine).astype(bf16)
        mixed_ref[:, part + at : part + at + lanes] = turned(keys_grad, cosine, sine).astype(bf16)
        mixed_ref[:, 2 * part + at : 2 * part + at + lanes] = values_grad.astype(bf16)


def attend_back(window, ends, qkv, grad, lse, tables, head, after=()):
    kernel = functools.partial(attend_back_kernel, head, window)
    return call(kernel, [ends, *tables, qkv, grad, lse], [shape16(*qkv.shape)], 6, after)


def acts_grad_kernel(
    heads_ref, up_ref, mixed_ref, hidden_ref, normed_ref, low_ref, high_ref, sums_ref
):
    mixed, hidden = mixed_ref[...], hidden_ref[...]
    half, width = low_ref.shape
    step = min(256, width)
    sums_ref[...] = jnp.zeros_like(sums_ref)
    for at in range(0, width, step):
        term = dot(mixed, heads_ref[at : at + step, :], ((1,), (1,)))
        term += dot(hidden, up_ref[at : at + step, :], ((1,), (1,)))
        sums_ref[0:1, at : at + step] = jnp.sum(
            term * normed_ref[:, at : at + step].astype(f32), axis=0, keepdims=True
        )
        sums_ref[1:2, at : at + step] = jnp.sum(term, axis=0, keepdims=True)
        low_ref[:, at : at + step] = term[:half].astype(bf16)
        high_ref[:, at : at + step] = term[half:].astype(bf16)


def acts_grad(heads, up, mixed, hidden, normed, after=()):
    length, width = normed.shape
    outs = [shape16(length // 2, width)] * 2 + [jax.ShapeDtypeStruct((8, width), f32)]
    (low, high, sums), done = call(
        acts_grad_kernel, [heads, up, mixed, hidden, normed], outs, 5, after
    )
    return (low, high), sums, done


def joined_windows(refs, scratch):
    at = 0
    for ref in refs:
        rows = ref.shape[0]
        scratch[at : at + rows, :] = ref[...]
        at += rows


def row_grads_kernel(rows, place_ref, *refs):
    activated, attended, grads = refs[:GROUP], refs[GROUP : 2 * GROUP], refs[2 * GROUP : 4 * GROUP]
    theirs_ref, mine_ref, a_ref, b_ref, g_ref = refs[4 * GROUP :]
    joined_windows(activated, a_ref)
    joined_windows(attended, b_ref)
    joined_windows(grads, g_ref)
    first = place_ref[2] == 0
    grad = g_ref[...]
    at = 0
    for ref, size in ((a_ref, theirs_ref.shape[1] - rows), (b_ref, rows)):
        step = min(256, ref.shape[1])
        for start in range(0, ref.shape[1], step):
            term = dot(ref[:, start : start + step], grad, ((0,), (0,))).astype(bf16)
            for pair in range(step // (CORES * size)):
                z = start // (CORES * size) + pair
                zero = term[pair * 2 * size : (pair * 2 + 1) * size]
                one = term[(pair * 2 + 1) * size : (pair * 2 + 2) * size]
                mine_ref[z, at : at + size, :] = jnp.where(first, zero, one)
                theirs_ref[z, at : at + size, :] = jnp.where(first, one, zero)
        at += size


def row_grads(where, steps, rows, activated, attended, grads, after=()):
    length, hidden_part = activated[0].shape
    part = attended[0].shape[1]
    width = grads[0].shape[1]
    out = shape16(steps, hidden_part // (steps * CORES) + rows, width)
    scratch = [pltpu.VMEM((GROUP * length, w), bf16) for w in (hidden_part, part, width)]
    ins = [where, *activated, *attended, *grads]
    kernel = functools.partial(row_grads_kernel, rows)
    return call(kernel, ins, [out, out], 12, after, scratch)


def column_grads_kernel(rows, place_ref, *refs):
    theirs_ref, mine_ref, a_ref, b_ref = refs[2 * GROUP :]
    steps = theirs_ref.shape[0]
    joined_windows(refs[:GROUP], a_ref)
    joined_windows(refs[GROUP : 2 * GROUP], b_ref)
    first = place_ref[2] == 0
    grad = b_ref[...]
    step = steps * CORES * rows
    for t in range(GROUP):
        term = dot(a_ref[:, t * step : (t + 1) * step], grad, ((0,), (0,))).astype(bf16)
        for z in range(steps):
            zero = term[z * 2 * rows : (z * 2 + 1) * rows]
            one = term[(z * 2 + 1) * rows : (z * 2 + 2) * rows]
            mine_ref[z, t * rows : (t + 1) * rows, :] = jnp.where(first, zero, one)
            theirs_ref[z, t * rows : (t + 1) * rows, :] = jnp.where(first, one, zero)


def column_grads(where, steps, rows, acts, grads, after=()):
    length, width = acts[0].shape
    columns = grads[0].shape[1]
    out = shape16(steps, GROUP * rows, columns)
    scratch = [pltpu.VMEM((GROUP * length, w), bf16) for w in (width, columns)]
    kernel = functools.partial(column_grads_kernel, rows)
    return call(kernel, [where, *acts, *grads], [out, out], 12, after, scratch)


def ring_begin_kernel(steps, place_ref, mine_ref, got_ref, chip_ref, first_ref):
    for z in range(steps):
        chip_ref[z] = (mine_ref[z].astype(f32) + got_ref[z].astype(f32)).astype(bf16)
    at = lax.rem(place_ref[1] + steps - 1, steps)
    first_ref[...] = chip_ref[at]


def ring_add_kernel(steps, step, place_ref, chip_ref, moving_ref, out_ref):
    at = lax.rem(place_ref[1] + 2 * steps - step, steps)
    out_ref[...] = (chip_ref[at].astype(f32) + moving_ref[...].astype(f32)).astype(bf16)


def ring_rows_kernel(place_ref, chip_ref, moving_ref, down_ref, merge_ref):
    total = chip_ref[place_ref[1]].astype(f32) + moving_ref[...].astype(f32)
    size = down_ref.shape[0]
    down_ref[...] = total[:size]
    merge_ref[...] = total[size:]


def ring_columns_kernel(place_ref, chip_ref, moving_ref, *outs):
    rows = outs[0].shape[0]
    for mask in range(GROUP):
        t = jnp.bitwise_xor(place_ref[0], mask)
        at = pl.ds(pl.multiple_of(t * rows, rows), rows)
        total = chip_ref[place_ref[1], at, :].astype(f32) + moving_ref[at, :].astype(f32)
        outs[mask][...] = total.astype(bf16)


def add_pairs_kernel(*refs):
    for i in range(len(refs) // 3):
        a, b, out = refs[2 * i], refs[2 * i + 1], refs[len(refs) // 3 * 2 + i]
        out[...] = (a[...].astype(f32) + b[...].astype(f32)).astype(bf16)


def add_pairs(*arrays, after=()):
    outs = [shape16(*a.shape) for a in arrays[::2]]
    return call(add_pairs_kernel, list(arrays), outs, 3, after)


def small_sums_kernel(*refs):
    out_ref = refs[-1]
    count = len(refs) // 2
    out_ref[...] = jnp.zeros_like(out_ref)
    out_ref[0:2, :] = sum((r[0:2, :] for r in refs[1:count]), refs[0][0:2, :])
    out_ref[2:4, :] = sum((r[0:2, :] for r in refs[count + 1 : -1]), refs[count][0:2, :])


def summed_halves(own, one, two, scratch):
    half = own[0].shape[0]
    for i in range(2):
        scratch[i * half : (i + 1) * half, :] = (
            own[i][...].astype(f32) + one[i][...].astype(f32) + two[i][...].astype(f32)
        )


def finish_out_kernel(low_ref, high_ref, small_ref, *refs):
    out_ref, scratch = refs[-2:]
    summed_halves(refs[0:2], refs[2:4], refs[4:6], scratch)
    tokens = stacked([low_ref, high_ref]).astype(f32)
    out_ref[...] = (tokens + scratch[...] + small_ref[2:3, :]).astype(bf16)


def finish_grad_kernel(low_ref, high_ref, grad_low_ref, grad_high_ref, small_ref, *refs):
    out_ref, scratch = refs[-2:]
    summed_halves(refs[0:2], refs[2:4], refs[4:6], scratch)
    normed, inverse_std = normalised(stacked([low_ref, high_ref]).astype(f32))
    normed_grad = scratch[...] * small_ref[0:1, :]
    mean = jnp.mean(normed_grad, axis=-1, keepdims=True)
    along = jnp.mean(normed_grad * normed, axis=-1, keepdims=True)
    grad = stacked([grad_low_ref, grad_high_ref]).astype(f32)
    out_ref[...] = (grad + inverse_std * (normed_grad - mean - normed * along)).astype(bf16)


def finish(kernel, arrays, terms, after=()):
    flat = [half for pair in terms for half in pair]
    half, width = flat[0].shape
    scratch = [pltpu.VMEM((2 * half, width), f32)]
    (out,), _ = call(kernel, [*arrays, *flat], [shape16(2 * half, width)], 8, after, scratch)
    return out


def prepare_kernel(
    place_ref, ends_ref, small_ref, heads_ref, up_ref, down_ref, merge_ref, tokens_ref, grad_ref, *refs
):
    outs, halves, tick_ref, sem = refs[: GROUP + 1], refs[GROUP + 1 : -2], refs[-2], refs[-1]
    rows = heads_ref.shape[0]
    part = heads_ref.shape[1] // 3 // GROUP
    hidden_part = up_ref.shape[1] // GROUP
    hidden_rows = down_ref.shape[0]
    copies = []

    def copy(src, dst):
        copies.append(pltpu.make_async_copy(src, dst, sem.at[len(copies)]))

    for mask in range(GROUP):
        to = jnp.bitwise_xor(place_ref[0], mask)
        for k in range(3):
            at = pl.multiple_of((k * GROUP + to) * part, part)
            copy(heads_ref.at[:, pl.ds(at, part)], outs[mask].at[:, pl.ds(k * part, part)])
        at = pl.multiple_of(to * hidden_part, hidden_part)
        copy(
            up_ref.at[:, pl.ds(at, hidden_part)],
            outs[mask].at[:, pl.ds(3 * part + 128, hidden_part)],
        )
    copy(down_ref, outs[GROUP].at[pl.ds(0, hidden_rows)])
    copy(merge_ref, outs[GROUP].at[pl.ds(hidden_rows, rows)])
    size = halves[0].shape[0]
    for i, half in enumerate(halves):
        copy((tokens_ref, grad_ref)[i // 2].at[pl.ds(i % 2 * size, size)], half)
    for each in copies:
        each.start()
    tick(tick_ref)
    quarter = place_ref[3]
    row = lax.broadcasted_iota(jnp.int32, (rows, 128), 0)
    lane = lax.broadcasted_iota(jnp.int32, (rows, 128), 1)
    first = jnp.broadcast_to(small_ref[0:1, :], (rows, 128))
    extra = jnp.zeros((rows, 128), f32)
    for k in range(3):
        moved = pltpu.roll(first, lax.rem(quarter * rows + (128 - k * rows), 128), 1)
        here = (row == k) & (lane >= quarter * rows) & (lane < (quarter + 1) * rows)
        extra = jnp.where(here, moved, extra)
    extra = jnp.where(row == 3, small_ref[1:2, :], extra)
    for k in range(2):
        value = ends_ref[k]
        for i, piece in enumerate((value // 16, value % 16)):
            extra = jnp.where((row == 4) & (lane == 2 * k + i), piece.astype(f32), extra)
    extra = extra.astype(bf16)
    for mask in range(GROUP):
        outs[mask][:, 3 * part : 3 * part + 128] = extra
    for each in copies:
        each.wait()


def prepare(where, ends, small, heads_weight, up_weight, down_weight, merge_weight, tokens, grad):
    rows, width3 = heads_weight.shape
    columns = width3 // GROUP + up_weight.shape[1] // GROUP + 128
    block = (down_weight.shape[0] + merge_weight.shape[0], down_weight.shape[1])
    half = (tokens.shape[0] // 2, tokens.shape[1])
    far = [heads_weight, up_weight, down_weight, merge_weight, tokens, grad]
    far = [pltpu.with_memory_space_constraint(x, pltpu.HBM) for x in far]
    return pl.pallas_call(
        prepare_kernel,
        in_specs=[spec(pltpu.SMEM)] * 2 + [spec(pltpu.VMEM)] + [spec(pltpu.HBM)] * len(far),
        out_specs=[spec(pltpu.VMEM)] * (GROUP + 6),
        out_shape=[shape16(rows, columns)] * GROUP + [shape16(*block)] + [shape16(*half)] * 4 + [TICK],
        scratch_shapes=[pltpu.SemaphoreType.DMA((4 * GROUP + 6,))],
        **settings(2),
    )(where, ends, small, *far)


def small_rows_kernel(count, place_ref, extra_ref, small_ref):
    total = extra_ref.shape[0]
    rows = total // (count * GROUP)
    row = lax.broadcasted_iota(jnp.int32, (8, 128), 0)
    per = 128 // rows
    for tile in range(small_ref.shape[1] // 128):
        value = jnp.zeros((8, 128), f32)
        for i in range(per):
            at = (tile * per + i) * rows
            value += extra_ref[at : at + 16, :].astype(f32)[:8]
        if tile < count:
            at = pl.multiple_of((place_ref[0] * count + tile) * rows, rows)
            value = jnp.where(row == 3, extra_ref[pl.ds(at, 16), :].astype(f32)[:8], value)
        small_ref[:, tile * 128 : (tile + 1) * 128] = value


def assemble_kernel(layout, steps, with_small, place_ref, *refs):
    count = steps * CORES
    pieces = refs[:count]
    outs = refs[-1 - len(layout) - 2 * with_small :]
    sem = refs[-1]
    copies = []

    def copy(src, dst):
        copies.append(pltpu.make_async_copy(src, dst, sem.at[len(copies)]))

    for number, piece in enumerate(pieces):
        z = place_ref[1] - number // CORES
        z = jnp.where(z < 0, z + steps, z)
        c = jnp.bitwise_xor(place_ref[2], number % CORES)
        row = 0
        for (rows, masks), out in zip(layout, outs):
            width = out.shape[1]
            for mask in range(masks):
                d = jnp.bitwise_xor(place_ref[0], mask) if masks > 1 else 0
                to = pl.ds(pl.multiple_of(((d * steps + z) * CORES + c) * rows, rows), rows)
                source = piece.at[pl.ds(row, rows)]
                if with_small:
                    copy(source.at[:, pl.ds(0, width)], out.at[to])
                    copy(source.at[:, pl.ds(width, 128)], refs[-2].at[to])
                else:
                    copy(source, out.at[to])
                row += rows
    for each in copies:
        each.start()
    for each in copies:
        each.wait()
    if with_small:
        small_rows_kernel(count, place_ref, refs[-2], outs[len(layout)])


def assemble(place, where, pieces, layout, with_small=False, after=()):
    steps = place.nz
    flat = [piece for pair in pieces for piece in pair]
    width = flat[0].shape[1]
    if place.no > 1 or any(r % 16 for r, _ in layout):
        stacked_pieces = jnp.stack(flat).reshape(steps, CORES, place.no, -1, width)
        stacked_pieces = jnp.take(stacked_pieces, (place.z - np.arange(steps)) % steps, axis=0)
        stacked_pieces = jnp.take(stacked_pieces, np.arange(CORES) ^ place.c, axis=1)
        outs, row = [], 0
        for r, masks in layout:
            part = stacked_pieces[:, :, :, row : row + r * masks]
            part = part.reshape(steps, CORES, place.no, masks, r, width)
            if masks > 1:
                part = jnp.take(part, np.arange(masks) ^ place.t, axis=3)
            outs.append(part.transpose(2, 3, 0, 1, 4, 5).reshape(-1, width))
            row += r * masks
        return outs
    if with_small:
        width -= 128
    count = len(flat) * sum(masks for _, masks in layout) * (2 if with_small else 1)
    totals = [len(flat) * r * masks for r, masks in layout]
    shapes = [jax.ShapeDtypeStruct((total, width), bf16) for total in totals]
    scratch = [pltpu.SemaphoreType.DMA((count,))]
    if with_small:
        shapes.append(jax.ShapeDtypeStruct((8, totals[0]), f32))
        scratch.insert(0, pltpu.VMEM((totals[0], 128), bf16))
    return pl.pallas_call(
        functools.partial(assemble_kernel, layout, steps, with_small),
        in_specs=[spec(pltpu.SMEM)] + [spec(pl.ANY)] * (len(flat) + len(after)),
        out_specs=[spec(pltpu.VMEM)] * len(shapes),
        out_shape=shapes,
        scratch_shapes=scratch,
        **settings(2),
    )(where, *flat, *after)


def columns_out_kernel(place_ref, group_ref, all_ref, *refs):
    ups, heads = refs[:GROUP], refs[GROUP : 2 * GROUP]
    heads_out_ref, up_out_ref, small_ref, own_ref = refs[2 * GROUP :]
    rows, hidden_part = ups[0].shape
    part = heads[0].shape[1] // 3
    for mask in range(GROUP):
        to = jnp.bitwise_xor(place_ref[0], mask)
        at = pl.multiple_of(to * hidden_part, hidden_part)
        up_out_ref[:, pl.ds(at, hidden_part)] = ups[mask][...].astype(f32)
        for k in range(3):
            at = pl.multiple_of((k * GROUP + to) * part, part)
            heads_out_ref[:, pl.ds(at, part)] = heads[mask][:, k * part : (k + 1) * part].astype(f32)
    tile = pl.ds(pl.multiple_of(place_ref[4] * 128, 128), 128)
    row = lax.broadcasted_iota(jnp.int32, (8, 128), 0)
    value = jnp.where(row < 2, all_ref[:, tile], group_ref[:, tile])
    small_ref[...] = pltpu.roll(value, lax.rem(128 - place_ref[3] * rows, 128), 1)
    own_ref[...] = group_ref[:, pl.ds(pl.multiple_of(place_ref[5] * 128, 128), 128)]


def columns_out(where, group_sums, all_sums, ups, heads):
    rows, hidden_part = ups[0].shape
    return pl.pallas_call(
        columns_out_kernel,
        in_specs=[spec(pltpu.SMEM)] + [spec(pltpu.VMEM)] * (2 * GROUP + 2),
        out_specs=[spec(pltpu.VMEM)] * 4,
        out_shape=[
            jax.ShapeDtypeStruct((rows, GROUP * heads[0].shape[1]), f32),
            jax.ShapeDtypeStruct((rows, GROUP * hidden_part), f32),
            jax.ShapeDtypeStruct((8, 128), f32),
            jax.ShapeDtypeStruct((8, 128), f32),
        ],
        **settings(4),
    )(where, group_sums, all_sums, *ups, *heads)


class Place:
    def __init__(self, sizes):
        self.ndp = sizes["dp"]
        self.no = self.ndp // GROUP
        self.nf = sizes["fsdp"]
        self.nz = self.nf // CORES
        fsdp = lax.axis_index("fsdp")
        self.dp = lax.axis_index("dp")
        self.t = self.dp % GROUP
        self.z = fsdp // CORES
        self.c = fsdp % CORES
        self.outer_groups = [[o * GROUP + t for o in range(self.no)] for t in range(GROUP)]

    def send(self, x, to):
        pairs = []
        for d in range(self.ndp):
            for z in range(self.nz):
                for c in range(CORES):
                    d2, z2, c2 = to(d, z, c)
                    pairs.append(
                        (d * self.nf + z * CORES + c, d2 * self.nf + z2 * CORES + c2)
                    )
        return lax.ppermute(x, AXES, pairs)

    def swap_t(self, x, mask):
        return self.send(x, lambda d, z, c: (d ^ mask, z, c))

    def shift_z(self, x, step=1):
        return self.send(x, lambda d, z, c: (d, (z + step) % self.nz, c))

    def swap_core(self, x):
        return self.send(x, lambda d, z, c: (d, z, CORES - 1 - c))


def later(x, *after):
    return lax.optimization_barrier((x,) + after)[0]


def add(a, b):
    return a.astype(f32) + b.astype(f32)


class RingSum:
    def __init__(self, place, where, theirs, mine):
        self.place, self.where, self.mine = place, where, mine
        self.got = place.swap_core(theirs)

    def run(self, kernel, arrays, outs, after=()):
        return call(kernel, [self.where, *arrays], outs, 6, after)[0]

    def begin(self, *after):
        kernel = functools.partial(ring_begin_kernel, self.place.nz)
        self.block = shape16(*self.mine.shape[1:])
        outs = [shape16(*self.mine.shape), self.block]
        self.chip, self.last = self.run(kernel, [self.mine, self.got], outs, after)
        self.moving = self.place.shift_z(self.last)
        self.sent = 1

    def step(self, *after):
        self.sent += 1
        kernel = functools.partial(ring_add_kernel, self.place.nz, self.sent)
        (self.last,) = self.run(kernel, [self.chip, self.moving], [self.block], after)
        self.moving = self.place.shift_z(self.last)

    def finish(self, kernel, outs, *after):
        while self.sent < self.place.nz - 1:
            self.step()
        return self.run(kernel, [self.chip, self.moving], outs, after)


class PlainSum:
    def __init__(self, place, terms):
        self.total = self.last = self.moving = plain_sum(place, terms)

    def begin(self, *after):
        pass

    step = begin


def plain_sum(place, terms):
    terms = lax.psum_scatter(terms, "dp", scatter_dimension=0, axis_index_groups=place.outer_groups)
    theirs = lax.dynamic_index_in_dim(terms, 1 - place.c, 1, keepdims=False)
    chip = lax.dynamic_index_in_dim(terms, place.c, 1, keepdims=False)
    chip = add(chip, place.swap_core(theirs)).astype(bf16)
    moving = None
    for step in range(1, place.nz + 1):
        own = lax.dynamic_index_in_dim(chip, (place.z - step) % place.nz, 0, keepdims=False)
        moving = own if moving is None else add(place.shift_z(moving), own).astype(bf16)
    return moving


def columns(place, heads_weight, up_weight, mask):
    rows, width3 = heads_weight.shape
    part = width3 // 3 // GROUP
    hidden_part = up_weight.shape[1] // GROUP
    to = place.t ^ mask
    joint = [
        lax.dynamic_slice_in_dim(heads_weight, (k * GROUP + to) * part, part, axis=1)
        for k in range(3)
    ]
    up = lax.dynamic_slice_in_dim(up_weight, to * hidden_part, hidden_part, axis=1)
    return jnp.concatenate(joint + [up], axis=1)


def spread(vector, at, count):
    n = vector.shape[0]
    row = jnp.tile(vector.astype(f32).reshape(1, n), (1, count))
    lane = lax.broadcasted_iota(jnp.int32, row.shape, 1)
    return jnp.where(lane // n == at, row, 0.0)


def small_gather(place, norm_gain, norm_bias, down_bias, up_bias, offsets, terminal):
    here = ((place.dp * place.nz) + place.z) * CORES + place.c
    count = place.ndp * place.nf
    rows = jnp.concatenate([spread(v, here, count) for v in (norm_gain, norm_bias, down_bias)])
    fsdp = (place.dp // GROUP * place.nz + place.z) * CORES + place.c
    own = spread(up_bias, fsdp, place.no * place.nf)
    lanes = rows.shape[1]
    both = jnp.concatenate([rows, jnp.pad(own, ((0, 0), (0, lanes - own.shape[1])))])
    if place.no > 1:
        both = lax.psum(both, "dp", axis_index_groups=place.outer_groups)
    shifted = [place.shift_z(both, s) for s in range(1, place.nz)]
    both = sum(shifted, both)
    both = both + place.swap_core(both)
    ends = jnp.concatenate([offsets, terminal]).astype(f32).reshape(1, -1)
    ends = jnp.pad(ends, ((0, 0), (0, lanes - ends.shape[1])))
    group = jnp.concatenate([both[:3], ends])
    others = [place.swap_t(group, m) for m in range(1, GROUP)]
    rows = sum((o[:3] for o in others), group[:3])
    windows = offsets.shape[0]
    ends = jnp.concatenate([g[3:4, : 2 * windows] for g in [group] + others])
    return rows, both[3:4, : own.shape[1]], ends


def shards(
    sizes,
    tokens,
    heads_weight,
    merge_weight,
    up_weight,
    up_bias,
    down_weight,
    down_bias,
    norm_gain,
    norm_bias,
    offsets,
    terminal,
    cotangent,
):
    place = Place(sizes)
    nz, no = place.nz, place.no
    _, length, width = tokens.shape
    half = length // 2
    head = width // HEADS
    rows = heads_weight.shape[0]
    hidden_rows = down_weight.shape[0]
    part = width // GROUP
    hidden_part = up_weight.shape[1] // GROUP
    fast = no == 1 and rows % 16 == 0 and 128 % rows == 0 and hidden_rows == 128 and part % 128 == 0
    number = place.dp * place.nf + place.z * CORES + place.c
    per = max(128 // rows, 1)
    fsdp = place.z * CORES + place.c
    where = jnp.stack([place.t, place.z, place.c, number % per, number // per, fsdp])
    where = where.astype(jnp.int32)
    own_tokens = tokens.reshape(length, width)
    own_grad = cotangent.reshape(length, width)

    if fast:
        vectors, at = 0.0, 0
        for v in (norm_gain, norm_bias, down_bias, up_bias):
            v = v.astype(f32)
            at = at if v.shape[0] < 128 else 128
            vectors += jnp.pad(v, (at, 256 - at - v.shape[0]))
            at += v.shape[0]
        *pieces, rows_block, tokens_low, tokens_high, grad_low, grad_high, _ = prepare(
            where,
            jnp.concatenate([offsets, terminal]),
            vectors.reshape(2, 128),
            heads_weight,
            up_weight,
            down_weight,
            merge_weight,
            own_tokens,
            own_grad,
        )
        joint = 3 * part + 128
    else:
        pieces = [columns(place, heads_weight, up_weight, m) for m in range(GROUP)]
        rows_block = jnp.concatenate([down_weight, merge_weight])
        tokens_low, tokens_high = own_tokens[:half], own_tokens[half:]
        grad_low, grad_high = own_grad[:half], own_grad[half:]
        joint = 3 * part
    arrived = [place.swap_t(pieces[m], m) for m in range(1, GROUP)]
    pieces = [pieces[0]] + arrived

    def outer(block):
        if no == 1:
            return block
        return lax.all_gather(block, "dp", axis_index_groups=place.outer_groups, tiled=True)

    joint_blocks = [outer(jnp.concatenate([p[:, :joint] for p in pieces]))]
    up_blocks = [outer(jnp.concatenate([p[:, joint:] for p in pieces]))]
    row_blocks = [outer(rows_block)]
    row_blocks.append(place.shift_z(row_blocks[0]))
    joint_blocks.append(place.shift_z(later(joint_blocks[0], row_blocks[1])))
    one_low = place.swap_t(later(tokens_low, *arrived), 1)
    two_high = place.swap_t(later(tokens_high, *arrived), 2)
    joint_swaps = [place.swap_core(joint_blocks[0])]
    up_blocks.append(place.shift_z(later(up_blocks[0], joint_blocks[1])))
    up_swaps = [place.swap_core(up_blocks[0])]
    joint_blocks.append(place.shift_z(later(joint_blocks[1], joint_swaps[0], one_low, two_high)))
    one_high = place.swap_t(later(tokens_high, one_low, two_high), 1)
    two_low = place.swap_t(later(tokens_low, one_low, two_high), 2)
    joint_swaps.append(place.swap_core(joint_blocks[1]))
    up_blocks.append(place.shift_z(later(up_blocks[1], up_swaps[0])))
    for step in range(3, nz):
        joint_blocks.append(
            place.shift_z(later(joint_blocks[-1], joint_swaps[1], one_high, two_low))
        )
    three_low = place.swap_t(one_low, 2)
    three_high = place.swap_t(two_high, 1)
    up_swaps.append(place.swap_core(up_blocks[1]))
    for step in range(3, nz):
        up_blocks.append(place.shift_z(later(up_blocks[-1], up_swaps[1])))
    for block in joint_blocks[2:-1]:
        joint_swaps.append(place.swap_core(block))
    joint_swaps.append(place.swap_core(later(joint_blocks[-1], three_low, three_high)))
    joint_pairs = list(zip(joint_blocks, joint_swaps))
    row_swaps = [place.swap_core(row_blocks[0])]
    row_blocks.append(place.shift_z(later(row_blocks[1], joint_blocks[-1], row_swaps[0])))
    row_swaps.append(place.swap_core(row_blocks[1]))
    grad_one_low = place.swap_t(later(grad_low, three_low, three_high), 1)
    grad_two_high = place.swap_t(later(grad_high, three_low, three_high), 2)

    if fast:
        heads, small = assemble(place, where, joint_pairs, [(rows, GROUP)], True)
        ends = joint_blocks[0]
    else:
        (heads,) = assemble(place, where, joint_pairs, [(rows, GROUP)])
        small, up_shift, ends = small_gather(
            place, norm_gain, norm_bias, down_bias, up_bias, offsets, terminal
        )
        up_shift = jnp.pad(up_shift, ((0, 4), (0, width - hidden_part)))
        small = jnp.concatenate([small, up_shift])
        ends = jnp.stack([ends // 16, ends % 16], axis=-1).reshape(GROUP, 1, 4)
        ends = jnp.pad(ends, ((0, 0), (4, 11), (0, 124))).reshape(16 * GROUP, 128)
    tables = turn_tables(length, head, 128)

    def attended_window(window, tokens, *after):
        return attend(window, ends, tokens, heads, small, tables, head, after)

    saved, units = [None] * GROUP, [None] * GROUP
    saved[0], done = attended_window(0, [tokens_low, tokens_high])
    saved[1], done = attended_window(1, [one_low, one_high], done, grad_one_low, grad_two_high)
    for block in up_blocks[2:]:
        up_swaps.append(place.swap_core(later(block, done)))
    grad_one_high = place.swap_t(later(grad_high, grad_one_low, grad_two_high, done), 1)
    grad_two_low = place.swap_t(later(grad_low, grad_one_low, grad_two_high, done), 2)
    saved[2], done = attended_window(2, [two_low, two_high], done)
    up_pairs = list(zip(up_blocks, up_swaps))
    (up,) = assemble(place, where, up_pairs, [(rows, GROUP)], after=[done, row_blocks[2]])
    for step in range(3, nz):
        row_blocks.append(place.shift_z(later(row_blocks[-1], row_swaps[1], up)))
    row_swaps.append(place.swap_core(later(row_blocks[2], up)))
    for window in range(3):
        units[window], done = hidden_units(saved[window][0], up, small, [done])
    saved[3], done = attended_window(
        3, [three_low, three_high], done, grad_one_high, grad_two_low, row_swaps[2]
    )
    grad_three_low = place.swap_t(later(grad_one_low, grad_one_high, grad_two_low), 2)
    grad_three_high = place.swap_t(later(grad_two_high, grad_one_high, grad_two_low), 1)
    for block in row_blocks[3:]:
        row_swaps.append(place.swap_core(later(block, done)))
    units[3], done = hidden_units(saved[3][0], up, small, [done])
    row_pairs = list(zip(row_blocks, row_swaps))
    down, merge = assemble(place, where, row_pairs, [(hidden_rows, 1), (rows, 1)], after=[done])
    acts, normed, attended, qkv, lse = zip(*saved)
    activated, slope = zip(*units)

    grads = [
        (grad_low, grad_high),
        (grad_one_low, grad_one_high),
        (grad_two_low, grad_two_high),
        (grad_three_low, grad_three_high),
    ]

    def out_of(window, *after):
        return out_terms(activated[window], attended[window], down, merge, after)

    def by_place(terms):
        terms = terms.reshape(no, GROUP, nz, CORES, rows, terms.shape[1])
        return terms.transpose(0, 2, 3, 1, 4, 5)

    def column_sum(grads, *after):
        if fast:
            (theirs, mine), done = column_grads(where, nz, rows, acts, grads, after)
            return RingSum(place, where, theirs, mine), done
        left, right = jnp.concatenate(acts), jnp.concatenate(grads)
        return PlainSum(place, by_place(dot(left, right, ((0,), (0,))).astype(bf16))), after[0]

    def row_sum_of(*after):
        flat = [h for pair in grads for h in pair]
        if fast:
            (theirs, mine), done = row_grads(where, nz, rows, activated, attended, flat, after)
            return RingSum(place, where, theirs, mine), done
        grad = jnp.concatenate(flat)
        down_terms = dot(jnp.concatenate(activated), grad, ((0,), (0,))).astype(bf16)
        merge_terms = dot(jnp.concatenate(attended), grad, ((0,), (0,))).astype(bf16)
        down_terms = down_terms.reshape(no, nz, CORES, hidden_rows, width)
        merge_terms = merge_terms.reshape(no, nz, CORES, rows, width)
        return PlainSum(place, jnp.concatenate([down_terms, merge_terms], axis=3)), after[0]

    outs = [None] * GROUP
    outs[3], done = out_of(3, done)
    out_low = place.swap_t(outs[3][0], 2)
    out_high = place.swap_t(outs[3][1], 1)
    hidden_grad, attended_grad = [None] * GROUP, [None] * GROUP
    joined_sums = [None] * GROUP
    for w in range(GROUP):
        (hidden_grad[w], attended_grad[w], joined_sums[w]), done = joined_grad(
            grads[w], down, merge, slope[w], [done]
        )
    row_sum, done = row_sum_of(done)
    outs[1], done = out_of(1, done)
    outs[2], done = out_of(2, done)
    out_one = [None, place.swap_t(outs[1][1], 1)]
    out_two = [place.swap_t(outs[2][0], 2), None]
    (one_low, two_high), done = add_pairs(outs[1][0], out_low, outs[2][1], out_high, after=[done])
    out_one[0] = place.swap_t(one_low, 1)
    out_two[1] = place.swap_t(two_high, 2)
    row_sum.begin(done)

    def back(window, *after):
        (mixed,), done = attend_back(
            window, ends, qkv[window], attended_grad[window], lse[window], tables, head, after
        )
        return mixed, done

    def acts_of(w, *after):
        return acts_grad(heads, up, mixed_grad[w], hidden_grad[w], normed[w], after)

    mixed_grad, terms, acts_sums = [None] * GROUP, [None] * GROUP, [None] * GROUP
    up_sum, done = column_sum(hidden_grad, done, row_sum.last)
    mixed_grad[3], done = back(3, done)
    up_sum.begin(done)
    terms[3], acts_sums[3], done = acts_of(3, done, up_sum.last)
    low = place.swap_t(terms[3][0], 2)
    high = place.swap_t(terms[3][1], 1)
    mixed_grad[1], done = back(1, done, row_sum.moving)
    row_sum.step(done)
    terms[1], acts_sums[1], done = acts_of(1, done, row_sum.last)
    one = [None, place.swap_t(terms[1][1], 1)]
    mixed_grad[2], done = back(2, done, up_sum.moving)
    up_sum.step(done)
    terms[2], acts_sums[2], done = acts_of(2, done, up_sum.last)
    two = [place.swap_t(terms[2][0], 2), None]
    mixed_grad[0], done = back(0, done, row_sum.moving, *out_one, *out_two)
    row_sum.step(done)
    heads_sum, done = column_sum(mixed_grad, done, up_sum.moving, row_sum.last)
    (one_low, two_high), done = add_pairs(terms[1][0], low, terms[2][1], high, after=[done])
    one[0] = place.swap_t(one_low, 1)
    two[1] = place.swap_t(two_high, 2)
    up_sum.step(done)
    terms[0], acts_sums[0], done = acts_of(0, done, up_sum.last)
    heads_sum.begin(done)
    outs[0], done = out_of(0, done, heads_sum.last, row_sum.moving)
    block_output = finish(
        finish_out_kernel,
        [tokens_low, tokens_high, small],
        [outs[0], out_one, out_two],
        [done],
    )

    (group_sums,), _ = call(
        small_sums_kernel,
        [*acts_sums, *joined_sums],
        [jax.ShapeDtypeStruct((8, width), f32)],
        2,
    )
    group_sums = group_sums + place.swap_core(group_sums)
    if no > 1:
        group_sums = lax.psum(group_sums, "dp", axis_index_groups=place.outer_groups)
    shifted = [place.shift_z(group_sums, s) for s in range(1, nz)]
    group_sums = sum(shifted, group_sums)
    all_sums = sum((place.swap_t(group_sums, m) for m in range(1, GROUP)), group_sums)

    def exchanged(blocks):
        return [blocks[0]] + [place.swap_t(blocks[m], m) for m in range(1, GROUP)]

    def finish_acts(*after):
        return finish(
            finish_grad_kernel,
            [tokens_low, tokens_high, grad_low, grad_high, small],
            [terms[0], one, two],
            after,
        )

    if fast:
        blocks = [shape16(rows, hidden_part)] * GROUP
        up_arrived = exchanged(up_sum.finish(ring_columns_kernel, blocks))
        heads_sum.step(block_output)
        grad_tokens = finish_acts()
        heads_sum.step(grad_tokens, *up_arrived[1:])
        blocks = [shape16(rows, 3 * part)] * GROUP
        heads_arrived = exchanged(heads_sum.finish(ring_columns_kernel, blocks))
        both = [jax.ShapeDtypeStruct((n, width), f32) for n in (hidden_rows, rows)]
        grad_down, grad_merge = row_sum.finish(ring_rows_kernel, both)
        grad_heads, grad_up, narrow, own = columns_out(
            where, group_sums, all_sums, up_arrived, heads_arrived
        )
        grad_gain, grad_bias, grad_down_bias = (narrow[k, :rows] for k in range(3))
        grad_up_bias = own[3, :hidden_rows]
    else:
        grad_tokens = finish_acts()

        def by_t(summed):
            blocks = [
                lax.dynamic_index_in_dim(summed, place.t ^ m, 0, keepdims=False)
                for m in range(GROUP)
            ]
            arrived = exchanged(blocks)
            return [lax.select_n(t ^ place.t, *arrived).astype(f32) for t in range(GROUP)]

        row_total = row_sum.total.astype(f32)
        grad_down, grad_merge = row_total[:hidden_rows], row_total[hidden_rows:]
        heads_by_t = by_t(heads_sum.total)
        grad_heads = jnp.concatenate(
            [h[:, k * part : (k + 1) * part] for k in range(3) for h in heads_by_t], axis=1
        )
        grad_up = jnp.concatenate(by_t(up_sum.total), axis=1)
        at = number * rows
        grad_gain, grad_bias = (
            lax.dynamic_slice_in_dim(all_sums[k], at, rows) for k in range(2)
        )
        grad_down_bias = lax.dynamic_slice_in_dim(group_sums[2], at, rows)
        at = (place.dp // GROUP * place.nf + fsdp) * hidden_rows
        grad_up_bias = lax.dynamic_slice_in_dim(group_sums[3], at, hidden_rows)
    return (
        block_output.reshape(tokens.shape),
        grad_tokens.reshape(tokens.shape),
        grad_heads,
        grad_merge,
        grad_up,
        grad_up_bias,
        grad_down,
        grad_down_bias,
        grad_gain,
        grad_bias,
    )


def solution(mesh):
    whole = P(AXES)
    return jax.shard_map(
        functools.partial(shards, dict(mesh.shape)),
        mesh=mesh,
        in_specs=(whole,) * 12,
        out_specs=(whole,) * 10,
        check_vma=False,
    )
```

```python
import functools

import jax
import jax.numpy as jnp
import numpy as np
from jax import lax
from jax.experimental import pallas as pl
from jax.experimental.pallas import tpu as pltpu
from jax.sharding import PartitionSpec as P

HEADS = 16
ROT = 32
CORES = 2
GROUP = 4
AXES = ("dp", "fsdp")

eps = 1e-05
big_negative = -1e30
gelu_scale = 0.7978845608028654
gelu_cubic = 0.044715

bf16 = jnp.bfloat16
f32 = jnp.float32


def turn_tables(length, head, lanes):
    position = np.arange(length, dtype=np.float32)
    exponent = np.arange(0, ROT, 2, dtype=np.float32) / np.float32(ROT)
    rate = (np.float32(1.0) / np.power(np.float32(10000.0), exponent)).astype(np.float32)
    phase = (position[:, None] * rate[None, :]).astype(np.float32)
    cosine = np.ones((length, head), np.float32)
    sine = np.zeros((length, head), np.float32)
    cosine[:, :ROT] = np.repeat(np.cos(phase), 2, axis=1)
    sine[:, :ROT] = np.repeat(np.sin(phase), 2, axis=1)
    sine[:, 0:ROT:2] *= -1.0
    copies = lanes // head
    return np.tile(cosine, (1, copies)), np.tile(sine, (1, copies))


def turned(values, cosine, sine):
    lanes = values.shape[1]
    even = lax.broadcasted_iota(jnp.int32, values.shape, 1) % 2 == 0
    other = jnp.where(even, pltpu.roll(values, lanes - 1, 1), pltpu.roll(values, 1, 1))
    return values * cosine + other * sine


def dot(a, b, dims=((1,), (0,))):
    return lax.dot_general(a, b, (dims, ((), ())), preferred_element_type=f32)


def allowed_pairs(ends, length):
    offset = (16.0 * ends[:, 0:1] + ends[:, 1:2]).astype(jnp.int32)
    end = (16.0 * ends[:, 2:3] + ends[:, 3:4]).astype(jnp.int32)
    key = lax.broadcasted_iota(jnp.int32, (length, 1), 0)
    query = lax.broadcasted_iota(jnp.int32, (1, length), 1)
    key_part = (key >= offset).astype(jnp.int32) + (key > end).astype(jnp.int32)
    query_part = (query >= offset).astype(jnp.int32) + (query > end).astype(jnp.int32)
    return (key_part == query_part) & (query >= key)


def spec(space):
    return pl.BlockSpec(memory_space=space)


def settings(mebibytes):
    return {
        "compiler_params": pltpu.CompilerParams(vmem_limit_bytes=mebibytes * 2**20),
        "cost_estimate": pl.CostEstimate(flops=1, bytes_accessed=1, transcendentals=0),
    }


TICK = jax.ShapeDtypeStruct((8, 128), jnp.float32)


def tick(ref):
    ref[...] = jnp.zeros_like(ref)


def call(kernel, ins, outs, mebibytes, after=(), scratch=()):
    many = len(ins)

    def body(*refs):
        rest = refs[many + len(after) :]
        tick(rest[len(outs)])
        kernel(*refs[:many], *rest[: len(outs)], *rest[len(outs) + 1 :])

    result = pl.pallas_call(
        body,
        in_specs=[spec(pltpu.SMEM if x.dtype == jnp.int32 else pltpu.VMEM) for x in ins]
        + [spec(pl.ANY)] * len(after),
        out_specs=[spec(pltpu.VMEM)] * (len(outs) + 1),
        out_shape=[*outs, TICK],
        scratch_shapes=list(scratch),
        **settings(mebibytes),
    )(*ins, *after)
    return result[:-1], result[-1]


def shape16(*dims):
    return jax.ShapeDtypeStruct(dims, bf16)


def stacked(refs):
    return jnp.concatenate([r[...] for r in refs])


def normalised(values):
    mean = jnp.mean(values, axis=-1, keepdims=True)
    centered = values - mean
    inverse_std = lax.rsqrt(jnp.mean(centered * centered, axis=-1, keepdims=True) + eps)
    return centered * inverse_std, inverse_std


def gelu_and_slope(h):
    square = h * h
    tanh_value = jnp.tanh(h * (gelu_scale + gelu_scale * gelu_cubic * square))
    half = 0.5 * (1.0 + tanh_value)
    slope = half + (0.5 * h) * (1.0 - tanh_value * tanh_value) * (
        gelu_scale + 3.0 * gelu_scale * gelu_cubic * square
    )
    return h * half, slope


def ends_of(window, ends_ref):
    rows, width = ends_ref.shape
    at = rows // GROUP * window
    return ends_ref[at : at + 16, width - 128 :].astype(f32)[4:5]


def attend_kernel(head, window, ends_ref, heads_ref, small_ref, cos_ref, sin_ref, *refs):
    tokens = refs[:-5]
    acts_ref, normed_ref, attended_ref, qkv_ref, lse_ref = refs[-5:]
    length, part = attended_ref.shape
    lanes = cos_ref.shape[1]
    normed, _ = normalised(stacked(tokens).astype(f32))
    normed_ref[...] = normed.astype(bf16)
    acts_ref[...] = (normed * small_ref[0:1, :] + small_ref[1:2, :]).astype(bf16)
    acts = acts_ref[...]
    query_all, keys_all, values_all = (
        dot(acts, heads_ref[:, k * part : (k + 1) * part]) for k in range(3)
    )
    allowed = allowed_pairs(ends_of(window, ends_ref), length)
    cosine, sine = cos_ref[...], sin_ref[...]
    lane = lax.broadcasted_iota(jnp.int32, (1, lanes), 1)
    for group in range(part // lanes):
        at = group * lanes
        query = (turned(query_all[:, at : at + lanes], cosine, sine) * head ** (-0.5)).astype(bf16)
        keys = turned(keys_all[:, at : at + lanes], cosine, sine).astype(bf16)
        values = values_all[:, at : at + lanes]
        qkv_ref[:, at : at + lanes] = query
        qkv_ref[:, part + at : part + at + lanes] = keys
        qkv_ref[:, 2 * part + at : 2 * part + at + lanes] = values.astype(bf16)
        values_turned = values.T.astype(bf16)
        outs = []
        for sub in range(lanes // head):
            mine = (lane >= sub * head) & (lane < (sub + 1) * head)
            scores = dot(jnp.where(mine, keys, 0), query, ((1,), (1,)))
            scores = jnp.where(allowed, scores, big_negative)
            top = jnp.max(scores, axis=0, keepdims=True)
            expo = jnp.exp(scores - top)
            total = jnp.sum(expo, axis=0, keepdims=True)
            probs = (expo * (1.0 / total)).astype(bf16)
            number = group * (lanes // head) + sub
            lse_ref[number : number + 1, :] = top + jnp.log(total)
            outs.append(dot(values_turned[sub * head : (sub + 1) * head, :], probs))
        attended_ref[:, at : at + lanes] = jnp.concatenate(outs, axis=0).T.astype(bf16)


def attend(window, ends, tokens, heads, small, tables, head, after=()):
    length, width = sum(t.shape[0] for t in tokens), tokens[0].shape[1]
    part = heads.shape[1] // 3
    outs = [shape16(length, w) for w in (width, width, part, 3 * part)]
    outs.append(jax.ShapeDtypeStruct((max(8, part // head), length), f32))
    kernel = functools.partial(attend_kernel, head, window)
    return call(kernel, [ends, heads, small, *tables, *tokens], outs, 6, after)


def hidden_kernel(up_ref, small_ref, acts_ref, activated_ref, slope_ref):
    acts = acts_ref[...]
    hidden_part = up_ref.shape[1]
    step = min(256, hidden_part)
    for at in range(0, hidden_part, step):
        hidden = dot(acts, up_ref[:, at : at + step])
        value, slope = gelu_and_slope(hidden + small_ref[3:4, at : at + step])
        activated_ref[:, at : at + step] = value.astype(bf16)
        slope_ref[:, at : at + step] = slope.astype(bf16)


def hidden_units(acts, up, small, after=()):
    outs = [shape16(acts.shape[0], up.shape[1])] * 2
    return call(hidden_kernel, [up, small, acts], outs, 4, after)


def out_kernel(down_ref, merge_ref, activated_ref, attended_ref, low_ref, high_ref):
    half, width = low_ref.shape
    activated, attended = activated_ref[...], attended_ref[...]
    step = min(256, width)
    for at in range(0, width, step):
        term = dot(activated, down_ref[:, at : at + step])
        term = (term + dot(attended, merge_ref[:, at : at + step])).astype(bf16)
        low_ref[:, at : at + step] = term[:half]
        high_ref[:, at : at + step] = term[half:]


def out_terms(activated, attended, down, merge, after=()):
    outs = [shape16(activated.shape[0] // 2, down.shape[1])] * 2
    return call(out_kernel, [down, merge, activated, attended], outs, 4, after)


def joined_grad_kernel(down_ref, merge_ref, slope_ref, *refs):
    hidden_ref, attended_ref, sums_ref = refs[-3:]
    hidden_part = hidden_ref.shape[1]
    grad = stacked(refs[:-3])
    sums_ref[...] = jnp.zeros_like(sums_ref)
    sums_ref[0:1, :] = jnp.sum(grad.astype(f32), axis=0, keepdims=True)
    step = min(256, hidden_part)
    for at in range(0, hidden_part, step):
        term = dot(grad, down_ref[at : at + step, :], ((1,), (1,)))
        term = (term * slope_ref[:, at : at + step].astype(f32)).astype(bf16)
        hidden_ref[:, at : at + step] = term
        sums_ref[1:2, at : at + step] = jnp.sum(term.astype(f32), axis=0, keepdims=True)
    attended_ref[...] = dot(grad, merge_ref[...], ((1,), (1,))).astype(bf16)


def joined_grad(grad, down, merge, slope, after=()):
    length, hidden_part = slope.shape
    outs = [shape16(length, hidden_part), shape16(length, merge.shape[0])]
    outs.append(jax.ShapeDtypeStruct((8, max(down.shape)), f32))
    return call(joined_grad_kernel, [down, merge, slope, *grad], outs, 5, after)


def attend_back_kernel(
    head, window, ends_ref, cos_ref, sin_ref, qkv_ref, grad_ref, lse_ref, mixed_ref
):
    length = qkv_ref.shape[0]
    part = qkv_ref.shape[1] // 3
    lanes = cos_ref.shape[1]
    allowed = allowed_pairs(ends_of(window, ends_ref), length)
    cosine, sine = cos_ref[...], -sin_ref[...]
    lane = lax.broadcasted_iota(jnp.int32, (1, lanes), 1)
    for group in range(part // lanes):
        at = group * lanes
        query = qkv_ref[:, at : at + lanes]
        keys = qkv_ref[:, part + at : part + at + lanes]
        values = qkv_ref[:, 2 * part + at : 2 * part + at + lanes]
        grad = grad_ref[:, at : at + lanes]
        keys_turned = keys.astype(f32).T.astype(bf16)
        values_grad = jnp.zeros((length, lanes), f32)
        keys_grad = jnp.zeros((length, lanes), f32)
        query_grads = []
        for sub in range(lanes // head):
            mine = (lane >= sub * head) & (lane < (sub + 1) * head)
            number = group * (lanes // head) + sub
            scores = dot(jnp.where(mine, keys, 0), query, ((1,), (1,)))
            probs = jnp.exp(
                jnp.where(allowed, scores, big_negative) - lse_ref[number : number + 1, :]
            )
            probs_grad = dot(jnp.where(mine, values, 0), grad, ((1,), (1,)))
            weighted = jnp.sum(probs * probs_grad, axis=0, keepdims=True)
            scores_grad = (probs * (probs_grad - weighted)).astype(bf16)
            values_grad += dot(probs.astype(bf16), jnp.where(mine, grad, 0))
            keys_grad += dot(scores_grad, jnp.where(mine, query, 0))
            query_grads.append(dot(keys_turned[sub * head : (sub + 1) * head, :], scores_grad))
        query_grad = jnp.concatenate(query_grads, axis=0).T * head ** (-0.5)
        mixed_ref[:, at : at + lanes] = turned(query_grad, cosine, sine).astype(bf16)
        mixed_ref[:, part + at : part + at + lanes] = turned(keys_grad, cosine, sine).astype(bf16)
        mixed_ref[:, 2 * part + at : 2 * part + at + lanes] = values_grad.astype(bf16)


def attend_back(window, ends, qkv, grad, lse, tables, head, after=()):
    kernel = functools.partial(attend_back_kernel, head, window)
    return call(kernel, [ends, *tables, qkv, grad, lse], [shape16(*qkv.shape)], 6, after)


def acts_grad_kernel(
    heads_ref, up_ref, mixed_ref, hidden_ref, normed_ref, low_ref, high_ref, sums_ref
):
    mixed, hidden = mixed_ref[...], hidden_ref[...]
    half, width = low_ref.shape
    step = min(256, width)
    sums_ref[...] = jnp.zeros_like(sums_ref)
    for at in range(0, width, step):
        term = dot(mixed, heads_ref[at : at + step, :], ((1,), (1,)))
        term += dot(hidden, up_ref[at : at + step, :], ((1,), (1,)))
        sums_ref[0:1, at : at + step] = jnp.sum(
            term * normed_ref[:, at : at + step].astype(f32), axis=0, keepdims=True
        )
        sums_ref[1:2, at : at + step] = jnp.sum(term, axis=0, keepdims=True)
        low_ref[:, at : at + step] = term[:half].astype(bf16)
        high_ref[:, at : at + step] = term[half:].astype(bf16)


def acts_grad(heads, up, mixed, hidden, normed, after=()):
    length, width = normed.shape
    outs = [shape16(length // 2, width)] * 2 + [jax.ShapeDtypeStruct((8, width), f32)]
    (low, high, sums), done = call(
        acts_grad_kernel, [heads, up, mixed, hidden, normed], outs, 5, after
    )
    return (low, high), sums, done


def joined_windows(refs, scratch):
    at = 0
    for ref in refs:
        rows = ref.shape[0]
        scratch[at : at + rows, :] = ref[...]
        at += rows


def halved(shape):
    return [shape16(shape.shape[0] // 2, *shape.shape[1:])] * 2


def row_grads_kernel(rows, place_ref, *refs):
    activated, attended, grads = refs[:GROUP], refs[GROUP : 2 * GROUP], refs[2 * GROUP : -6]
    *theirs, mine_ref, a_ref, b_ref, g_ref = refs[-6:]
    joined_windows(activated, a_ref)
    joined_windows(attended, b_ref)
    joined_windows(grads, g_ref)
    first = place_ref[2] == 0
    grad = g_ref[...]
    at = 0
    for ref, size in ((a_ref, mine_ref.shape[1] - rows), (b_ref, rows)):
        step = min(256, ref.shape[1])
        for start in range(0, ref.shape[1], step):
            term = dot(ref[:, start : start + step], grad, ((0,), (0,))).astype(bf16)
            for pair in range(step // (CORES * size)):
                z = start // (CORES * size) + pair
                zero = term[pair * 2 * size : (pair * 2 + 1) * size]
                one = term[(pair * 2 + 1) * size : (pair * 2 + 2) * size]
                mine_ref[z, at : at + size, :] = jnp.where(first, zero, one)
                theirs[z // 2][z % 2, at : at + size, :] = jnp.where(first, one, zero)
        at += size


def row_grads(where, steps, rows, activated, attended, grads, after=()):
    length, hidden_part = activated[0].shape
    part = attended[0].shape[1]
    width = grads[0].shape[1]
    out = shape16(steps, hidden_part // (steps * CORES) + rows, width)
    scratch = [pltpu.VMEM((GROUP * length, w), bf16) for w in (hidden_part, part, width)]
    ins = [where, *activated, *attended, *grads]
    kernel = functools.partial(row_grads_kernel, rows)
    return call(kernel, ins, [*halved(out), out], 12, after, scratch)


def column_grads_kernel(rows, sums, place_ref, *refs):
    *theirs, mine_ref, a_ref, b_ref = refs[-5:]
    steps = mine_ref.shape[0]
    columns = b_ref.shape[1]
    joined_windows(refs[:GROUP], a_ref)
    joined_windows(refs[GROUP : 2 * GROUP], b_ref)
    first = place_ref[2] == 0
    grad = b_ref[...]
    step = steps * CORES * rows
    if sums:
        refs = refs[2 * GROUP :]
        acts_sums = sum((r[0:2, :] for r in refs[1:GROUP]), refs[0][0:2, :])
        joined_sums = sum((r[0:2, :] for r in refs[GROUP + 1 : 2 * GROUP]), refs[GROUP][0:2, :])
        row = lax.broadcasted_iota(jnp.int32, (rows, 128), 0)

        def tiles(t, z, c):
            number = (t * steps + z) * CORES + c
            at, up = number * rows // 128 * 128, (z * CORES + c) * 128
            value = jnp.zeros((rows, 128), f32)
            for k, line in enumerate(
                (
                    acts_sums[0:1, at : at + 128],
                    acts_sums[1:2, at : at + 128],
                    joined_sums[0:1, at : at + 128],
                    joined_sums[1:2, up : up + 128],
                )
            ):
                value = jnp.where(row == k, line, value)
            return value.astype(bf16)

    for t in range(GROUP):
        term = dot(a_ref[:, t * step : (t + 1) * step], grad, ((0,), (0,))).astype(bf16)
        here = slice(t * rows, (t + 1) * rows)
        for z in range(steps):
            zero = term[z * 2 * rows : (z * 2 + 1) * rows]
            one = term[(z * 2 + 1) * rows : (z * 2 + 2) * rows]
            mine_ref[z, here, :columns] = jnp.where(first, zero, one)
            theirs[z // 2][z % 2, here, :columns] = jnp.where(first, one, zero)
            if sums:
                zero, one = tiles(t, z, 0), tiles(t, z, 1)
                mine_ref[z, here, columns:] = jnp.where(first, zero, one)
                theirs[z // 2][z % 2, here, columns:] = jnp.where(first, one, zero)


def column_grads(where, steps, rows, acts, grads, after=(), sums=()):
    length, width = acts[0].shape
    columns = grads[0].shape[1]
    out = shape16(steps, GROUP * rows, columns + (128 if sums else 0))
    scratch = [pltpu.VMEM((GROUP * length, w), bf16) for w in (width, columns)]
    kernel = functools.partial(column_grads_kernel, rows, bool(sums))
    return call(kernel, [where, *acts, *grads, *sums], [*halved(out), out], 12, after, scratch)


def ring_begin_kernel(steps_on, place_ref, mine_ref, low_ref, high_ref, chip_ref, *firsts):
    steps = mine_ref.shape[0]
    for z in range(steps):
        got = (low_ref, high_ref)[z // 2][z % 2]
        chip_ref[z] = (mine_ref[z].astype(f32) + got.astype(f32)).astype(bf16)
    for on, ref in zip(steps_on, firsts):
        ref[...] = chip_ref[lax.rem(place_ref[1] + on, steps)]


def ring_add_kernel(on, place_ref, chip_ref, moving_ref, out_ref):
    at = lax.rem(place_ref[1] + on, chip_ref.shape[0])
    out_ref[...] = (chip_ref[at].astype(f32) + moving_ref[...].astype(f32)).astype(bf16)


def ring_rows_kernel(place_ref, chip_ref, *refs):
    down_ref, merge_ref = refs[-2:]
    total = chip_ref[place_ref[1]].astype(f32)
    for other in refs[:-2]:
        total += other[...].astype(f32)
    size = down_ref.shape[0]
    down_ref[...] = total[:size]
    merge_ref[...] = total[size:]


def ring_columns_kernel(count, place_ref, *refs):
    outs = refs[-GROUP:]
    rows = outs[0].shape[0]
    for mask in range(GROUP):
        t = jnp.bitwise_xor(place_ref[0], mask)
        at = pl.ds(pl.multiple_of(t * rows, rows), rows)
        column = 0
        for chip, *others in (refs[:count], refs[count:-GROUP]):
            total = chip[place_ref[1], at, :].astype(f32)
            for other in others:
                total += other[at, :].astype(f32)
            width = total.shape[1]
            outs[mask][:, column : column + width] = total.astype(bf16)
            column += width


def add_halves_kernel(*refs):
    one, two, low, high, one_ref, two_ref = refs[0:2], refs[2:4], *refs[4:]
    half = low.shape[0]
    one_ref[:half] = (one[0][...].astype(f32) + low[...].astype(f32)).astype(bf16)
    one_ref[half:] = one[1][...]
    two_ref[:half] = two[0][...]
    two_ref[half:] = (two[1][...].astype(f32) + high[...].astype(f32)).astype(bf16)


def add_halves(one, two, low, high, after=()):
    outs = [shape16(2 * low.shape[0], low.shape[1])] * 2
    return call(add_halves_kernel, [*one, *two, low, high], outs, 4, after)


def summed(own, one, two):
    return stacked(own).astype(f32) + one[...].astype(f32) + two[...].astype(f32)


def finish_out_kernel(tokens_ref, small_ref, low_ref, high_ref, one_ref, two_ref, out_ref):
    total = summed([low_ref, high_ref], one_ref, two_ref)
    out_ref[...] = (tokens_ref[...].astype(f32) + total + small_ref[2:3, :]).astype(bf16)


def finish_grad_kernel(
    tokens_ref, grad_ref, small_ref, low_ref, high_ref, one_ref, two_ref, out_ref
):
    normed, inverse_std = normalised(tokens_ref[...].astype(f32))
    normed_grad = summed([low_ref, high_ref], one_ref, two_ref) * small_ref[0:1, :]
    mean = jnp.mean(normed_grad, axis=-1, keepdims=True)
    along = jnp.mean(normed_grad * normed, axis=-1, keepdims=True)
    grad = grad_ref[...].astype(f32)
    out_ref[...] = (grad + inverse_std * (normed_grad - mean - normed * along)).astype(bf16)


def finish(kernel, arrays, own, one, two, after=()):
    (out,), done = call(kernel, [*arrays, *own, one, two], [shape16(*one.shape)], 10, after)
    return out, done


def prepare_kernel(
    place_ref, ends_ref, small_ref, heads_ref, up_ref, down_ref, merge_ref, *refs
):
    outs, sem = refs[: GROUP + 1], refs[-1]
    rows = heads_ref.shape[0]
    part = heads_ref.shape[1] // 3 // GROUP
    hidden_part = up_ref.shape[1] // GROUP
    hidden_rows = down_ref.shape[0]
    copies = []

    def copy(src, dst):
        copies.append(pltpu.make_async_copy(src, dst, sem.at[len(copies)]))

    for mask in range(GROUP):
        to = jnp.bitwise_xor(place_ref[0], mask)
        for k in range(3):
            at = pl.multiple_of((k * GROUP + to) * part, part)
            copy(heads_ref.at[:, pl.ds(at, part)], outs[mask].at[:, pl.ds(k * part, part)])
        at = pl.multiple_of(to * hidden_part, hidden_part)
        copy(
            up_ref.at[:, pl.ds(at, hidden_part)],
            outs[mask].at[:, pl.ds(3 * part + 128, hidden_part)],
        )
    copy(down_ref, outs[GROUP].at[pl.ds(0, hidden_rows)])
    copy(merge_ref, outs[GROUP].at[pl.ds(hidden_rows, rows)])
    for each in copies:
        each.start()
    quarter = place_ref[3]
    row = lax.broadcasted_iota(jnp.int32, (rows, 128), 0)
    lane = lax.broadcasted_iota(jnp.int32, (rows, 128), 1)
    first = jnp.broadcast_to(small_ref[0:1, :], (rows, 128))
    extra = jnp.zeros((rows, 128), f32)
    for k in range(3):
        moved = pltpu.roll(first, lax.rem(quarter * rows + (128 - k * rows), 128), 1)
        here = (row == k) & (lane >= quarter * rows) & (lane < (quarter + 1) * rows)
        extra = jnp.where(here, moved, extra)
    extra = jnp.where(row == 3, small_ref[1:2, :], extra)
    for k in range(2):
        value = ends_ref[k]
        for i, piece in enumerate((value // 16, value % 16)):
            extra = jnp.where((row == 4) & (lane == 2 * k + i), piece.astype(f32), extra)
    extra = extra.astype(bf16)
    for mask in range(GROUP):
        outs[mask][:, 3 * part : 3 * part + 128] = extra
    for each in copies:
        each.wait()


def prepare(where, ends, small, heads_weight, up_weight, down_weight, merge_weight):
    rows, width3 = heads_weight.shape
    columns = width3 // GROUP + up_weight.shape[1] // GROUP + 128
    block = (down_weight.shape[0] + merge_weight.shape[0], down_weight.shape[1])
    far = [heads_weight, up_weight, down_weight, merge_weight]
    far = [pltpu.with_memory_space_constraint(x, pltpu.HBM) for x in far]
    return pl.pallas_call(
        prepare_kernel,
        in_specs=[spec(pltpu.SMEM)] * 2 + [spec(pltpu.VMEM)] + [spec(pltpu.HBM)] * len(far),
        out_specs=[spec(pltpu.VMEM)] * (GROUP + 1),
        out_shape=[shape16(rows, columns)] * GROUP + [shape16(*block)],
        scratch_shapes=[pltpu.SemaphoreType.DMA((4 * GROUP + 2,))],
        **settings(2),
    )(where, ends, small, *far)


def small_rows_kernel(count, place_ref, extra_ref, small_ref):
    total = extra_ref.shape[0]
    rows = total // (count * GROUP)
    row = lax.broadcasted_iota(jnp.int32, (8, 128), 0)
    per = 128 // rows
    for tile in range(small_ref.shape[1] // 128):
        value = jnp.zeros((8, 128), f32)
        for i in range(per):
            at = (tile * per + i) * rows
            value += extra_ref[at : at + 16, :].astype(f32)[:8]
        if tile < count:
            at = pl.multiple_of((place_ref[0] * count + tile) * rows, rows)
            value = jnp.where(row == 3, extra_ref[pl.ds(at, 16), :].astype(f32)[:8], value)
        small_ref[:, tile * 128 : (tile + 1) * 128] = value


def assemble_kernel(layout, steps, with_small, sources, place_ref, *refs):
    count = steps * CORES
    extra_ref = refs[-1]
    outs = refs[-1 - len(layout) - with_small : -1]
    for number, (source, part) in enumerate(sources):
        piece = refs[source] if part is None else refs[source].at[part]
        z = place_ref[1] - number // CORES
        z = jnp.where(z < 0, z + steps, z)
        c = jnp.bitwise_xor(place_ref[2], number % CORES)
        row = 0
        for (rows, masks), out in zip(layout, outs):
            width = out.shape[1]
            for mask in range(masks):
                d = jnp.bitwise_xor(place_ref[0], mask) if masks > 1 else 0
                to = pl.ds(pl.multiple_of(((d * steps + z) * CORES + c) * rows, rows), rows)
                out[to, :] = piece[row : row + rows, :width]
                if with_small:
                    extra_ref[to, :] = piece[row : row + rows, width:]
                row += rows
    if with_small:
        small_rows_kernel(count, place_ref, extra_ref, outs[-1])


def assemble(place, where, arrays, sources, layout, with_small=False, after=()):
    width = arrays[0].shape[1] - (128 if with_small else 0)
    totals = [len(sources) * r * masks for r, masks in layout]
    outs = [shape16(total, width) for total in totals]
    if with_small:
        outs.append(jax.ShapeDtypeStruct((8, totals[0]), f32))
    kernel = functools.partial(assemble_kernel, layout, place.nz, with_small, sources)
    scratch = [pltpu.VMEM((totals[0], 128), bf16)]
    return call(kernel, [where, *arrays], outs, 2, after, scratch)


def stack_kernel(*refs):
    for i, ref in enumerate(refs[:-1]):
        refs[-1][i] = ref[...]


def stack(*arrays, after=()):
    (out,), done = call(stack_kernel, list(arrays), [shape16(len(arrays), *arrays[0].shape)], 2, after)
    return out, done


def halves_kernel(x_ref, low_ref, high_ref):
    half = low_ref.shape[0]
    low_ref[...] = x_ref[:half]
    high_ref[...] = x_ref[half:]


def halves(x, after=()):
    outs = [shape16(x.shape[0] // 2, x.shape[1])] * 2
    return call(halves_kernel, [x], outs, 3, after)


def cut_kernel(one_ref, two_ref, low_ref, high_ref):
    half = low_ref.shape[0]
    low_ref[...] = one_ref[:half]
    high_ref[...] = two_ref[half:]


def cut(one, two, after=()):
    outs = [shape16(one.shape[0] // 2, one.shape[1])] * 2
    return call(cut_kernel, [one, two], outs, 2, after)


def plain_assemble(place, pieces, layout):
    steps = place.nz
    flat = [piece for pair in pieces for piece in pair]
    width = flat[0].shape[1]
    stacked_pieces = jnp.stack(flat).reshape(steps, CORES, place.no, -1, width)
    stacked_pieces = jnp.take(stacked_pieces, (place.z - np.arange(steps)) % steps, axis=0)
    stacked_pieces = jnp.take(stacked_pieces, np.arange(CORES) ^ place.c, axis=1)
    outs, row = [], 0
    for r, masks in layout:
        part = stacked_pieces[:, :, :, row : row + r * masks]
        part = part.reshape(steps, CORES, place.no, masks, r, width)
        if masks > 1:
            part = jnp.take(part, np.arange(masks) ^ place.t, axis=3)
        outs.append(part.transpose(2, 3, 0, 1, 4, 5).reshape(-1, width))
        row += r * masks
    return outs


def columns_out_kernel(place_ref, *refs):
    blocks = refs[:GROUP]
    heads_out_ref, up_out_ref, small_ref = refs[GROUP:]
    rows = blocks[0].shape[0]
    hidden_part = up_out_ref.shape[1] // GROUP
    part = heads_out_ref.shape[1] // GROUP // 3
    total = jnp.zeros((16, 128), f32)
    for mask in range(GROUP):
        to = jnp.bitwise_xor(place_ref[0], mask)
        at = pl.multiple_of(to * hidden_part, hidden_part)
        up_out_ref[:, pl.ds(at, hidden_part)] = blocks[mask][:, :hidden_part].astype(f32)
        for k in range(3):
            at = pl.multiple_of((k * GROUP + to) * part, part)
            start = hidden_part + k * part
            heads_out_ref[:, pl.ds(at, part)] = blocks[mask][:, start : start + part].astype(f32)
        total += blocks[mask][:16, hidden_part + 3 * part :].astype(f32)
    own = blocks[0][:16, hidden_part + 3 * part :].astype(f32)
    row = lax.broadcasted_iota(jnp.int32, (16, 128), 0)
    value = jnp.where(row < 2, total, own)
    moved = pltpu.roll(value, lax.rem(128 - place_ref[3] * rows, 128), 1)
    small_ref[...] = jnp.where(row < 3, moved, value)[:8]


def columns_out(where, blocks, hidden_part):
    rows, columns = blocks[0].shape
    outs = [
        jax.ShapeDtypeStruct((rows, GROUP * (columns - 128 - hidden_part)), f32),
        jax.ShapeDtypeStruct((rows, GROUP * hidden_part), f32),
        jax.ShapeDtypeStruct((8, 128), f32),
    ]
    return call(columns_out_kernel, [where, *blocks], outs, 4)[0]


class Place:
    def __init__(self, sizes):
        self.ndp = sizes["dp"]
        self.no = self.ndp // GROUP
        self.nf = sizes["fsdp"]
        self.nz = self.nf // CORES
        fsdp = lax.axis_index("fsdp")
        self.dp = lax.axis_index("dp")
        self.t = self.dp % GROUP
        self.z = fsdp // CORES
        self.c = fsdp % CORES
        self.outer_groups = [[o * GROUP + t for o in range(self.no)] for t in range(GROUP)]

    def send(self, x, to):
        pairs = []
        for d in range(self.ndp):
            for z in range(self.nz):
                for c in range(CORES):
                    d2, z2, c2 = to(d, z, c)
                    pairs.append(
                        (d * self.nf + z * CORES + c, d2 * self.nf + z2 * CORES + c2)
                    )
        return lax.ppermute(x, AXES, pairs)

    def swap_t(self, x, mask):
        return self.send(x, lambda d, z, c: (d ^ mask, z, c))

    def shift_z(self, x, step=1):
        return self.send(x, lambda d, z, c: (d, (z + step) % self.nz, c))

    def swap_core(self, x):
        return self.send(x, lambda d, z, c: (d, z, CORES - 1 - c))


def later(x, *after):
    return lax.optimization_barrier((x,) + after)[0]


def add(a, b):
    return a.astype(f32) + b.astype(f32)


class RingSum:
    def __init__(self, place, where, theirs, mine, *after):
        self.place, self.where, self.mine = place, where, mine
        self.got = [place.swap_core(later(x, *after)) for x in theirs]

    def run(self, kernel, arrays, outs, after):
        return call(kernel, [self.where, *arrays], outs, 6, after)

    def first(self, steps_on, after):
        block = shape16(*self.mine.shape[1:])
        outs = [shape16(*self.mine.shape)] + [block] * len(steps_on)
        kernel = functools.partial(ring_begin_kernel, steps_on)
        (self.chip, *firsts), done = self.run(kernel, [self.mine, *self.got], outs, after)
        return firsts, done

    def added(self, on, after):
        outs = [shape16(*self.moving.shape)]
        kernel = functools.partial(ring_add_kernel, on)
        (out,), done = self.run(kernel, [self.chip, self.moving], outs, after)
        return out, done

    def begin(self, *after):
        (first,), done = self.first((3,), after)
        self.moving, self.on = self.place.shift_z(first), 3
        return done

    def step(self, *after):
        self.on -= 1
        out, done = self.added(self.on, after)
        self.moving = self.place.shift_z(out)
        return done

    def terms(self):
        return [self.chip, self.moving]


class PairSum(RingSum):
    def begin(self, *after):
        (far, back), done = self.first((2, 3), after)
        self.moving, self.back = self.place.shift_z(far), self.place.shift_z(back, -1)
        return done

    def step(self, *after):
        out, done = self.added(1, after)
        self.moving = self.place.shift_z(out)
        return done

    def terms(self):
        return [self.chip, self.back, self.moving]


def plain_sum(place, terms):
    terms = lax.psum_scatter(terms, "dp", scatter_dimension=0, axis_index_groups=place.outer_groups)
    theirs = lax.dynamic_index_in_dim(terms, 1 - place.c, 1, keepdims=False)
    chip = lax.dynamic_index_in_dim(terms, place.c, 1, keepdims=False)
    chip = add(chip, place.swap_core(theirs)).astype(bf16)
    moving = None
    for step in range(1, place.nz + 1):
        own = lax.dynamic_index_in_dim(chip, (place.z - step) % place.nz, 0, keepdims=False)
        moving = own if moving is None else add(place.shift_z(moving), own).astype(bf16)
    return moving.astype(f32)


def plain_gather(place, block):
    block = lax.all_gather(block, "dp", axis_index_groups=place.outer_groups, tiled=True)
    blocks = [block]
    for _ in range(place.nz - 1):
        blocks.append(place.shift_z(blocks[-1]))
    return [(b, place.swap_core(b)) for b in blocks]


def gather_windows(place, own):
    half = own.shape[0] // 2
    one, two = place.swap_t(own, 1), place.swap_t(own, 2)
    three = [place.swap_t(one[:half], 2), place.swap_t(two[half:], 1)]
    return [[own], [one], [two], three]


def sum_windows(place, terms):
    low, high = place.swap_t(terms[3][0], 2), place.swap_t(terms[3][1], 1)
    (one, two), _ = add_halves(terms[1], terms[2], low, high)
    return terms[0], place.swap_t(one, 1), place.swap_t(two, 2)


def columns(place, heads_weight, up_weight, mask):
    rows, width3 = heads_weight.shape
    part = width3 // 3 // GROUP
    hidden_part = up_weight.shape[1] // GROUP
    to = place.t ^ mask
    joint = [
        lax.dynamic_slice_in_dim(heads_weight, (k * GROUP + to) * part, part, axis=1)
        for k in range(3)
    ]
    up = lax.dynamic_slice_in_dim(up_weight, to * hidden_part, hidden_part, axis=1)
    return jnp.concatenate(joint + [up], axis=1)


def spread(vector, at, count):
    n = vector.shape[0]
    row = jnp.tile(vector.astype(f32).reshape(1, n), (1, count))
    lane = lax.broadcasted_iota(jnp.int32, row.shape, 1)
    return jnp.where(lane // n == at, row, 0.0)


def small_gather(place, norm_gain, norm_bias, down_bias, up_bias, offsets, terminal):
    here = ((place.dp * place.nz) + place.z) * CORES + place.c
    count = place.ndp * place.nf
    rows = jnp.concatenate([spread(v, here, count) for v in (norm_gain, norm_bias, down_bias)])
    fsdp = (place.dp // GROUP * place.nz + place.z) * CORES + place.c
    own = spread(up_bias, fsdp, place.no * place.nf)
    lanes = rows.shape[1]
    both = jnp.concatenate([rows, jnp.pad(own, ((0, 0), (0, lanes - own.shape[1])))])
    if place.no > 1:
        both = lax.psum(both, "dp", axis_index_groups=place.outer_groups)
    shifted = [place.shift_z(both, s) for s in range(1, place.nz)]
    both = sum(shifted, both)
    both = both + place.swap_core(both)
    ends = jnp.concatenate([offsets, terminal]).astype(f32).reshape(1, -1)
    ends = jnp.pad(ends, ((0, 0), (0, lanes - ends.shape[1])))
    group = jnp.concatenate([both[:3], ends])
    others = [place.swap_t(group, m) for m in range(1, GROUP)]
    rows = sum((o[:3] for o in others), group[:3])
    windows = offsets.shape[0]
    ends = jnp.concatenate([g[3:4, : 2 * windows] for g in [group] + others])
    return rows, both[3:4, : own.shape[1]], ends


def plain_shards(
    place,
    tokens,
    heads_weight,
    merge_weight,
    up_weight,
    up_bias,
    down_weight,
    down_bias,
    norm_gain,
    norm_bias,
    offsets,
    terminal,
    cotangent,
):
    nz, no = place.nz, place.no
    length, width = tokens.shape
    head = width // HEADS
    rows = heads_weight.shape[0]
    hidden_rows = down_weight.shape[0]
    part = width // GROUP
    hidden_part = up_weight.shape[1] // GROUP
    number = place.dp * place.nf + place.z * CORES + place.c
    tables = turn_tables(length, head, 128)
    pieces = [columns(place, heads_weight, up_weight, m) for m in range(GROUP)]
    pieces = jnp.concatenate([pieces[0]] + [place.swap_t(pieces[m], m) for m in range(1, GROUP)])
    layout = [(rows, GROUP)]
    (heads,) = plain_assemble(place, plain_gather(place, pieces[:, : 3 * part]), layout)
    (up,) = plain_assemble(place, plain_gather(place, pieces[:, 3 * part :]), layout)
    block = jnp.concatenate([down_weight, merge_weight])
    layout = [(hidden_rows, 1), (rows, 1)]
    down, merge = plain_assemble(place, plain_gather(place, block), layout)
    small, up_shift, ends = small_gather(
        place, norm_gain, norm_bias, down_bias, up_bias, offsets, terminal
    )
    up_shift = jnp.pad(up_shift, ((0, 4), (0, width - hidden_part)))
    small = jnp.concatenate([small, up_shift])
    ends = jnp.stack([jnp.floor(ends / 16.0), ends % 16.0], axis=-1).reshape(GROUP, 1, 4)
    ends = jnp.pad(ends, ((0, 0), (4, 11), (0, 124))).reshape(16 * GROUP, 128)
    windows = gather_windows(place, tokens)
    grads = gather_windows(place, cotangent)

    saved = [attend(w, ends, windows[w], heads, small, tables, head)[0] for w in range(GROUP)]
    acts, normed, attended, qkv, lse = zip(*saved)
    activated, slope = zip(*(hidden_units(a, up, small)[0] for a in acts))
    outs = [out_terms(activated[w], attended[w], down, merge)[0] for w in range(GROUP)]
    block_output, _ = finish(finish_out_kernel, [tokens, small], *sum_windows(place, outs))
    joined = [joined_grad(grads[w], down, merge, slope[w])[0] for w in range(GROUP)]
    hidden_grad, attended_grad, joined_sums = zip(*joined)
    mixed_grad, terms, acts_sums = [], [], []
    for w in range(GROUP):
        mixed = attend_back(w, ends, qkv[w], attended_grad[w], lse[w], tables, head)[0][0]
        halves, sums, _ = acts_grad(heads, up, mixed, hidden_grad[w], normed[w])
        mixed_grad.append(mixed)
        terms.append(halves)
        acts_sums.append(sums)
    grad_tokens, _ = finish(
        finish_grad_kernel, [tokens, cotangent, small], *sum_windows(place, terms)
    )

    def product(left, right):
        left, right = jnp.concatenate(left), jnp.concatenate(right)
        return dot(left, right, ((0,), (0,))).astype(bf16)

    def by_place(terms):
        terms = terms.reshape(no, GROUP, nz, CORES, rows, terms.shape[1])
        return terms.transpose(0, 2, 3, 1, 4, 5)

    def by_t(summed):
        blocks = [
            lax.dynamic_index_in_dim(summed, place.t ^ m, 0, keepdims=False) for m in range(GROUP)
        ]
        arrived = [blocks[0]] + [place.swap_t(blocks[m].astype(bf16), m) for m in range(1, GROUP)]
        arrived = [a.astype(f32) for a in arrived]
        return [lax.select_n(t ^ place.t, *arrived) for t in range(GROUP)]

    flat = [h for pair in grads for h in pair]
    down_terms = product(activated, flat).reshape(no, nz, CORES, hidden_rows, width)
    merge_terms = product(attended, flat).reshape(no, nz, CORES, rows, width)
    row_total = plain_sum(place, jnp.concatenate([down_terms, merge_terms], axis=3))
    heads_by_t = by_t(plain_sum(place, by_place(product(acts, mixed_grad))))
    up_by_t = by_t(plain_sum(place, by_place(product(acts, hidden_grad))))
    grad_heads = jnp.concatenate(
        [h[:, k * part : (k + 1) * part] for k in range(3) for h in heads_by_t], axis=1
    )
    group_sums = jnp.concatenate([sum(acts_sums)[:2], sum(joined_sums)[:2, :width]])
    group_sums = group_sums + place.swap_core(group_sums)
    group_sums = lax.psum(group_sums, "dp", axis_index_groups=place.outer_groups)
    group_sums = sum((place.shift_z(group_sums, s) for s in range(1, nz)), group_sums)
    all_sums = sum((place.swap_t(group_sums, m) for m in range(1, GROUP)), group_sums)
    grad_gain, grad_bias = (
        lax.dynamic_slice_in_dim(all_sums[k], number * rows, rows) for k in range(2)
    )
    at = (place.dp // GROUP * place.nf + place.z * CORES + place.c) * hidden_rows
    return (
        block_output,
        grad_tokens,
        grad_heads,
        row_total[hidden_rows:],
        jnp.concatenate(up_by_t, axis=1),
        lax.dynamic_slice_in_dim(group_sums[3], at, hidden_rows),
        row_total[:hidden_rows],
        lax.dynamic_slice_in_dim(group_sums[2], number * rows, rows),
        grad_gain,
        grad_bias,
    )


def paced_shards(
    place,
    tokens,
    heads_weight,
    merge_weight,
    up_weight,
    up_bias,
    down_weight,
    down_bias,
    norm_gain,
    norm_bias,
    offsets,
    terminal,
    cotangent,
):
    nz = place.nz
    length, width = tokens.shape
    head = width // HEADS
    rows = heads_weight.shape[0]
    hidden_rows = down_weight.shape[0]
    part = width // GROUP
    hidden_part = up_weight.shape[1] // GROUP
    number = place.dp * place.nf + place.z * CORES + place.c
    where = jnp.stack([place.t, place.z, place.c, number % (128 // rows)]).astype(jnp.int32)
    tables = turn_tables(length, head, 128)
    send, shift, swap = place.swap_t, place.shift_z, place.swap_core

    vectors, at = 0.0, 0
    for v in (norm_gain, norm_bias, down_bias, up_bias):
        v = v.astype(f32)
        at = at if v.shape[0] < 128 else 128
        vectors += jnp.pad(v, (at, 256 - at - v.shape[0]))
        at += v.shape[0]
    *pieces, row_block = prepare(
        where,
        jnp.concatenate([offsets, terminal]),
        vectors.reshape(2, 128),
        heads_weight,
        up_weight,
        down_weight,
        merge_weight,
    )
    joint = 3 * part + 128
    arrived = [send(pieces[m], m) for m in range(1, GROUP)]
    pieces = [pieces[0]] + arrived
    joint_block = jnp.concatenate([p[:, :joint] for p in pieces])
    up_block = jnp.concatenate([p[:, joint:] for p in pieces])

    joint_blocks, up_blocks, row_blocks = [joint_block], [up_block], [row_block]
    joint_blocks.append(shift(joint_block))
    tokens_one = send(later(tokens, *arrived), 1)
    tokens_two = send(later(tokens, *arrived), 2)
    joint_blocks.append(shift(joint_blocks[1]))
    early, _ = stack(*joint_blocks[:2])
    early = swap(early)
    up_blocks.append(shift(later(up_block, joint_blocks[1])))
    joint_blocks.append(shift(joint_blocks[2]))
    (three_low, three_high), cut_done = cut(tokens_one, tokens_two, [joint_blocks[2]])
    up_blocks.append(shift(later(up_blocks[1], joint_blocks[3])))
    late, _ = stack(*joint_blocks[2:], after=[cut_done])
    late = swap(late)
    three_low, three_high = send(three_low, 2), send(three_high, 1)
    sources = [(0, None), (4, 0), (1, None), (4, 1), (2, None), (5, 0), (3, None), (5, 1)]
    whole = [(k, None if k < 4 else i) for i in range(4) for k in (i, 4)]
    layout = [(rows, GROUP)]
    (heads, small), done = assemble(
        place, where, [*joint_blocks, early, late], sources, layout, True, [cut_done]
    )

    def attended_window(window, parts, *after):
        return attend(window, joint_block, parts, heads, small, tables, head, after)

    saved, units = [None] * GROUP, [None] * GROUP
    row_blocks.append(shift(later(row_block, joint_blocks[3])))
    saved[0], done = attended_window(0, [tokens], done)
    grad_one, grad_two = send(later(cotangent, done), 1), send(later(cotangent, done), 2)
    saved[1], done = attended_window(1, [tokens_one], done)
    up_blocks.append(shift(later(up_blocks[2], done)))
    saved[2], done = attended_window(2, [tokens_two], done)
    saved[3], done = attended_window(3, [three_low, three_high], done)
    early, done = stack(*up_blocks[:2], after=[done, row_blocks[1]])
    late, done = stack(*up_blocks[2:], after=[done])
    early, late = swap(early), swap(late)
    row_blocks.append(shift(later(row_blocks[1], done)))
    (up,), done = assemble(
        place, where, [*up_blocks, early, late], sources, layout, after=[done]
    )
    units[0], done = hidden_units(saved[0][0], up, small, [done])
    units[1], done = hidden_units(saved[1][0], up, small, [done])
    units[2], done = hidden_units(saved[2][0], up, small, [done])
    (grad_low, grad_high), done = cut(grad_one, grad_two, [done])
    grad_low, grad_high = send(grad_low, 2), send(grad_high, 1)
    row_blocks.append(shift(later(row_blocks[2], done)))
    units[3], done = hidden_units(saved[3][0], up, small, [done])
    acts, normed, attended, qkv, lse = zip(*saved)
    activated, slope = zip(*units)
    grads = [[cotangent], [grad_one], [grad_two], [grad_low, grad_high]]

    flat = [h for parts in grads for h in parts]
    early, done = stack(*row_blocks[:2], after=[done])
    early = swap(early)
    (*theirs, mine), done = row_grads(where, nz, rows, activated, attended, flat, [done])
    late, done = stack(*row_blocks[2:], after=[done])
    late = swap(late)
    row_sum = RingSum(place, where, theirs, mine, done)
    (down, merge), done = assemble(
        place,
        where,
        [*row_blocks, early, late],
        sources,
        [(hidden_rows, 1), (rows, 1)],
        after=[done],
    )

    def out_of(window, *after):
        return out_terms(activated[window], attended[window], down, merge, after)

    outs = [None] * GROUP
    outs[3], done = out_of(3, done)
    out_low, out_high = send(outs[3][0], 2), send(outs[3][1], 1)
    done = row_sum.begin(done)
    outs[1], done = out_of(1, done)
    outs[2], done = out_of(2, done)
    hidden_grad, attended_grad = [None] * GROUP, [None] * GROUP
    joined_sums = [None] * GROUP
    for w in range(GROUP):
        (hidden_grad[w], attended_grad[w], joined_sums[w]), done = joined_grad(
            grads[w], down, merge, slope[w], [done]
        )

    mixed_grad, terms, acts_sums = [None] * GROUP, [None] * GROUP, [None] * GROUP

    def acts_of(w, *after):
        return acts_grad(heads, up, mixed_grad[w], hidden_grad[w], normed[w], after)

    (*theirs, mine), done = column_grads(where, nz, rows, acts, hidden_grad, [done])
    after = [done, row_sum.moving]
    (out_one, out_two), done = add_halves(outs[1], outs[2], out_low, out_high, after)
    out_one, out_two = send(out_one, 1), send(out_two, 2)
    up_sum = RingSum(place, where, theirs, mine, done)
    done = up_sum.begin(done)

    def back(w, *after):
        (mixed_grad[w],), done = attend_back(
            w, joint_block, qkv[w], attended_grad[w], lse[w], tables, head, after
        )
        return done

    done = row_sum.step(done)
    done = back(3, done)
    done = back(1, done)
    done = up_sum.step(done)
    done = back(2, done)
    done = back(0, done)
    done = row_sum.step(done)
    terms[3], acts_sums[3], done = acts_of(3, done, out_one, out_two)
    low, high = send(terms[3][0], 2), send(terms[3][1], 1)
    terms[1], acts_sums[1], done = acts_of(1, done)
    terms[2], acts_sums[2], done = acts_of(2, done)
    done = up_sum.step(done)
    terms[0], acts_sums[0], done = acts_of(0, done)
    sums = [*acts_sums, *joined_sums]
    (*theirs, mine), done = column_grads(where, nz, rows, acts, mixed_grad, [done], sums)
    heads_sum = PairSum(place, where, theirs, mine, done)
    after = [done, up_sum.moving, row_sum.moving]
    (one, two), done = add_halves(terms[1], terms[2], low, high, after)
    one, two = send(one, 1), send(two, 2)
    outs[0], done = out_of(0, done)
    block_output, done = finish(
        finish_out_kernel, [tokens, small], outs[0], out_one, out_two, [done]
    )
    done = heads_sum.begin(done)
    done = heads_sum.step(done)
    grad_tokens, done = finish(
        finish_grad_kernel, [tokens, cotangent, small], terms[0], one, two, [done, heads_sum.back]
    )
    both = [jax.ShapeDtypeStruct((n, width), f32) for n in (hidden_rows, rows)]
    (grad_down, grad_merge), done = call(
        ring_rows_kernel, [where, *row_sum.terms()], both, 4, [done]
    )
    columns = hidden_part + 3 * part + 128
    blocks, done = call(
        functools.partial(ring_columns_kernel, len(up_sum.terms())),
        [where, *up_sum.terms(), *heads_sum.terms()],
        [shape16(rows, columns)] * GROUP,
        4,
        [done],
    )
    blocks = [blocks[0]] + [send(blocks[m], m) for m in range(1, GROUP)]
    grad_heads, grad_up, narrow = columns_out(where, blocks, hidden_part)
    grad_gain, grad_bias, grad_down_bias = (narrow[k, :rows] for k in range(3))
    return (
        block_output,
        grad_tokens,
        grad_heads,
        grad_merge,
        grad_up,
        narrow[3, :hidden_rows],
        grad_down,
        grad_down_bias,
        grad_gain,
        grad_bias,
    )


def shards(sizes, tokens, *arrays):
    *weights, cotangent = arrays
    place = Place(sizes)
    rows, hidden_rows, part = weights[0].shape[0], weights[4].shape[0], tokens.shape[2] // GROUP
    paced = (
        (place.no, place.nz) == (1, 4)
        and rows % 16 == 0
        and 128 % rows == 0
        and hidden_rows == 128
        and part % 128 == 0
    )
    run = paced_shards if paced else plain_shards
    block_output, grad_tokens, *grads = run(place, tokens[0], *weights, cotangent[0])
    return (block_output[None], grad_tokens[None], *grads)


def solution(mesh):
    whole = P(AXES)
    return jax.shard_map(
        functools.partial(shards, dict(mesh.shape)),
        mesh=mesh,
        in_specs=(whole,) * 12,
        out_specs=(whole,) * 10,
        check_vma=False,
    )
```

```python
import functools

import jax
import jax.numpy as jnp
import numpy as np
from jax import lax
from jax.experimental import pallas as pl
from jax.experimental.pallas import tpu as pltpu
from jax.sharding import PartitionSpec as P

HEADS = 16
ROT = 32
CORES = 2
GROUP = 4
AXES = ("dp", "fsdp")

eps = 1e-05
big_negative = -1e30
gelu_scale = 0.7978845608028654
gelu_cubic = 0.044715

bf16 = jnp.bfloat16
f32 = jnp.float32


def turn_tables(length, head, lanes):
    position = np.arange(length, dtype=np.float32)
    exponent = np.arange(0, ROT, 2, dtype=np.float32) / np.float32(ROT)
    rate = (np.float32(1.0) / np.power(np.float32(10000.0), exponent)).astype(np.float32)
    phase = (position[:, None] * rate[None, :]).astype(np.float32)
    cosine = np.ones((length, head), np.float32)
    sine = np.zeros((length, head), np.float32)
    cosine[:, :ROT] = np.repeat(np.cos(phase), 2, axis=1)
    sine[:, :ROT] = np.repeat(np.sin(phase), 2, axis=1)
    sine[:, 0:ROT:2] *= -1.0
    copies = lanes // head
    return np.tile(cosine, (1, copies)), np.tile(sine, (1, copies))


def turned(values, cosine, sine):
    lanes = values.shape[1]
    even = lax.broadcasted_iota(jnp.int32, values.shape, 1) % 2 == 0
    other = jnp.where(even, pltpu.roll(values, lanes - 1, 1), pltpu.roll(values, 1, 1))
    return values * cosine + other * sine


def dot(a, b, dims=((1,), (0,))):
    return lax.dot_general(a, b, (dims, ((), ())), preferred_element_type=f32)


def allowed_pairs(ends, length):
    offset = (16.0 * ends[:, 0:1] + ends[:, 1:2]).astype(jnp.int32)
    end = (16.0 * ends[:, 2:3] + ends[:, 3:4]).astype(jnp.int32)
    key = lax.broadcasted_iota(jnp.int32, (length, 1), 0)
    query = lax.broadcasted_iota(jnp.int32, (1, length), 1)
    key_part = (key >= offset).astype(jnp.int32) + (key > end).astype(jnp.int32)
    query_part = (query >= offset).astype(jnp.int32) + (query > end).astype(jnp.int32)
    return (key_part == query_part) & (query >= key)


def spec(space):
    return pl.BlockSpec(memory_space=space)


def settings(mebibytes):
    return {
        "compiler_params": pltpu.CompilerParams(vmem_limit_bytes=mebibytes * 2**20),
        "cost_estimate": pl.CostEstimate(flops=1, bytes_accessed=1, transcendentals=0),
    }


TICK = jax.ShapeDtypeStruct((8, 128), jnp.float32)


def tick(ref):
    ref[...] = jnp.zeros_like(ref)


def call(kernel, ins, outs, mebibytes, after=(), scratch=()):
    many = len(ins)

    def body(*refs):
        rest = refs[many + len(after) :]
        tick(rest[len(outs)])
        kernel(*refs[:many], *rest[: len(outs)], *rest[len(outs) + 1 :])

    result = pl.pallas_call(
        body,
        in_specs=[spec(pltpu.SMEM if x.dtype == jnp.int32 else pltpu.VMEM) for x in ins]
        + [spec(pl.ANY)] * len(after),
        out_specs=[spec(pltpu.VMEM)] * (len(outs) + 1),
        out_shape=[*outs, TICK],
        scratch_shapes=list(scratch),
        **settings(mebibytes),
    )(*ins, *after)
    return result[:-1], result[-1]


def shape16(*dims):
    return jax.ShapeDtypeStruct(dims, bf16)


def stacked(refs):
    return jnp.concatenate([r[...] for r in refs])


def normalised(values):
    mean = jnp.mean(values, axis=-1, keepdims=True)
    centered = values - mean
    inverse_std = lax.rsqrt(jnp.mean(centered * centered, axis=-1, keepdims=True) + eps)
    return centered * inverse_std, inverse_std


def gelu_and_slope(h):
    square = h * h
    tanh_value = jnp.tanh(h * (gelu_scale + gelu_scale * gelu_cubic * square))
    half = 0.5 * (1.0 + tanh_value)
    slope = half + (0.5 * h) * (1.0 - tanh_value * tanh_value) * (
        gelu_scale + 3.0 * gelu_scale * gelu_cubic * square
    )
    return h * half, slope


def ends_of(window, ends_ref):
    rows, width = ends_ref.shape
    at = rows // GROUP * window
    return ends_ref[at : at + 16, width - 128 :].astype(f32)[4:5]


def attend_kernel(head, window, ends_ref, heads_ref, small_ref, cos_ref, sin_ref, *refs):
    tokens = refs[:-5]
    acts_ref, normed_ref, attended_ref, qkv_ref, lse_ref = refs[-5:]
    length, part = attended_ref.shape
    lanes = cos_ref.shape[1]
    normed, _ = normalised(stacked(tokens).astype(f32))
    normed_ref[...] = normed.astype(bf16)
    acts_ref[...] = (normed * small_ref[0:1, :] + small_ref[1:2, :]).astype(bf16)
    acts = acts_ref[...]
    query_all, keys_all, values_all = (
        dot(acts, heads_ref[:, k * part : (k + 1) * part]) for k in range(3)
    )
    allowed = allowed_pairs(ends_of(window, ends_ref), length)
    cosine, sine = cos_ref[...], sin_ref[...]
    lane = lax.broadcasted_iota(jnp.int32, (1, lanes), 1)
    for group in range(part // lanes):
        at = group * lanes
        query = (turned(query_all[:, at : at + lanes], cosine, sine) * head ** (-0.5)).astype(bf16)
        keys = turned(keys_all[:, at : at + lanes], cosine, sine).astype(bf16)
        values = values_all[:, at : at + lanes]
        qkv_ref[:, at : at + lanes] = query
        qkv_ref[:, part + at : part + at + lanes] = keys
        qkv_ref[:, 2 * part + at : 2 * part + at + lanes] = values.astype(bf16)
        values_turned = values.T.astype(bf16)
        outs = []
        for sub in range(lanes // head):
            mine = (lane >= sub * head) & (lane < (sub + 1) * head)
            scores = dot(jnp.where(mine, keys, 0), query, ((1,), (1,)))
            scores = jnp.where(allowed, scores, big_negative)
            top = jnp.max(scores, axis=0, keepdims=True)
            expo = jnp.exp(scores - top)
            total = jnp.sum(expo, axis=0, keepdims=True)
            probs = (expo * (1.0 / total)).astype(bf16)
            number = group * (lanes // head) + sub
            lse_ref[number : number + 1, :] = top + jnp.log(total)
            outs.append(dot(values_turned[sub * head : (sub + 1) * head, :], probs))
        attended_ref[:, at : at + lanes] = jnp.concatenate(outs, axis=0).T.astype(bf16)


def attend(window, ends, tokens, heads, small, tables, head, after=()):
    length, width = sum(t.shape[0] for t in tokens), tokens[0].shape[1]
    part = heads.shape[1] // 3
    outs = [shape16(length, w) for w in (width, width, part, 3 * part)]
    outs.append(jax.ShapeDtypeStruct((max(8, part // head), length), f32))
    kernel = functools.partial(attend_kernel, head, window)
    return call(kernel, [ends, heads, small, *tables, *tokens], outs, 6, after)


def hidden_kernel(up_ref, small_ref, *refs):
    count = len(refs) // 3
    acts = stacked(refs[:count])
    length, hidden_part = refs[count].shape
    step = min(256, hidden_part)
    for at in range(0, hidden_part, step):
        here = slice(at, at + step)
        hidden = dot(acts, up_ref[:, here])
        value, slope = gelu_and_slope(hidden + small_ref[3:4, here])
        for w in range(count):
            rows = slice(w * length, (w + 1) * length)
            refs[count + w][:, here] = value[rows].astype(bf16)
            refs[2 * count + w][:, here] = slope[rows].astype(bf16)


def hidden_units(acts, up, small, after=()):
    outs = [shape16(acts[0].shape[0], up.shape[1])] * (2 * len(acts))
    outs, done = call(hidden_kernel, [up, small, *acts], outs, 8, after)
    return list(zip(outs[: len(acts)], outs[len(acts) :])), done


def out_kernel(down_ref, merge_ref, *refs):
    count = len(refs) // 4
    activated, attended = stacked(refs[:count]), stacked(refs[count : 2 * count])
    halves = refs[2 * count :]
    half, width = halves[0].shape
    step = min(256, width)
    for at in range(0, width, step):
        here = slice(at, at + step)
        term = dot(activated, down_ref[:, here])
        term = (term + dot(attended, merge_ref[:, here])).astype(bf16)
        for i, ref in enumerate(halves):
            ref[:, here] = term[i * half : (i + 1) * half]


def out_terms(activated, attended, down, merge, after=()):
    outs = [shape16(activated[0].shape[0] // 2, down.shape[1])] * (2 * len(activated))
    outs, done = call(out_kernel, [down, merge, *activated, *attended], outs, 8, after)
    return list(zip(outs[::2], outs[1::2])), done


def joined_grad_kernel(count, down_ref, merge_ref, *refs):
    slopes, grads, outs = refs[:count], refs[count : -3 * count], refs[-3 * count :]
    hiddens, attendeds, sums = outs[:count], outs[count : 2 * count], outs[2 * count :]
    length, hidden_part = hiddens[0].shape
    grad = stacked(grads)
    windows = [slice(w * length, (w + 1) * length) for w in range(count)]
    for ref, rows in zip(sums, windows):
        ref[...] = jnp.zeros_like(ref)
        ref[0:1, :] = jnp.sum(grad[rows].astype(f32), axis=0, keepdims=True)
    step = min(256, hidden_part)
    for at in range(0, hidden_part, step):
        here = slice(at, at + step)
        terms = dot(grad, down_ref[here, :], ((1,), (1,)))
        for w, rows in enumerate(windows):
            term = (terms[rows] * slopes[w][:, here].astype(f32)).astype(bf16)
            hiddens[w][:, here] = term
            sums[w][1:2, here] = jnp.sum(term.astype(f32), axis=0, keepdims=True)
    terms = dot(grad, merge_ref[...], ((1,), (1,))).astype(bf16)
    for ref, rows in zip(attendeds, windows):
        ref[...] = terms[rows]


def joined_grad(grads, down, merge, slopes, after=()):
    count = len(slopes)
    length, hidden_part = slopes[0].shape
    outs = [shape16(length, hidden_part)] * count + [shape16(length, merge.shape[0])] * count
    outs += [jax.ShapeDtypeStruct((8, max(down.shape)), f32)] * count
    flat = [part for parts in grads for part in parts]
    kernel = functools.partial(joined_grad_kernel, count)
    outs, done = call(kernel, [down, merge, *slopes, *flat], outs, 16, after)
    return [outs[k * count : (k + 1) * count] for k in range(3)], done


def attend_back_kernel(
    head, window, ends_ref, cos_ref, sin_ref, qkv_ref, grad_ref, lse_ref, mixed_ref
):
    length = qkv_ref.shape[0]
    part = qkv_ref.shape[1] // 3
    lanes = cos_ref.shape[1]
    allowed = allowed_pairs(ends_of(window, ends_ref), length)
    cosine, sine = cos_ref[...], -sin_ref[...]
    lane = lax.broadcasted_iota(jnp.int32, (1, lanes), 1)
    for group in range(part // lanes):
        at = group * lanes
        query = qkv_ref[:, at : at + lanes]
        keys = qkv_ref[:, part + at : part + at + lanes]
        values = qkv_ref[:, 2 * part + at : 2 * part + at + lanes]
        grad = grad_ref[:, at : at + lanes]
        keys_turned = keys.astype(f32).T.astype(bf16)
        values_grad = jnp.zeros((length, lanes), f32)
        keys_grad = jnp.zeros((length, lanes), f32)
        query_grads = []
        for sub in range(lanes // head):
            mine = (lane >= sub * head) & (lane < (sub + 1) * head)
            number = group * (lanes // head) + sub
            scores = dot(jnp.where(mine, keys, 0), query, ((1,), (1,)))
            probs = jnp.exp(
                jnp.where(allowed, scores, big_negative) - lse_ref[number : number + 1, :]
            )
            probs_grad = dot(jnp.where(mine, values, 0), grad, ((1,), (1,)))
            weighted = jnp.sum(probs * probs_grad, axis=0, keepdims=True)
            scores_grad = (probs * (probs_grad - weighted)).astype(bf16)
            values_grad += dot(probs.astype(bf16), jnp.where(mine, grad, 0))
            keys_grad += dot(scores_grad, jnp.where(mine, query, 0))
            query_grads.append(dot(keys_turned[sub * head : (sub + 1) * head, :], scores_grad))
        query_grad = jnp.concatenate(query_grads, axis=0).T * head ** (-0.5)
        mixed_ref[:, at : at + lanes] = turned(query_grad, cosine, sine).astype(bf16)
        mixed_ref[:, part + at : part + at + lanes] = turned(keys_grad, cosine, sine).astype(bf16)
        mixed_ref[:, 2 * part + at : 2 * part + at + lanes] = values_grad.astype(bf16)


def attend_back(window, ends, qkv, grad, lse, tables, head, after=()):
    kernel = functools.partial(attend_back_kernel, head, window)
    return call(kernel, [ends, *tables, qkv, grad, lse], [shape16(*qkv.shape)], 6, after)


def acts_grad_kernel(count, heads_ref, up_ref, *refs):
    mixed, hidden = stacked(refs[:count]), stacked(refs[count : 2 * count])
    normed = refs[2 * count : 3 * count]
    halves, sums = refs[3 * count : 5 * count], refs[5 * count :]
    half, width = halves[0].shape
    for ref in sums:
        ref[...] = jnp.zeros_like(ref)
    step = min(256, width)
    for at in range(0, width, step):
        here = slice(at, at + step)
        terms = dot(mixed, heads_ref[here, :], ((1,), (1,)))
        terms += dot(hidden, up_ref[here, :], ((1,), (1,)))
        for w, ref in enumerate(sums):
            term = terms[2 * w * half : 2 * (w + 1) * half]
            ref[0:1, here] = jnp.sum(
                term * normed[w][:, here].astype(f32), axis=0, keepdims=True
            )
            ref[1:2, here] = jnp.sum(term, axis=0, keepdims=True)
        for i, ref in enumerate(halves):
            ref[:, here] = terms[i * half : (i + 1) * half].astype(bf16)


def acts_grad(heads, up, mixed, hidden, normed, after=()):
    count = len(mixed)
    length, width = normed[0].shape
    outs = [shape16(length // 2, width)] * (2 * count)
    outs += [jax.ShapeDtypeStruct((8, width), f32)] * count
    kernel = functools.partial(acts_grad_kernel, count)
    outs, done = call(kernel, [heads, up, *mixed, *hidden, *normed], outs, 10, after)
    return list(zip(outs[0 : 2 * count : 2], outs[1 : 2 * count : 2])), outs[2 * count :], done


def joined_windows(refs, scratch):
    at = 0
    for ref in refs:
        rows = ref.shape[0]
        scratch[at : at + rows, :] = ref[...]
        at += rows


def halved(shape):
    return [shape16(shape.shape[0] // 2, *shape.shape[1:])] * 2


def row_grads_kernel(rows, place_ref, *refs):
    activated, attended, grads = refs[:GROUP], refs[GROUP : 2 * GROUP], refs[2 * GROUP : -6]
    *theirs, mine_ref, a_ref, b_ref, g_ref = refs[-6:]
    joined_windows(activated, a_ref)
    joined_windows(attended, b_ref)
    joined_windows(grads, g_ref)
    first = place_ref[2] == 0
    grad = g_ref[...]
    at = 0
    for ref, size in ((a_ref, mine_ref.shape[1] - rows), (b_ref, rows)):
        step = min(256, ref.shape[1])
        for start in range(0, ref.shape[1], step):
            term = dot(ref[:, start : start + step], grad, ((0,), (0,))).astype(bf16)
            for pair in range(step // (CORES * size)):
                z = start // (CORES * size) + pair
                zero = term[pair * 2 * size : (pair * 2 + 1) * size]
                one = term[(pair * 2 + 1) * size : (pair * 2 + 2) * size]
                mine_ref[z, at : at + size, :] = jnp.where(first, zero, one)
                theirs[z // 2][z % 2, at : at + size, :] = jnp.where(first, one, zero)
        at += size


def row_grads(where, steps, rows, activated, attended, grads, after=()):
    length, hidden_part = activated[0].shape
    part = attended[0].shape[1]
    width = grads[0].shape[1]
    out = shape16(steps, hidden_part // (steps * CORES) + rows, width)
    scratch = [pltpu.VMEM((GROUP * length, w), bf16) for w in (hidden_part, part, width)]
    ins = [where, *activated, *attended, *grads]
    kernel = functools.partial(row_grads_kernel, rows)
    return call(kernel, ins, [*halved(out), out], 12, after, scratch)


def column_grads_kernel(rows, sums, place_ref, *refs):
    *theirs, mine_ref, a_ref, b_ref = refs[-5:]
    steps = mine_ref.shape[0]
    columns = b_ref.shape[1]
    joined_windows(refs[:GROUP], a_ref)
    joined_windows(refs[GROUP : 2 * GROUP], b_ref)
    first = place_ref[2] == 0
    grad = b_ref[...]
    step = steps * CORES * rows
    if sums:
        refs = refs[2 * GROUP :]
        acts_sums = sum((r[0:2, :] for r in refs[1:GROUP]), refs[0][0:2, :])
        joined_sums = sum((r[0:2, :] for r in refs[GROUP + 1 : 2 * GROUP]), refs[GROUP][0:2, :])
        row = lax.broadcasted_iota(jnp.int32, (rows, 128), 0)

        def tiles(t, z, c):
            number = (t * steps + z) * CORES + c
            at, up = number * rows // 128 * 128, (z * CORES + c) * 128
            value = jnp.zeros((rows, 128), f32)
            for k, line in enumerate(
                (
                    acts_sums[0:1, at : at + 128],
                    acts_sums[1:2, at : at + 128],
                    joined_sums[0:1, at : at + 128],
                    joined_sums[1:2, up : up + 128],
                )
            ):
                value = jnp.where(row == k, line, value)
            return value.astype(bf16)

    for t in range(GROUP):
        term = dot(a_ref[:, t * step : (t + 1) * step], grad, ((0,), (0,))).astype(bf16)
        here = slice(t * rows, (t + 1) * rows)
        for z in range(steps):
            zero = term[z * 2 * rows : (z * 2 + 1) * rows]
            one = term[(z * 2 + 1) * rows : (z * 2 + 2) * rows]
            mine_ref[z, here, :columns] = jnp.where(first, zero, one)
            theirs[z // 2][z % 2, here, :columns] = jnp.where(first, one, zero)
            if sums:
                zero, one = tiles(t, z, 0), tiles(t, z, 1)
                mine_ref[z, here, columns:] = jnp.where(first, zero, one)
                theirs[z // 2][z % 2, here, columns:] = jnp.where(first, one, zero)


def column_grads(where, steps, rows, acts, grads, after=(), sums=()):
    length, width = acts[0].shape
    columns = grads[0].shape[1]
    out = shape16(steps, GROUP * rows, columns + (128 if sums else 0))
    scratch = [pltpu.VMEM((GROUP * length, w), bf16) for w in (width, columns)]
    kernel = functools.partial(column_grads_kernel, rows, bool(sums))
    return call(kernel, [where, *acts, *grads, *sums], [*halved(out), out], 12, after, scratch)


def ring_begin_kernel(steps_on, place_ref, mine_ref, low_ref, high_ref, chip_ref, *firsts):
    steps = mine_ref.shape[0]
    for z in range(steps):
        got = (low_ref, high_ref)[z // 2][z % 2]
        chip_ref[z] = (mine_ref[z].astype(f32) + got.astype(f32)).astype(bf16)
    for on, ref in zip(steps_on, firsts):
        ref[...] = chip_ref[lax.rem(place_ref[1] + on, steps)]


def ring_add_kernel(on, place_ref, chip_ref, moving_ref, out_ref):
    at = lax.rem(place_ref[1] + on, chip_ref.shape[0])
    out_ref[...] = (chip_ref[at].astype(f32) + moving_ref[...].astype(f32)).astype(bf16)


def ring_rows_kernel(place_ref, chip_ref, *refs):
    down_ref, merge_ref = refs[-2:]
    total = chip_ref[place_ref[1]].astype(f32)
    for other in refs[:-2]:
        total += other[...].astype(f32)
    size = down_ref.shape[0]
    down_ref[...] = total[:size]
    merge_ref[...] = total[size:]


def ring_columns_kernel(count, place_ref, *refs):
    outs = refs[-GROUP:]
    rows = outs[0].shape[0]
    for mask in range(GROUP):
        t = jnp.bitwise_xor(place_ref[0], mask)
        at = pl.ds(pl.multiple_of(t * rows, rows), rows)
        column = 0
        for chip, *others in (refs[:count], refs[count:-GROUP]):
            total = chip[place_ref[1], at, :].astype(f32)
            for other in others:
                total += other[at, :].astype(f32)
            width = total.shape[1]
            outs[mask][:, column : column + width] = total.astype(bf16)
            column += width


def add_halves_kernel(*refs):
    one, two, low, high, one_ref, two_ref = refs[0:2], refs[2:4], *refs[4:]
    half = low.shape[0]
    one_ref[:half] = (one[0][...].astype(f32) + low[...].astype(f32)).astype(bf16)
    one_ref[half:] = one[1][...]
    two_ref[:half] = two[0][...]
    two_ref[half:] = (two[1][...].astype(f32) + high[...].astype(f32)).astype(bf16)


def add_halves(one, two, low, high, after=()):
    outs = [shape16(2 * low.shape[0], low.shape[1])] * 2
    return call(add_halves_kernel, [*one, *two, low, high], outs, 4, after)


def summed(own, one, two):
    return stacked(own).astype(f32) + one[...].astype(f32) + two[...].astype(f32)


def finish_out_kernel(tokens_ref, small_ref, low_ref, high_ref, one_ref, two_ref, out_ref):
    total = summed([low_ref, high_ref], one_ref, two_ref)
    out_ref[...] = (tokens_ref[...].astype(f32) + total + small_ref[2:3, :]).astype(bf16)


def finish_grad_kernel(
    tokens_ref, grad_ref, small_ref, low_ref, high_ref, one_ref, two_ref, out_ref
):
    normed, inverse_std = normalised(tokens_ref[...].astype(f32))
    normed_grad = summed([low_ref, high_ref], one_ref, two_ref) * small_ref[0:1, :]
    mean = jnp.mean(normed_grad, axis=-1, keepdims=True)
    along = jnp.mean(normed_grad * normed, axis=-1, keepdims=True)
    grad = grad_ref[...].astype(f32)
    out_ref[...] = (grad + inverse_std * (normed_grad - mean - normed * along)).astype(bf16)


def finish(kernel, arrays, own, one, two, after=()):
    (out,), done = call(kernel, [*arrays, *own, one, two], [shape16(*one.shape)], 10, after)
    return out, done


def prepare_kernel(
    place_ref, ends_ref, small_ref, heads_ref, up_ref, down_ref, merge_ref, *refs
):
    outs, sem = refs[: GROUP + 1], refs[-1]
    rows = heads_ref.shape[0]
    part = heads_ref.shape[1] // 3 // GROUP
    hidden_part = up_ref.shape[1] // GROUP
    hidden_rows = down_ref.shape[0]
    copies = []

    def copy(src, dst):
        copies.append(pltpu.make_async_copy(src, dst, sem.at[len(copies)]))

    for mask in range(GROUP):
        to = jnp.bitwise_xor(place_ref[0], mask)
        for k in range(3):
            at = pl.multiple_of((k * GROUP + to) * part, part)
            copy(heads_ref.at[:, pl.ds(at, part)], outs[mask].at[:, pl.ds(k * part, part)])
        at = pl.multiple_of(to * hidden_part, hidden_part)
        copy(
            up_ref.at[:, pl.ds(at, hidden_part)],
            outs[mask].at[:, pl.ds(3 * part + 128, hidden_part)],
        )
    copy(down_ref, outs[GROUP].at[pl.ds(0, hidden_rows)])
    copy(merge_ref, outs[GROUP].at[pl.ds(hidden_rows, rows)])
    for each in copies:
        each.start()
    quarter = place_ref[3]
    row = lax.broadcasted_iota(jnp.int32, (rows, 128), 0)
    lane = lax.broadcasted_iota(jnp.int32, (rows, 128), 1)
    first = jnp.broadcast_to(small_ref[0:1, :], (rows, 128))
    extra = jnp.zeros((rows, 128), f32)
    for k in range(3):
        moved = pltpu.roll(first, lax.rem(quarter * rows + (128 - k * rows), 128), 1)
        here = (row == k) & (lane >= quarter * rows) & (lane < (quarter + 1) * rows)
        extra = jnp.where(here, moved, extra)
    extra = jnp.where(row == 3, small_ref[1:2, :], extra)
    for k in range(2):
        value = ends_ref[k]
        for i, piece in enumerate((value // 16, value % 16)):
            extra = jnp.where((row == 4) & (lane == 2 * k + i), piece.astype(f32), extra)
    extra = extra.astype(bf16)
    for mask in range(GROUP):
        outs[mask][:, 3 * part : 3 * part + 128] = extra
    for each in copies:
        each.wait()


def prepare(where, ends, small, heads_weight, up_weight, down_weight, merge_weight):
    rows, width3 = heads_weight.shape
    columns = width3 // GROUP + up_weight.shape[1] // GROUP + 128
    block = (down_weight.shape[0] + merge_weight.shape[0], down_weight.shape[1])
    far = [heads_weight, up_weight, down_weight, merge_weight]
    far = [pltpu.with_memory_space_constraint(x, pltpu.HBM) for x in far]
    return pl.pallas_call(
        prepare_kernel,
        in_specs=[spec(pltpu.SMEM)] * 2 + [spec(pltpu.VMEM)] + [spec(pltpu.HBM)] * len(far),
        out_specs=[spec(pltpu.VMEM)] * (GROUP + 1),
        out_shape=[shape16(rows, columns)] * GROUP + [shape16(*block)],
        scratch_shapes=[pltpu.SemaphoreType.DMA((4 * GROUP + 2,))],
        **settings(2),
    )(where, ends, small, *far)


def small_rows_kernel(count, place_ref, extra_ref, small_ref):
    total = extra_ref.shape[0]
    rows = total // (count * GROUP)
    row = lax.broadcasted_iota(jnp.int32, (8, 128), 0)
    per = 128 // rows
    for tile in range(small_ref.shape[1] // 128):
        value = jnp.zeros((8, 128), f32)
        for i in range(per):
            at = (tile * per + i) * rows
            value += extra_ref[at : at + 16, :].astype(f32)[:8]
        if tile < count:
            at = pl.multiple_of((place_ref[0] * count + tile) * rows, rows)
            value = jnp.where(row == 3, extra_ref[pl.ds(at, 16), :].astype(f32)[:8], value)
        small_ref[:, tile * 128 : (tile + 1) * 128] = value


def assemble_kernel(layout, steps, with_small, sources, place_ref, *refs):
    count = steps * CORES
    extra_ref = refs[-1]
    outs = refs[-1 - len(layout) - with_small : -1]
    for number, (source, part) in enumerate(sources):
        piece = refs[source] if part is None else refs[source].at[part]
        z = place_ref[1] - number // CORES
        z = jnp.where(z < 0, z + steps, z)
        c = jnp.bitwise_xor(place_ref[2], number % CORES)
        row = 0
        for (rows, masks), out in zip(layout, outs):
            width = out.shape[1]
            for mask in range(masks):
                d = jnp.bitwise_xor(place_ref[0], mask) if masks > 1 else 0
                to = pl.ds(pl.multiple_of(((d * steps + z) * CORES + c) * rows, rows), rows)
                out[to, :] = piece[row : row + rows, :width]
                if with_small:
                    extra_ref[to, :] = piece[row : row + rows, width:]
                row += rows
    if with_small:
        small_rows_kernel(count, place_ref, extra_ref, outs[-1])


def assemble(place, where, arrays, sources, layout, with_small=False, after=()):
    width = arrays[0].shape[1] - (128 if with_small else 0)
    totals = [len(sources) * r * masks for r, masks in layout]
    outs = [shape16(total, width) for total in totals]
    if with_small:
        outs.append(jax.ShapeDtypeStruct((8, totals[0]), f32))
    kernel = functools.partial(assemble_kernel, layout, place.nz, with_small, sources)
    scratch = [pltpu.VMEM((totals[0], 128), bf16)]
    return call(kernel, [where, *arrays], outs, 2, after, scratch)


def stack_kernel(*refs):
    for i, ref in enumerate(refs[:-1]):
        refs[-1][i] = ref[...]


def stack(*arrays, after=()):
    (out,), done = call(stack_kernel, list(arrays), [shape16(len(arrays), *arrays[0].shape)], 2, after)
    return out, done


def halves_kernel(x_ref, low_ref, high_ref):
    half = low_ref.shape[0]
    low_ref[...] = x_ref[:half]
    high_ref[...] = x_ref[half:]


def halves(x, after=()):
    outs = [shape16(x.shape[0] // 2, x.shape[1])] * 2
    return call(halves_kernel, [x], outs, 3, after)


def cut_kernel(one_ref, two_ref, low_ref, high_ref):
    half = low_ref.shape[0]
    low_ref[...] = one_ref[:half]
    high_ref[...] = two_ref[half:]


def cut(one, two, after=()):
    outs = [shape16(one.shape[0] // 2, one.shape[1])] * 2
    return call(cut_kernel, [one, two], outs, 2, after)


def plain_assemble(place, pieces, layout):
    steps = place.nz
    flat = [piece for pair in pieces for piece in pair]
    width = flat[0].shape[1]
    stacked_pieces = jnp.stack(flat).reshape(steps, CORES, place.no, -1, width)
    stacked_pieces = jnp.take(stacked_pieces, (place.z - np.arange(steps)) % steps, axis=0)
    stacked_pieces = jnp.take(stacked_pieces, np.arange(CORES) ^ place.c, axis=1)
    outs, row = [], 0
    for r, masks in layout:
        part = stacked_pieces[:, :, :, row : row + r * masks]
        part = part.reshape(steps, CORES, place.no, masks, r, width)
        if masks > 1:
            part = jnp.take(part, np.arange(masks) ^ place.t, axis=3)
        outs.append(part.transpose(2, 3, 0, 1, 4, 5).reshape(-1, width))
        row += r * masks
    return outs


def columns_out_kernel(place_ref, *refs):
    blocks = refs[:GROUP]
    heads_out_ref, up_out_ref, small_ref = refs[GROUP:]
    rows = blocks[0].shape[0]
    hidden_part = up_out_ref.shape[1] // GROUP
    part = heads_out_ref.shape[1] // GROUP // 3
    total = jnp.zeros((16, 128), f32)
    for mask in range(GROUP):
        to = jnp.bitwise_xor(place_ref[0], mask)
        at = pl.multiple_of(to * hidden_part, hidden_part)
        up_out_ref[:, pl.ds(at, hidden_part)] = blocks[mask][:, :hidden_part].astype(f32)
        for k in range(3):
            at = pl.multiple_of((k * GROUP + to) * part, part)
            start = hidden_part + k * part
            heads_out_ref[:, pl.ds(at, part)] = blocks[mask][:, start : start + part].astype(f32)
        total += blocks[mask][:16, hidden_part + 3 * part :].astype(f32)
    own = blocks[0][:16, hidden_part + 3 * part :].astype(f32)
    row = lax.broadcasted_iota(jnp.int32, (16, 128), 0)
    value = jnp.where(row < 2, total, own)
    moved = pltpu.roll(value, lax.rem(128 - place_ref[3] * rows, 128), 1)
    small_ref[...] = jnp.where(row < 3, moved, value)[:8]


def columns_out(where, blocks, hidden_part):
    rows, columns = blocks[0].shape
    outs = [
        jax.ShapeDtypeStruct((rows, GROUP * (columns - 128 - hidden_part)), f32),
        jax.ShapeDtypeStruct((rows, GROUP * hidden_part), f32),
        jax.ShapeDtypeStruct((8, 128), f32),
    ]
    return call(columns_out_kernel, [where, *blocks], outs, 4)[0]


class Place:
    def __init__(self, sizes):
        self.ndp = sizes["dp"]
        self.no = self.ndp // GROUP
        self.nf = sizes["fsdp"]
        self.nz = self.nf // CORES
        fsdp = lax.axis_index("fsdp")
        self.dp = lax.axis_index("dp")
        self.t = self.dp % GROUP
        self.z = fsdp // CORES
        self.c = fsdp % CORES
        self.outer_groups = [[o * GROUP + t for o in range(self.no)] for t in range(GROUP)]

    def send(self, x, to):
        pairs = []
        for d in range(self.ndp):
            for z in range(self.nz):
                for c in range(CORES):
                    d2, z2, c2 = to(d, z, c)
                    pairs.append(
                        (d * self.nf + z * CORES + c, d2 * self.nf + z2 * CORES + c2)
                    )
        return lax.ppermute(x, AXES, pairs)

    def swap_t(self, x, mask):
        return self.send(x, lambda d, z, c: (d ^ mask, z, c))

    def shift_z(self, x, step=1):
        return self.send(x, lambda d, z, c: (d, (z + step) % self.nz, c))

    def swap_core(self, x):
        return self.send(x, lambda d, z, c: (d, z, CORES - 1 - c))


def later(x, *after):
    return lax.optimization_barrier((x,) + after)[0]


def add(a, b):
    return a.astype(f32) + b.astype(f32)


class RingSum:
    def __init__(self, place, where, theirs, mine, *after):
        self.place, self.where, self.mine = place, where, mine
        self.got = [place.swap_core(later(x, *after)) for x in theirs]

    def run(self, kernel, arrays, outs, after):
        return call(kernel, [self.where, *arrays], outs, 6, after)

    def first(self, steps_on, after):
        block = shape16(*self.mine.shape[1:])
        outs = [shape16(*self.mine.shape)] + [block] * len(steps_on)
        kernel = functools.partial(ring_begin_kernel, steps_on)
        (self.chip, *firsts), done = self.run(kernel, [self.mine, *self.got], outs, after)
        return firsts, done

    def added(self, on, after):
        outs = [shape16(*self.moving.shape)]
        kernel = functools.partial(ring_add_kernel, on)
        (out,), done = self.run(kernel, [self.chip, self.moving], outs, after)
        return out, done

    def begin(self, *after):
        (first,), done = self.first((3,), after)
        self.moving, self.on = self.place.shift_z(first), 3
        return done

    def step(self, *after):
        self.on -= 1
        out, done = self.added(self.on, after)
        self.moving = self.place.shift_z(out)
        return done

    def terms(self):
        return [self.chip, self.moving]


class PairSum(RingSum):
    def begin(self, *after):
        (far, back), done = self.first((2, 3), after)
        self.moving, self.back = self.place.shift_z(far), self.place.shift_z(back, -1)
        return done

    def step(self, *after):
        out, done = self.added(1, after)
        self.moving = self.place.shift_z(out)
        return done

    def terms(self):
        return [self.chip, self.back, self.moving]


def plain_sum(place, terms):
    terms = lax.psum_scatter(terms, "dp", scatter_dimension=0, axis_index_groups=place.outer_groups)
    theirs = lax.dynamic_index_in_dim(terms, 1 - place.c, 1, keepdims=False)
    chip = lax.dynamic_index_in_dim(terms, place.c, 1, keepdims=False)
    chip = add(chip, place.swap_core(theirs)).astype(bf16)
    moving = None
    for step in range(1, place.nz + 1):
        own = lax.dynamic_index_in_dim(chip, (place.z - step) % place.nz, 0, keepdims=False)
        moving = own if moving is None else add(place.shift_z(moving), own).astype(bf16)
    return moving.astype(f32)


def plain_gather(place, block):
    block = lax.all_gather(block, "dp", axis_index_groups=place.outer_groups, tiled=True)
    blocks = [block]
    for _ in range(place.nz - 1):
        blocks.append(place.shift_z(blocks[-1]))
    return [(b, place.swap_core(b)) for b in blocks]


def gather_windows(place, own):
    half = own.shape[0] // 2
    one, two = place.swap_t(own, 1), place.swap_t(own, 2)
    three = [place.swap_t(one[:half], 2), place.swap_t(two[half:], 1)]
    return [[own], [one], [two], three]


def sum_windows(place, terms):
    low, high = place.swap_t(terms[3][0], 2), place.swap_t(terms[3][1], 1)
    (one, two), _ = add_halves(terms[1], terms[2], low, high)
    return terms[0], place.swap_t(one, 1), place.swap_t(two, 2)


def columns(place, heads_weight, up_weight, mask):
    rows, width3 = heads_weight.shape
    part = width3 // 3 // GROUP
    hidden_part = up_weight.shape[1] // GROUP
    to = place.t ^ mask
    joint = [
        lax.dynamic_slice_in_dim(heads_weight, (k * GROUP + to) * part, part, axis=1)
        for k in range(3)
    ]
    up = lax.dynamic_slice_in_dim(up_weight, to * hidden_part, hidden_part, axis=1)
    return jnp.concatenate(joint + [up], axis=1)


def spread(vector, at, count):
    n = vector.shape[0]
    row = jnp.tile(vector.astype(f32).reshape(1, n), (1, count))
    lane = lax.broadcasted_iota(jnp.int32, row.shape, 1)
    return jnp.where(lane // n == at, row, 0.0)


def small_gather(place, norm_gain, norm_bias, down_bias, up_bias, offsets, terminal):
    here = ((place.dp * place.nz) + place.z) * CORES + place.c
    count = place.ndp * place.nf
    rows = jnp.concatenate([spread(v, here, count) for v in (norm_gain, norm_bias, down_bias)])
    fsdp = (place.dp // GROUP * place.nz + place.z) * CORES + place.c
    own = spread(up_bias, fsdp, place.no * place.nf)
    lanes = rows.shape[1]
    both = jnp.concatenate([rows, jnp.pad(own, ((0, 0), (0, lanes - own.shape[1])))])
    if place.no > 1:
        both = lax.psum(both, "dp", axis_index_groups=place.outer_groups)
    shifted = [place.shift_z(both, s) for s in range(1, place.nz)]
    both = sum(shifted, both)
    both = both + place.swap_core(both)
    ends = jnp.concatenate([offsets, terminal]).astype(f32).reshape(1, -1)
    ends = jnp.pad(ends, ((0, 0), (0, lanes - ends.shape[1])))
    group = jnp.concatenate([both[:3], ends])
    others = [place.swap_t(group, m) for m in range(1, GROUP)]
    rows = sum((o[:3] for o in others), group[:3])
    windows = offsets.shape[0]
    ends = jnp.concatenate([g[3:4, : 2 * windows] for g in [group] + others])
    return rows, both[3:4, : own.shape[1]], ends


def plain_shards(
    place,
    tokens,
    heads_weight,
    merge_weight,
    up_weight,
    up_bias,
    down_weight,
    down_bias,
    norm_gain,
    norm_bias,
    offsets,
    terminal,
    cotangent,
):
    nz, no = place.nz, place.no
    length, width = tokens.shape
    head = width // HEADS
    rows = heads_weight.shape[0]
    hidden_rows = down_weight.shape[0]
    part = width // GROUP
    hidden_part = up_weight.shape[1] // GROUP
    number = place.dp * place.nf + place.z * CORES + place.c
    tables = turn_tables(length, head, 128)
    pieces = [columns(place, heads_weight, up_weight, m) for m in range(GROUP)]
    pieces = jnp.concatenate([pieces[0]] + [place.swap_t(pieces[m], m) for m in range(1, GROUP)])
    layout = [(rows, GROUP)]
    (heads,) = plain_assemble(place, plain_gather(place, pieces[:, : 3 * part]), layout)
    (up,) = plain_assemble(place, plain_gather(place, pieces[:, 3 * part :]), layout)
    block = jnp.concatenate([down_weight, merge_weight])
    layout = [(hidden_rows, 1), (rows, 1)]
    down, merge = plain_assemble(place, plain_gather(place, block), layout)
    small, up_shift, ends = small_gather(
        place, norm_gain, norm_bias, down_bias, up_bias, offsets, terminal
    )
    up_shift = jnp.pad(up_shift, ((0, 4), (0, width - hidden_part)))
    small = jnp.concatenate([small, up_shift])
    ends = jnp.stack([jnp.floor(ends / 16.0), ends % 16.0], axis=-1).reshape(GROUP, 1, 4)
    ends = jnp.pad(ends, ((0, 0), (4, 11), (0, 124))).reshape(16 * GROUP, 128)
    windows = gather_windows(place, tokens)
    grads = gather_windows(place, cotangent)

    saved = [attend(w, ends, windows[w], heads, small, tables, head)[0] for w in range(GROUP)]
    acts, normed, attended, qkv, lse = zip(*saved)
    activated, slope = zip(*(hidden_units([a], up, small)[0][0] for a in acts))
    outs = [out_terms([activated[w]], [attended[w]], down, merge)[0][0] for w in range(GROUP)]
    block_output, _ = finish(finish_out_kernel, [tokens, small], *sum_windows(place, outs))
    (hidden_grad, attended_grad, joined_sums), _ = joined_grad(grads, down, merge, slope)
    mixed_grad, terms, acts_sums = [], [], []
    for w in range(GROUP):
        mixed = attend_back(w, ends, qkv[w], attended_grad[w], lse[w], tables, head)[0][0]
        halves, sums, _ = acts_grad(heads, up, [mixed], [hidden_grad[w]], [normed[w]])
        mixed_grad.append(mixed)
        terms += halves
        acts_sums += sums
    grad_tokens, _ = finish(
        finish_grad_kernel, [tokens, cotangent, small], *sum_windows(place, terms)
    )

    def product(left, right):
        left, right = jnp.concatenate(left), jnp.concatenate(right)
        return dot(left, right, ((0,), (0,))).astype(bf16)

    def by_place(terms):
        terms = terms.reshape(no, GROUP, nz, CORES, rows, terms.shape[1])
        return terms.transpose(0, 2, 3, 1, 4, 5)

    def by_t(summed):
        blocks = [
            lax.dynamic_index_in_dim(summed, place.t ^ m, 0, keepdims=False) for m in range(GROUP)
        ]
        arrived = [blocks[0]] + [place.swap_t(blocks[m].astype(bf16), m) for m in range(1, GROUP)]
        arrived = [a.astype(f32) for a in arrived]
        return [lax.select_n(t ^ place.t, *arrived) for t in range(GROUP)]

    flat = [h for pair in grads for h in pair]
    down_terms = product(activated, flat).reshape(no, nz, CORES, hidden_rows, width)
    merge_terms = product(attended, flat).reshape(no, nz, CORES, rows, width)
    row_total = plain_sum(place, jnp.concatenate([down_terms, merge_terms], axis=3))
    heads_by_t = by_t(plain_sum(place, by_place(product(acts, mixed_grad))))
    up_by_t = by_t(plain_sum(place, by_place(product(acts, hidden_grad))))
    grad_heads = jnp.concatenate(
        [h[:, k * part : (k + 1) * part] for k in range(3) for h in heads_by_t], axis=1
    )
    group_sums = jnp.concatenate([sum(acts_sums)[:2], sum(joined_sums)[:2, :width]])
    group_sums = group_sums + place.swap_core(group_sums)
    group_sums = lax.psum(group_sums, "dp", axis_index_groups=place.outer_groups)
    group_sums = sum((place.shift_z(group_sums, s) for s in range(1, nz)), group_sums)
    all_sums = sum((place.swap_t(group_sums, m) for m in range(1, GROUP)), group_sums)
    grad_gain, grad_bias = (
        lax.dynamic_slice_in_dim(all_sums[k], number * rows, rows) for k in range(2)
    )
    at = (place.dp // GROUP * place.nf + place.z * CORES + place.c) * hidden_rows
    return (
        block_output,
        grad_tokens,
        grad_heads,
        row_total[hidden_rows:],
        jnp.concatenate(up_by_t, axis=1),
        lax.dynamic_slice_in_dim(group_sums[3], at, hidden_rows),
        row_total[:hidden_rows],
        lax.dynamic_slice_in_dim(group_sums[2], number * rows, rows),
        grad_gain,
        grad_bias,
    )


def paced_shards(
    place,
    tokens,
    heads_weight,
    merge_weight,
    up_weight,
    up_bias,
    down_weight,
    down_bias,
    norm_gain,
    norm_bias,
    offsets,
    terminal,
    cotangent,
):
    nz = place.nz
    length, width = tokens.shape
    head = width // HEADS
    rows = heads_weight.shape[0]
    hidden_rows = down_weight.shape[0]
    part = width // GROUP
    hidden_part = up_weight.shape[1] // GROUP
    number = place.dp * place.nf + place.z * CORES + place.c
    where = jnp.stack([place.t, place.z, place.c, number % (128 // rows)]).astype(jnp.int32)
    tables = turn_tables(length, head, 128)
    send, shift, swap = place.swap_t, place.shift_z, place.swap_core

    vectors, at = 0.0, 0
    for v in (norm_gain, norm_bias, down_bias, up_bias):
        v = v.astype(f32)
        at = at if v.shape[0] < 128 else 128
        vectors += jnp.pad(v, (at, 256 - at - v.shape[0]))
        at += v.shape[0]
    *pieces, row_block = prepare(
        where,
        jnp.concatenate([offsets, terminal]),
        vectors.reshape(2, 128),
        heads_weight,
        up_weight,
        down_weight,
        merge_weight,
    )
    joint = 3 * part + 128
    arrived = [send(pieces[m], m) for m in range(1, GROUP)]
    pieces = [pieces[0]] + arrived
    joint_block = jnp.concatenate([p[:, :joint] for p in pieces])
    up_block = jnp.concatenate([p[:, joint:] for p in pieces])

    joint_blocks, up_blocks, row_blocks = [joint_block], [up_block], [row_block]
    joint_blocks.append(shift(joint_block))
    tokens_one = send(later(tokens, *arrived), 1)
    tokens_two = send(later(tokens, *arrived), 2)
    joint_blocks.append(shift(joint_blocks[1]))
    early, _ = stack(*joint_blocks[:2])
    early = swap(early)
    up_blocks.append(shift(later(up_block, joint_blocks[1])))
    joint_blocks.append(shift(joint_blocks[2]))
    (three_low, three_high), cut_done = cut(tokens_one, tokens_two, [joint_blocks[2]])
    up_blocks.append(shift(later(up_blocks[1], joint_blocks[3])))
    third, fourth = swap(joint_blocks[2]), swap(later(joint_blocks[3], cut_done))
    three_low, three_high = send(three_low, 2), send(three_high, 1)
    sources = [(0, None), (4, 0), (1, None), (4, 1), (2, None), (5, 0), (3, None), (5, 1)]
    split = [*sources[:5], (5, None), (3, None), (6, None)]
    layout = [(rows, GROUP)]
    (heads, small), done = assemble(
        place, where, [*joint_blocks, early, third, fourth], split, layout, True, [cut_done]
    )

    def attended_window(window, parts, *after):
        return attend(window, joint_block, parts, heads, small, tables, head, after)

    saved, units = [None] * GROUP, [None] * GROUP
    row_blocks.append(shift(later(row_block, joint_blocks[3])))
    grad_one, grad_two = send(later(cotangent, done), 1), send(later(cotangent, done), 2)
    saved[0], done = attended_window(0, [tokens], done, three_low, three_high)
    saved[1], done = attended_window(1, [tokens_one], done)
    up_blocks.append(shift(later(up_blocks[2], done)))
    saved[2], done = attended_window(2, [tokens_two], done)
    saved[3], done = attended_window(3, [three_low, three_high], done)
    early, done = stack(*up_blocks[:2], after=[done, row_blocks[1]])
    late, done = stack(*up_blocks[2:], after=[done])
    early, late = swap(early), swap(late)
    row_blocks.append(shift(later(row_blocks[1], done)))
    (up,), done = assemble(
        place, where, [*up_blocks, early, late], sources, layout, after=[done]
    )
    units[0:1], done = hidden_units([saved[0][0]], up, small, [done])
    (grad_low, grad_high), done = cut(grad_one, grad_two, [done])
    grad_low, grad_high = send(grad_low, 2), send(grad_high, 1)
    units[1:3], done = hidden_units([saved[1][0], saved[2][0]], up, small, [done])
    row_blocks.append(shift(later(row_blocks[2], done)))
    units[3:4], done = hidden_units([saved[3][0]], up, small, [done])
    acts, normed, attended, qkv, lse = zip(*saved)
    activated, slope = zip(*units)
    grads = [[cotangent], [grad_one], [grad_two], [grad_low, grad_high]]

    flat = [h for parts in grads for h in parts]
    early, done = stack(*row_blocks[:2], after=[done])
    early = swap(early)
    (*theirs, mine), done = row_grads(where, nz, rows, activated, attended, flat, [done])
    late, done = stack(*row_blocks[2:], after=[done])
    late = swap(late)
    row_sum = RingSum(place, where, theirs, mine, done)
    (down, merge), done = assemble(
        place,
        where,
        [*row_blocks, early, late],
        sources,
        [(hidden_rows, 1), (rows, 1)],
        after=[done],
    )

    def out_of(windows, *after):
        picked = [activated[w] for w in windows], [attended[w] for w in windows]
        return out_terms(*picked, down, merge, after)

    outs = [None] * GROUP
    outs[3:4], done = out_of([3], done)
    out_low, out_high = send(outs[3][0], 2), send(outs[3][1], 1)
    done = row_sum.begin(done)
    outs[1:3], done = out_of([1, 2], done)
    (hidden_grad, attended_grad, joined_sums), done = joined_grad(grads, down, merge, slope, [done])

    mixed_grad, terms, acts_sums = [None] * GROUP, [None] * GROUP, [None] * GROUP

    def acts_of(windows, *after):
        picked = [[x[w] for w in windows] for x in (mixed_grad, hidden_grad, normed)]
        return acts_grad(heads, up, *picked, after)

    (*theirs, mine), done = column_grads(where, nz, rows, acts, hidden_grad, [done])
    after = [done, row_sum.moving]
    (out_one, out_two), done = add_halves(outs[1], outs[2], out_low, out_high, after)
    out_one, out_two = send(out_one, 1), send(out_two, 2)
    up_sum = RingSum(place, where, theirs, mine, done)
    done = up_sum.begin(done)

    def back(w, *after):
        (mixed_grad[w],), done = attend_back(
            w, joint_block, qkv[w], attended_grad[w], lse[w], tables, head, after
        )
        return done

    done = back(3, done)
    done = row_sum.step(done)
    done = back(1, done)
    done = back(2, done)
    done = up_sum.step(done)
    done = back(0, done)
    terms[3:4], acts_sums[3:4], done = acts_of([3], done, out_one, out_two)
    low, high = send(terms[3][0], 2), send(terms[3][1], 1)
    done = up_sum.step(done)
    terms[0:3], acts_sums[0:3], done = acts_of([0, 1, 2], done)
    sums = [*acts_sums, *joined_sums]
    (*theirs, mine), done = column_grads(where, nz, rows, acts, mixed_grad, [done], sums)
    heads_sum = PairSum(place, where, theirs, mine, done)
    done = row_sum.step(done)
    after = [done, up_sum.moving]
    (one, two), done = add_halves(terms[1], terms[2], low, high, after)
    one, two = send(one, 1), send(two, 2)
    done = heads_sum.begin(done)
    outs[0:1], done = out_of([0], done)
    block_output, done = finish(
        finish_out_kernel, [tokens, small], outs[0], out_one, out_two, [done]
    )
    done = heads_sum.step(done)
    grad_tokens, done = finish(
        finish_grad_kernel, [tokens, cotangent, small], terms[0], one, two, [done, heads_sum.back]
    )
    columns = hidden_part + 3 * part + 128
    blocks, done = call(
        functools.partial(ring_columns_kernel, len(up_sum.terms())),
        [where, *up_sum.terms(), *heads_sum.terms()],
        [shape16(rows, columns)] * GROUP,
        4,
        [done],
    )
    blocks = [blocks[0]] + [send(blocks[m], m) for m in range(1, GROUP)]
    both = [jax.ShapeDtypeStruct((n, width), f32) for n in (hidden_rows, rows)]
    (grad_down, grad_merge), done = call(
        ring_rows_kernel, [where, *row_sum.terms()], both, 4, [done]
    )
    grad_heads, grad_up, narrow = columns_out(where, blocks, hidden_part)
    grad_gain, grad_bias, grad_down_bias = (narrow[k, :rows] for k in range(3))
    return (
        block_output,
        grad_tokens,
        grad_heads,
        grad_merge,
        grad_up,
        narrow[3, :hidden_rows],
        grad_down,
        grad_down_bias,
        grad_gain,
        grad_bias,
    )


def shards(sizes, tokens, *arrays):
    *weights, cotangent = arrays
    place = Place(sizes)
    rows, hidden_rows, part = weights[0].shape[0], weights[4].shape[0], tokens.shape[2] // GROUP
    paced = (
        (place.no, place.nz) == (1, 4)
        and rows % 16 == 0
        and 128 % rows == 0
        and hidden_rows == 128
        and part % 128 == 0
    )
    run = paced_shards if paced else plain_shards
    block_output, grad_tokens, *grads = run(place, tokens[0], *weights, cotangent[0])
    return (block_output[None], grad_tokens[None], *grads)


def solution(mesh):
    whole = P(AXES)
    return jax.shard_map(
        functools.partial(shards, dict(mesh.shape)),
        mesh=mesh,
        in_specs=(whole,) * 12,
        out_specs=(whole,) * 10,
        check_vma=False,
    )
```

```python
import functools

import jax
import jax.numpy as jnp
import numpy as np
from jax import lax
from jax.experimental import pallas as pl
from jax.experimental.pallas import tpu as pltpu
from jax.sharding import PartitionSpec as P

HEADS = 16
ROT = 32
CORES = 2
GROUP = 4
AXES = ("dp", "fsdp")

eps = 1e-05
big_negative = -1e30
gelu_scale = 0.7978845608028654
gelu_cubic = 0.044715

bf16 = jnp.bfloat16
f32 = jnp.float32


def turn_tables(length, head, lanes):
    position = np.arange(length, dtype=np.float32)
    exponent = np.arange(0, ROT, 2, dtype=np.float32) / np.float32(ROT)
    rate = (np.float32(1.0) / np.power(np.float32(10000.0), exponent)).astype(np.float32)
    phase = (position[:, None] * rate[None, :]).astype(np.float32)
    cosine = np.ones((length, head), np.float32)
    sine = np.zeros((length, head), np.float32)
    cosine[:, :ROT] = np.repeat(np.cos(phase), 2, axis=1)
    sine[:, :ROT] = np.repeat(np.sin(phase), 2, axis=1)
    sine[:, 0:ROT:2] *= -1.0
    copies = lanes // head
    return np.tile(cosine, (1, copies)), np.tile(sine, (1, copies))


def turned(values, cosine, sine):
    lanes = values.shape[1]
    even = lax.broadcasted_iota(jnp.int32, values.shape, 1) % 2 == 0
    other = jnp.where(even, pltpu.roll(values, lanes - 1, 1), pltpu.roll(values, 1, 1))
    return values * cosine + other * sine


def dot(a, b, dims=((1,), (0,))):
    return lax.dot_general(a, b, (dims, ((), ())), preferred_element_type=f32)


def allowed_pairs(ends, length):
    offset = (16.0 * ends[:, 0:1] + ends[:, 1:2]).astype(jnp.int32)
    end = (16.0 * ends[:, 2:3] + ends[:, 3:4]).astype(jnp.int32)
    key = lax.broadcasted_iota(jnp.int32, (length, 1), 0)
    query = lax.broadcasted_iota(jnp.int32, (1, length), 1)
    key_part = (key >= offset).astype(jnp.int32) + (key > end).astype(jnp.int32)
    query_part = (query >= offset).astype(jnp.int32) + (query > end).astype(jnp.int32)
    return (key_part == query_part) & (query >= key)


def spec(space):
    return pl.BlockSpec(memory_space=space)


def settings(mebibytes):
    return {
        "compiler_params": pltpu.CompilerParams(vmem_limit_bytes=mebibytes * 2**20),
        "cost_estimate": pl.CostEstimate(flops=1, bytes_accessed=1, transcendentals=0),
    }


TICK = jax.ShapeDtypeStruct((8, 128), jnp.float32)


def tick(ref):
    ref[...] = jnp.zeros_like(ref)


def call(kernel, ins, outs, mebibytes, after=(), scratch=()):
    many = len(ins)

    def body(*refs):
        rest = refs[many + len(after) :]
        tick(rest[len(outs)])
        kernel(*refs[:many], *rest[: len(outs)], *rest[len(outs) + 1 :])

    result = pl.pallas_call(
        body,
        in_specs=[spec(pltpu.SMEM if x.dtype == jnp.int32 else pltpu.VMEM) for x in ins]
        + [spec(pl.ANY)] * len(after),
        out_specs=[spec(pltpu.VMEM)] * (len(outs) + 1),
        out_shape=[*outs, TICK],
        scratch_shapes=list(scratch),
        **settings(mebibytes),
    )(*ins, *after)
    return result[:-1], result[-1]


def shape16(*dims):
    return jax.ShapeDtypeStruct(dims, bf16)


def stacked(refs):
    return jnp.concatenate([r[...] for r in refs])


def normalised(values):
    mean = jnp.mean(values, axis=-1, keepdims=True)
    centered = values - mean
    inverse_std = lax.rsqrt(jnp.mean(centered * centered, axis=-1, keepdims=True) + eps)
    return centered * inverse_std, inverse_std


def gelu_and_slope(h):
    square = h * h
    tanh_value = jnp.tanh(h * (gelu_scale + gelu_scale * gelu_cubic * square))
    half = 0.5 + 0.5 * tanh_value
    value = h * half
    factor = 2.0 * gelu_scale + 6.0 * gelu_scale * gelu_cubic * square
    return value, half + (value - value * half) * factor


def ends_of(window, ends_ref):
    rows, width = ends_ref.shape
    at = rows // GROUP * window
    return ends_ref[at : at + 16, width - 128 :].astype(f32)[4:5]


def attend_kernel(head, window, ends_ref, heads_ref, small_ref, cos_ref, sin_ref, *refs):
    tokens = refs[:-5]
    acts_ref, normed_ref, attended_ref, qkv_ref, lse_ref = refs[-5:]
    length, part = attended_ref.shape
    lanes = cos_ref.shape[1]
    normed, _ = normalised(stacked(tokens).astype(f32))
    normed_ref[...] = normed.astype(bf16)
    acts_ref[...] = (normed * small_ref[0:1, :] + small_ref[1:2, :]).astype(bf16)
    acts = acts_ref[...]
    query_all, keys_all, values_all = (
        dot(acts, heads_ref[:, k * part : (k + 1) * part]) for k in range(3)
    )
    allowed = allowed_pairs(ends_of(window, ends_ref), length)
    cosine, sine = cos_ref[...], sin_ref[...]
    lane = lax.broadcasted_iota(jnp.int32, (1, lanes), 1)
    heads_of = [(at, sub) for at in range(0, part, lanes) for sub in range(lanes // head)]
    queries, scores, values_turned = {}, [], {}
    for at in range(0, part, lanes):
        query = (turned(query_all[:, at : at + lanes], cosine, sine) * head ** (-0.5)).astype(bf16)
        keys = turned(keys_all[:, at : at + lanes], cosine, sine).astype(bf16)
        values = values_all[:, at : at + lanes]
        qkv_ref[:, at : at + lanes] = query
        qkv_ref[:, part + at : part + at + lanes] = keys
        qkv_ref[:, 2 * part + at : 2 * part + at + lanes] = values.astype(bf16)
        values_turned[at] = values.T.astype(bf16)
        for sub in range(lanes // head):
            mine = (lane >= sub * head) & (lane < (sub + 1) * head)
            scores.append(dot(jnp.where(mine, keys, 0), query, ((1,), (1,))))
    probs = []
    for number, score in enumerate(scores):
        score = jnp.where(allowed, score, big_negative)
        top = jnp.max(score, axis=0, keepdims=True)
        expo = jnp.exp(score - top)
        total = jnp.sum(expo, axis=0, keepdims=True)
        probs.append((expo * (1.0 / total)).astype(bf16))
        lse_ref[number : number + 1, :] = top + jnp.log(total)
    outs = [
        dot(values_turned[at][sub * head : (sub + 1) * head, :], prob)
        for (at, sub), prob in zip(heads_of, probs)
    ]
    attended_ref[...] = jnp.concatenate(outs, axis=0).T.astype(bf16)


def attend(window, ends, tokens, heads, small, tables, head, after=()):
    length, width = sum(t.shape[0] for t in tokens), tokens[0].shape[1]
    part = heads.shape[1] // 3
    outs = [shape16(length, w) for w in (width, width, part, 3 * part)]
    outs.append(jax.ShapeDtypeStruct((max(8, part // head), length), f32))
    kernel = functools.partial(attend_kernel, head, window)
    return call(kernel, [ends, heads, small, *tables, *tokens], outs, 6, after)


def hidden_kernel(up_ref, small_ref, *refs):
    count = len(refs) // 3
    acts = stacked(refs[:count])
    length, hidden_part = refs[count].shape
    step = min(256, hidden_part)
    for at in range(0, hidden_part, step):
        here = slice(at, at + step)
        hidden = dot(acts, up_ref[:, here])
        value, slope = gelu_and_slope(hidden + small_ref[3:4, here])
        for w in range(count):
            rows = slice(w * length, (w + 1) * length)
            refs[count + w][:, here] = value[rows].astype(bf16)
            refs[2 * count + w][:, here] = slope[rows].astype(bf16)


def hidden_units(acts, up, small, after=()):
    outs = [shape16(acts[0].shape[0], up.shape[1])] * (2 * len(acts))
    outs, done = call(hidden_kernel, [up, small, *acts], outs, 8, after)
    return list(zip(outs[: len(acts)], outs[len(acts) :])), done


def out_kernel(down_ref, merge_ref, *refs):
    count = len(refs) // 4
    activated, attended = stacked(refs[:count]), stacked(refs[count : 2 * count])
    halves = refs[2 * count :]
    half, width = halves[0].shape
    step = min(256, width)
    for at in range(0, width, step):
        here = slice(at, at + step)
        term = dot(activated, down_ref[:, here])
        term = (term + dot(attended, merge_ref[:, here])).astype(bf16)
        for i, ref in enumerate(halves):
            ref[:, here] = term[i * half : (i + 1) * half]


def out_terms(activated, attended, down, merge, after=()):
    outs = [shape16(activated[0].shape[0] // 2, down.shape[1])] * (2 * len(activated))
    outs, done = call(out_kernel, [down, merge, *activated, *attended], outs, 8, after)
    return list(zip(outs[::2], outs[1::2])), done


def joined_grad_kernel(count, down_ref, merge_ref, *refs):
    slopes, grads, outs = refs[:count], refs[count : -3 * count], refs[-3 * count :]
    hiddens, attendeds, sums = outs[:count], outs[count : 2 * count], outs[2 * count :]
    length, hidden_part = hiddens[0].shape
    grad = stacked(grads)
    windows = [slice(w * length, (w + 1) * length) for w in range(count)]
    for ref, rows in zip(sums, windows):
        ref[...] = jnp.zeros_like(ref)
        ref[0:1, :] = jnp.sum(grad[rows].astype(f32), axis=0, keepdims=True)
    step = min(256, hidden_part)
    for at in range(0, hidden_part, step):
        here = slice(at, at + step)
        terms = dot(grad, down_ref[here, :], ((1,), (1,)))
        for w, rows in enumerate(windows):
            term = (terms[rows] * slopes[w][:, here].astype(f32)).astype(bf16)
            hiddens[w][:, here] = term
            sums[w][1:2, here] = jnp.sum(term.astype(f32), axis=0, keepdims=True)
    terms = dot(grad, merge_ref[...], ((1,), (1,))).astype(bf16)
    for ref, rows in zip(attendeds, windows):
        ref[...] = terms[rows]


def joined_grad(grads, down, merge, slopes, after=()):
    count = len(slopes)
    length, hidden_part = slopes[0].shape
    outs = [shape16(length, hidden_part)] * count + [shape16(length, merge.shape[0])] * count
    outs += [jax.ShapeDtypeStruct((8, max(down.shape)), f32)] * count
    flat = [part for parts in grads for part in parts]
    kernel = functools.partial(joined_grad_kernel, count)
    outs, done = call(kernel, [down, merge, *slopes, *flat], outs, 16, after)
    return [outs[k * count : (k + 1) * count] for k in range(3)], done


def attend_back_kernel(
    head, window, ends_ref, cos_ref, sin_ref, qkv_ref, grad_ref, lse_ref, mixed_ref
):
    length = qkv_ref.shape[0]
    part = qkv_ref.shape[1] // 3
    lanes = cos_ref.shape[1]
    allowed = allowed_pairs(ends_of(window, ends_ref), length)
    cosine, sine = cos_ref[...], -sin_ref[...]
    lane = lax.broadcasted_iota(jnp.int32, (1, lanes), 1)
    for group in range(part // lanes):
        at = group * lanes
        query = qkv_ref[:, at : at + lanes]
        keys = qkv_ref[:, part + at : part + at + lanes]
        values = qkv_ref[:, 2 * part + at : 2 * part + at + lanes]
        grad = grad_ref[:, at : at + lanes]
        keys_turned = keys.astype(f32).T.astype(bf16)
        subs = range(lanes // head)
        mines = [(lane >= sub * head) & (lane < (sub + 1) * head) for sub in subs]
        scores = [dot(jnp.where(m, keys, 0), query, ((1,), (1,))) for m in mines]
        probs_grads = [dot(jnp.where(m, values, 0), grad, ((1,), (1,))) for m in mines]
        probs, scores_grads = [], []
        for sub in subs:
            number = group * (lanes // head) + sub
            prob = jnp.exp(
                jnp.where(allowed, scores[sub], big_negative) - lse_ref[number : number + 1, :]
            )
            weighted = jnp.sum(prob * probs_grads[sub], axis=0, keepdims=True)
            scores_grads.append((prob * (probs_grads[sub] - weighted)).astype(bf16))
            probs.append(prob.astype(bf16))
        values_grad = jnp.concatenate(
            [dot(p, grad)[:, sub * head : (sub + 1) * head] for sub, p in enumerate(probs)], axis=1
        )
        keys_grad = jnp.concatenate(
            [dot(x, query)[:, sub * head : (sub + 1) * head] for sub, x in enumerate(scores_grads)],
            axis=1,
        )
        query_grads = [
            dot(keys_turned[sub * head : (sub + 1) * head, :], scores_grads[sub]) for sub in subs
        ]
        query_grad = jnp.concatenate(query_grads, axis=0).T * head ** (-0.5)
        mixed_ref[:, at : at + lanes] = turned(query_grad, cosine, sine).astype(bf16)
        mixed_ref[:, part + at : part + at + lanes] = turned(keys_grad, cosine, sine).astype(bf16)
        mixed_ref[:, 2 * part + at : 2 * part + at + lanes] = values_grad.astype(bf16)


def attend_back(window, ends, qkv, grad, lse, tables, head, after=()):
    kernel = functools.partial(attend_back_kernel, head, window)
    return call(kernel, [ends, *tables, qkv, grad, lse], [shape16(*qkv.shape)], 6, after)


def acts_grad_kernel(count, heads_ref, up_ref, *refs):
    mixed, hidden = stacked(refs[:count]), stacked(refs[count : 2 * count])
    normed = refs[2 * count : 3 * count]
    halves, sums = refs[3 * count : 5 * count], refs[5 * count :]
    half, width = halves[0].shape
    for ref in sums:
        ref[...] = jnp.zeros_like(ref)
    step = min(256, width)
    for at in range(0, width, step):
        here = slice(at, at + step)
        terms = dot(mixed, heads_ref[here, :], ((1,), (1,)))
        terms += dot(hidden, up_ref[here, :], ((1,), (1,)))
        for w, ref in enumerate(sums):
            term = terms[2 * w * half : 2 * (w + 1) * half]
            ref[0:1, here] = jnp.sum(
                term * normed[w][:, here].astype(f32), axis=0, keepdims=True
            )
            ref[1:2, here] = jnp.sum(term, axis=0, keepdims=True)
        for i, ref in enumerate(halves):
            ref[:, here] = terms[i * half : (i + 1) * half].astype(bf16)


def acts_grad(heads, up, mixed, hidden, normed, after=()):
    count = len(mixed)
    length, width = normed[0].shape
    outs = [shape16(length // 2, width)] * (2 * count)
    outs += [jax.ShapeDtypeStruct((8, width), f32)] * count
    kernel = functools.partial(acts_grad_kernel, count)
    outs, done = call(kernel, [heads, up, *mixed, *hidden, *normed], outs, 10, after)
    return list(zip(outs[0 : 2 * count : 2], outs[1 : 2 * count : 2])), outs[2 * count :], done


def joined_windows(refs, scratch):
    at = 0
    for ref in refs:
        rows = ref.shape[0]
        scratch[at : at + rows, :] = ref[...]
        at += rows


def halved(shape):
    return [shape16(shape.shape[0] // 2, *shape.shape[1:])] * 2


def row_grads_kernel(rows, place_ref, *refs):
    activated, attended, grads = refs[:GROUP], refs[GROUP : 2 * GROUP], refs[2 * GROUP : -6]
    *theirs, mine_ref, a_ref, b_ref, g_ref = refs[-6:]
    joined_windows(activated, a_ref)
    joined_windows(attended, b_ref)
    joined_windows(grads, g_ref)
    first = place_ref[2] == 0
    grad = g_ref[...]
    at = 0
    for ref, size in ((a_ref, mine_ref.shape[1] - rows), (b_ref, rows)):
        step = min(256, ref.shape[1])
        for start in range(0, ref.shape[1], step):
            term = dot(ref[:, start : start + step], grad, ((0,), (0,))).astype(bf16)
            for pair in range(step // (CORES * size)):
                z = start // (CORES * size) + pair
                zero = term[pair * 2 * size : (pair * 2 + 1) * size]
                one = term[(pair * 2 + 1) * size : (pair * 2 + 2) * size]
                mine_ref[z, at : at + size, :] = jnp.where(first, zero, one)
                theirs[z // 2][z % 2, at : at + size, :] = jnp.where(first, one, zero)
        at += size


def row_grads(where, steps, rows, activated, attended, grads, after=()):
    length, hidden_part = activated[0].shape
    part = attended[0].shape[1]
    width = grads[0].shape[1]
    out = shape16(steps, hidden_part // (steps * CORES) + rows, width)
    scratch = [pltpu.VMEM((GROUP * length, w), bf16) for w in (hidden_part, part, width)]
    ins = [where, *activated, *attended, *grads]
    kernel = functools.partial(row_grads_kernel, rows)
    return call(kernel, ins, [*halved(out), out], 12, after, scratch)


def column_grads_kernel(rows, sums, place_ref, *refs):
    *theirs, mine_ref, a_ref, b_ref = refs[-5:]
    steps = mine_ref.shape[0]
    columns = b_ref.shape[1]
    joined_windows(refs[:GROUP], a_ref)
    joined_windows(refs[GROUP : 2 * GROUP], b_ref)
    first = place_ref[2] == 0
    grad = b_ref[...]
    step = steps * CORES * rows
    if sums:
        refs = refs[2 * GROUP :]
        acts_sums = sum((r[0:2, :] for r in refs[1:GROUP]), refs[0][0:2, :])
        joined_sums = sum((r[0:2, :] for r in refs[GROUP + 1 : 2 * GROUP]), refs[GROUP][0:2, :])
        row = lax.broadcasted_iota(jnp.int32, (rows, 128), 0)

        def tiles(t, z, c):
            number = (t * steps + z) * CORES + c
            at, up = number * rows // 128 * 128, (z * CORES + c) * 128
            value = jnp.zeros((rows, 128), f32)
            for k, line in enumerate(
                (
                    acts_sums[0:1, at : at + 128],
                    acts_sums[1:2, at : at + 128],
                    joined_sums[0:1, at : at + 128],
                    joined_sums[1:2, up : up + 128],
                )
            ):
                value = jnp.where(row == k, line, value)
            return value.astype(bf16)

    for t in range(GROUP):
        term = dot(a_ref[:, t * step : (t + 1) * step], grad, ((0,), (0,))).astype(bf16)
        here = slice(t * rows, (t + 1) * rows)
        for z in range(steps):
            zero = term[z * 2 * rows : (z * 2 + 1) * rows]
            one = term[(z * 2 + 1) * rows : (z * 2 + 2) * rows]
            mine_ref[z, here, :columns] = jnp.where(first, zero, one)
            theirs[z // 2][z % 2, here, :columns] = jnp.where(first, one, zero)
            if sums:
                zero, one = tiles(t, z, 0), tiles(t, z, 1)
                mine_ref[z, here, columns:] = jnp.where(first, zero, one)
                theirs[z // 2][z % 2, here, columns:] = jnp.where(first, one, zero)


def column_grads(where, steps, rows, acts, grads, after=(), sums=()):
    length, width = acts[0].shape
    columns = grads[0].shape[1]
    out = shape16(steps, GROUP * rows, columns + (128 if sums else 0))
    scratch = [pltpu.VMEM((GROUP * length, w), bf16) for w in (width, columns)]
    kernel = functools.partial(column_grads_kernel, rows, bool(sums))
    return call(kernel, [where, *acts, *grads, *sums], [*halved(out), out], 12, after, scratch)


def ring_begin_kernel(steps_on, place_ref, mine_ref, low_ref, high_ref, chip_ref, *firsts):
    steps = mine_ref.shape[0]
    for z in range(steps):
        got = (low_ref, high_ref)[z // 2][z % 2]
        chip_ref[z] = (mine_ref[z].astype(f32) + got.astype(f32)).astype(bf16)
    for on, ref in zip(steps_on, firsts):
        ref[...] = chip_ref[lax.rem(place_ref[1] + on, steps)]


def ring_add_kernel(on, place_ref, chip_ref, moving_ref, out_ref):
    at = lax.rem(place_ref[1] + on, chip_ref.shape[0])
    out_ref[...] = (chip_ref[at].astype(f32) + moving_ref[...].astype(f32)).astype(bf16)


def ring_rows_kernel(place_ref, chip_ref, *refs):
    down_ref, merge_ref = refs[-2:]
    total = chip_ref[place_ref[1]].astype(f32)
    for other in refs[:-2]:
        total += other[...].astype(f32)
    size = down_ref.shape[0]
    down_ref[...] = total[:size]
    merge_ref[...] = total[size:]


def ring_columns_kernel(count, place_ref, *refs):
    outs = refs[-GROUP:]
    rows = outs[0].shape[0]
    for mask in range(GROUP):
        t = jnp.bitwise_xor(place_ref[0], mask)
        at = pl.ds(pl.multiple_of(t * rows, rows), rows)
        column = 0
        for chip, *others in (refs[:count], refs[count:-GROUP]):
            total = chip[place_ref[1], at, :].astype(f32)
            for other in others:
                total += other[at, :].astype(f32)
            width = total.shape[1]
            outs[mask][:, column : column + width] = total.astype(bf16)
            column += width


def add_halves_kernel(*refs):
    one, two, low, high, one_ref, two_ref = refs[0:2], refs[2:4], *refs[4:]
    half = low.shape[0]
    one_ref[:half] = (one[0][...].astype(f32) + low[...].astype(f32)).astype(bf16)
    one_ref[half:] = one[1][...]
    two_ref[:half] = two[0][...]
    two_ref[half:] = (two[1][...].astype(f32) + high[...].astype(f32)).astype(bf16)


def add_halves(one, two, low, high, after=()):
    outs = [shape16(2 * low.shape[0], low.shape[1])] * 2
    return call(add_halves_kernel, [*one, *two, low, high], outs, 4, after)


def summed(own, one, two):
    return stacked(own).astype(f32) + one[...].astype(f32) + two[...].astype(f32)


def finish_out_kernel(tokens_ref, small_ref, low_ref, high_ref, one_ref, two_ref, out_ref):
    total = summed([low_ref, high_ref], one_ref, two_ref)
    out_ref[...] = (tokens_ref[...].astype(f32) + total + small_ref[2:3, :]).astype(bf16)


def finish_grad_kernel(
    tokens_ref, grad_ref, small_ref, low_ref, high_ref, one_ref, two_ref, out_ref
):
    normed, inverse_std = normalised(tokens_ref[...].astype(f32))
    normed_grad = summed([low_ref, high_ref], one_ref, two_ref) * small_ref[0:1, :]
    mean = jnp.mean(normed_grad, axis=-1, keepdims=True)
    along = jnp.mean(normed_grad * normed, axis=-1, keepdims=True)
    grad = grad_ref[...].astype(f32)
    out_ref[...] = (grad + inverse_std * (normed_grad - mean - normed * along)).astype(bf16)


def finish(kernel, arrays, own, one, two, after=()):
    (out,), done = call(kernel, [*arrays, *own, one, two], [shape16(*one.shape)], 10, after)
    return out, done


def prepare_kernel(
    place_ref, ends_ref, small_ref, heads_ref, up_ref, down_ref, merge_ref, *refs
):
    outs, sem = refs[: GROUP + 1], refs[-1]
    rows = heads_ref.shape[0]
    part = heads_ref.shape[1] // 3 // GROUP
    hidden_part = up_ref.shape[1] // GROUP
    hidden_rows = down_ref.shape[0]
    copies = []

    def copy(src, dst):
        copies.append(pltpu.make_async_copy(src, dst, sem.at[len(copies)]))

    for mask in range(GROUP):
        to = jnp.bitwise_xor(place_ref[0], mask)
        for k in range(3):
            at = pl.multiple_of((k * GROUP + to) * part, part)
            copy(heads_ref.at[:, pl.ds(at, part)], outs[mask].at[:, pl.ds(k * part, part)])
        at = pl.multiple_of(to * hidden_part, hidden_part)
        copy(
            up_ref.at[:, pl.ds(at, hidden_part)],
            outs[mask].at[:, pl.ds(3 * part + 128, hidden_part)],
        )
    copy(down_ref, outs[GROUP].at[pl.ds(0, hidden_rows)])
    copy(merge_ref, outs[GROUP].at[pl.ds(hidden_rows, rows)])
    for each in copies:
        each.start()
    quarter = place_ref[3]
    row = lax.broadcasted_iota(jnp.int32, (rows, 128), 0)
    lane = lax.broadcasted_iota(jnp.int32, (rows, 128), 1)
    first = jnp.broadcast_to(small_ref[0:1, :], (rows, 128))
    extra = jnp.zeros((rows, 128), f32)
    for k in range(3):
        moved = pltpu.roll(first, lax.rem(quarter * rows + (128 - k * rows), 128), 1)
        here = (row == k) & (lane >= quarter * rows) & (lane < (quarter + 1) * rows)
        extra = jnp.where(here, moved, extra)
    extra = jnp.where(row == 3, small_ref[1:2, :], extra)
    for k in range(2):
        value = ends_ref[k]
        for i, piece in enumerate((value // 16, value % 16)):
            extra = jnp.where((row == 4) & (lane == 2 * k + i), piece.astype(f32), extra)
    extra = extra.astype(bf16)
    for mask in range(GROUP):
        outs[mask][:, 3 * part : 3 * part + 128] = extra
    for each in copies:
        each.wait()


def prepare(where, ends, small, heads_weight, up_weight, down_weight, merge_weight):
    rows, width3 = heads_weight.shape
    columns = width3 // GROUP + up_weight.shape[1] // GROUP + 128
    block = (down_weight.shape[0] + merge_weight.shape[0], down_weight.shape[1])
    far = [heads_weight, up_weight, down_weight, merge_weight]
    far = [pltpu.with_memory_space_constraint(x, pltpu.HBM) for x in far]
    return pl.pallas_call(
        prepare_kernel,
        in_specs=[spec(pltpu.SMEM)] * 2 + [spec(pltpu.VMEM)] + [spec(pltpu.HBM)] * len(far),
        out_specs=[spec(pltpu.VMEM)] * (GROUP + 1),
        out_shape=[shape16(rows, columns)] * GROUP + [shape16(*block)],
        scratch_shapes=[pltpu.SemaphoreType.DMA((4 * GROUP + 2,))],
        **settings(2),
    )(where, ends, small, *far)


def small_rows_kernel(count, place_ref, extra_ref, small_ref):
    total = extra_ref.shape[0]
    rows = total // (count * GROUP)
    row = lax.broadcasted_iota(jnp.int32, (8, 128), 0)
    per = 128 // rows
    for tile in range(small_ref.shape[1] // 128):
        value = jnp.zeros((8, 128), f32)
        for i in range(per):
            at = (tile * per + i) * rows
            value += extra_ref[at : at + 16, :].astype(f32)[:8]
        if tile < count:
            at = pl.multiple_of((place_ref[0] * count + tile) * rows, rows)
            value = jnp.where(row == 3, extra_ref[pl.ds(at, 16), :].astype(f32)[:8], value)
        small_ref[:, tile * 128 : (tile + 1) * 128] = value


def assemble_kernel(layout, steps, with_small, sources, place_ref, *refs):
    count = steps * CORES
    extra_ref = refs[-1]
    outs = refs[-1 - len(layout) - with_small : -1]
    for number, (source, part) in enumerate(sources):
        piece = refs[source] if part is None else refs[source].at[part]
        z = place_ref[1] - number // CORES
        z = jnp.where(z < 0, z + steps, z)
        c = jnp.bitwise_xor(place_ref[2], number % CORES)
        row = 0
        for (rows, masks), out in zip(layout, outs):
            width = out.shape[1]
            for mask in range(masks):
                d = jnp.bitwise_xor(place_ref[0], mask) if masks > 1 else 0
                to = pl.ds(pl.multiple_of(((d * steps + z) * CORES + c) * rows, rows), rows)
                out[to, :] = piece[row : row + rows, :width]
                if with_small:
                    extra_ref[to, :] = piece[row : row + rows, width:]
                row += rows
    if with_small:
        small_rows_kernel(count, place_ref, extra_ref, outs[-1])


def assemble(place, where, arrays, sources, layout, with_small=False, after=()):
    width = arrays[0].shape[1] - (128 if with_small else 0)
    totals = [len(sources) * r * masks for r, masks in layout]
    outs = [shape16(total, width) for total in totals]
    if with_small:
        outs.append(jax.ShapeDtypeStruct((8, totals[0]), f32))
    kernel = functools.partial(assemble_kernel, layout, place.nz, with_small, sources)
    scratch = [pltpu.VMEM((totals[0], 128), bf16)]
    return call(kernel, [where, *arrays], outs, 2, after, scratch)


def stack_kernel(*refs):
    for i, ref in enumerate(refs[:-1]):
        refs[-1][i] = ref[...]


def stack(*arrays, after=()):
    (out,), done = call(stack_kernel, list(arrays), [shape16(len(arrays), *arrays[0].shape)], 2, after)
    return out, done


def halves_kernel(x_ref, low_ref, high_ref):
    half = low_ref.shape[0]
    low_ref[...] = x_ref[:half]
    high_ref[...] = x_ref[half:]


def halves(x, after=()):
    outs = [shape16(x.shape[0] // 2, x.shape[1])] * 2
    return call(halves_kernel, [x], outs, 3, after)


def cut_kernel(one_ref, two_ref, low_ref, high_ref):
    half = low_ref.shape[0]
    low_ref[...] = one_ref[:half]
    high_ref[...] = two_ref[half:]


def cut(one, two, after=()):
    outs = [shape16(one.shape[0] // 2, one.shape[1])] * 2
    return call(cut_kernel, [one, two], outs, 2, after)


def plain_assemble(place, pieces, layout):
    steps = place.nz
    flat = [piece for pair in pieces for piece in pair]
    width = flat[0].shape[1]
    stacked_pieces = jnp.stack(flat).reshape(steps, CORES, place.no, -1, width)
    stacked_pieces = jnp.take(stacked_pieces, (place.z - np.arange(steps)) % steps, axis=0)
    stacked_pieces = jnp.take(stacked_pieces, np.arange(CORES) ^ place.c, axis=1)
    outs, row = [], 0
    for r, masks in layout:
        part = stacked_pieces[:, :, :, row : row + r * masks]
        part = part.reshape(steps, CORES, place.no, masks, r, width)
        if masks > 1:
            part = jnp.take(part, np.arange(masks) ^ place.t, axis=3)
        outs.append(part.transpose(2, 3, 0, 1, 4, 5).reshape(-1, width))
        row += r * masks
    return outs


def columns_out_kernel(place_ref, *refs):
    blocks = refs[:GROUP]
    heads_out_ref, up_out_ref, small_ref = refs[GROUP:]
    rows = blocks[0].shape[0]
    hidden_part = up_out_ref.shape[1] // GROUP
    part = heads_out_ref.shape[1] // GROUP // 3
    total = jnp.zeros((16, 128), f32)
    for mask in range(GROUP):
        to = jnp.bitwise_xor(place_ref[0], mask)
        at = pl.multiple_of(to * hidden_part, hidden_part)
        up_out_ref[:, pl.ds(at, hidden_part)] = blocks[mask][:, :hidden_part].astype(f32)
        for k in range(3):
            at = pl.multiple_of((k * GROUP + to) * part, part)
            start = hidden_part + k * part
            heads_out_ref[:, pl.ds(at, part)] = blocks[mask][:, start : start + part].astype(f32)
        total += blocks[mask][:16, hidden_part + 3 * part :].astype(f32)
    own = blocks[0][:16, hidden_part + 3 * part :].astype(f32)
    row = lax.broadcasted_iota(jnp.int32, (16, 128), 0)
    value = jnp.where(row < 2, total, own)
    moved = pltpu.roll(value, lax.rem(128 - place_ref[3] * rows, 128), 1)
    small_ref[...] = jnp.where(row < 3, moved, value)[:8]


def columns_out(where, blocks, hidden_part):
    rows, columns = blocks[0].shape
    outs = [
        jax.ShapeDtypeStruct((rows, GROUP * (columns - 128 - hidden_part)), f32),
        jax.ShapeDtypeStruct((rows, GROUP * hidden_part), f32),
        jax.ShapeDtypeStruct((8, 128), f32),
    ]
    return call(columns_out_kernel, [where, *blocks], outs, 4)[0]


class Place:
    def __init__(self, sizes):
        self.ndp = sizes["dp"]
        self.no = self.ndp // GROUP
        self.nf = sizes["fsdp"]
        self.nz = self.nf // CORES
        fsdp = lax.axis_index("fsdp")
        self.dp = lax.axis_index("dp")
        self.t = self.dp % GROUP
        self.z = fsdp // CORES
        self.c = fsdp % CORES
        self.outer_groups = [[o * GROUP + t for o in range(self.no)] for t in range(GROUP)]

    def send(self, x, to):
        pairs = []
        for d in range(self.ndp):
            for z in range(self.nz):
                for c in range(CORES):
                    d2, z2, c2 = to(d, z, c)
                    pairs.append(
                        (d * self.nf + z * CORES + c, d2 * self.nf + z2 * CORES + c2)
                    )
        return lax.ppermute(x, AXES, pairs)

    def swap_t(self, x, mask):
        return self.send(x, lambda d, z, c: (d ^ mask, z, c))

    def shift_z(self, x, step=1):
        return self.send(x, lambda d, z, c: (d, (z + step) % self.nz, c))

    def swap_core(self, x):
        return self.send(x, lambda d, z, c: (d, z, CORES - 1 - c))


def later(x, *after):
    return lax.optimization_barrier((x,) + after)[0]


def add(a, b):
    return a.astype(f32) + b.astype(f32)


class RingSum:
    def __init__(self, place, where, theirs, mine, *after):
        self.place, self.where, self.mine = place, where, mine
        self.got = [place.swap_core(later(x, *after)) for x in theirs]

    def run(self, kernel, arrays, outs, after):
        return call(kernel, [self.where, *arrays], outs, 6, after)

    def first(self, steps_on, after):
        block = shape16(*self.mine.shape[1:])
        outs = [shape16(*self.mine.shape)] + [block] * len(steps_on)
        kernel = functools.partial(ring_begin_kernel, steps_on)
        (self.chip, *firsts), done = self.run(kernel, [self.mine, *self.got], outs, after)
        return firsts, done

    def added(self, on, after):
        outs = [shape16(*self.moving.shape)]
        kernel = functools.partial(ring_add_kernel, on)
        (out,), done = self.run(kernel, [self.chip, self.moving], outs, after)
        return out, done

    def begin(self, *after):
        (first,), done = self.first((3,), after)
        self.moving, self.on = self.place.shift_z(first), 3
        return done

    def pass_on(self, out):
        self.moving = self.place.shift_z(out)

    def next(self, *after):
        self.on -= 1
        return self.added(self.on, after)

    def step(self, *after):
        out, done = self.next(*after)
        self.pass_on(out)
        return done

    def terms(self):
        return [self.chip, self.moving]


class PairSum(RingSum):
    def begin(self, *after):
        (far, back), done = self.first((2, 3), after)
        self.moving, self.back = self.place.shift_z(far), self.place.shift_z(back, -1)
        return done

    def step(self, *after):
        out, done = self.added(1, after)
        self.moving = self.place.shift_z(out)
        return done

    def terms(self):
        return [self.chip, self.back, self.moving]


def plain_sum(place, terms):
    terms = lax.psum_scatter(terms, "dp", scatter_dimension=0, axis_index_groups=place.outer_groups)
    theirs = lax.dynamic_index_in_dim(terms, 1 - place.c, 1, keepdims=False)
    chip = lax.dynamic_index_in_dim(terms, place.c, 1, keepdims=False)
    chip = add(chip, place.swap_core(theirs)).astype(bf16)
    moving = None
    for step in range(1, place.nz + 1):
        own = lax.dynamic_index_in_dim(chip, (place.z - step) % place.nz, 0, keepdims=False)
        moving = own if moving is None else add(place.shift_z(moving), own).astype(bf16)
    return moving.astype(f32)


def plain_gather(place, block):
    block = lax.all_gather(block, "dp", axis_index_groups=place.outer_groups, tiled=True)
    blocks = [block]
    for _ in range(place.nz - 1):
        blocks.append(place.shift_z(blocks[-1]))
    return [(b, place.swap_core(b)) for b in blocks]


def gather_windows(place, own):
    half = own.shape[0] // 2
    one, two = place.swap_t(own, 1), place.swap_t(own, 2)
    three = [place.swap_t(one[:half], 2), place.swap_t(two[half:], 1)]
    return [[own], [one], [two], three]


def sum_windows(place, terms):
    low, high = place.swap_t(terms[3][0], 2), place.swap_t(terms[3][1], 1)
    (one, two), _ = add_halves(terms[1], terms[2], low, high)
    return terms[0], place.swap_t(one, 1), place.swap_t(two, 2)


def columns(place, heads_weight, up_weight, mask):
    rows, width3 = heads_weight.shape
    part = width3 // 3 // GROUP
    hidden_part = up_weight.shape[1] // GROUP
    to = place.t ^ mask
    joint = [
        lax.dynamic_slice_in_dim(heads_weight, (k * GROUP + to) * part, part, axis=1)
        for k in range(3)
    ]
    up = lax.dynamic_slice_in_dim(up_weight, to * hidden_part, hidden_part, axis=1)
    return jnp.concatenate(joint + [up], axis=1)


def spread(vector, at, count):
    n = vector.shape[0]
    row = jnp.tile(vector.astype(f32).reshape(1, n), (1, count))
    lane = lax.broadcasted_iota(jnp.int32, row.shape, 1)
    return jnp.where(lane // n == at, row, 0.0)


def small_gather(place, norm_gain, norm_bias, down_bias, up_bias, offsets, terminal):
    here = ((place.dp * place.nz) + place.z) * CORES + place.c
    count = place.ndp * place.nf
    rows = jnp.concatenate([spread(v, here, count) for v in (norm_gain, norm_bias, down_bias)])
    fsdp = (place.dp // GROUP * place.nz + place.z) * CORES + place.c
    own = spread(up_bias, fsdp, place.no * place.nf)
    lanes = rows.shape[1]
    both = jnp.concatenate([rows, jnp.pad(own, ((0, 0), (0, lanes - own.shape[1])))])
    if place.no > 1:
        both = lax.psum(both, "dp", axis_index_groups=place.outer_groups)
    shifted = [place.shift_z(both, s) for s in range(1, place.nz)]
    both = sum(shifted, both)
    both = both + place.swap_core(both)
    ends = jnp.concatenate([offsets, terminal]).astype(f32).reshape(1, -1)
    ends = jnp.pad(ends, ((0, 0), (0, lanes - ends.shape[1])))
    group = jnp.concatenate([both[:3], ends])
    others = [place.swap_t(group, m) for m in range(1, GROUP)]
    rows = sum((o[:3] for o in others), group[:3])
    windows = offsets.shape[0]
    ends = jnp.concatenate([g[3:4, : 2 * windows] for g in [group] + others])
    return rows, both[3:4, : own.shape[1]], ends


def plain_shards(
    place,
    tokens,
    heads_weight,
    merge_weight,
    up_weight,
    up_bias,
    down_weight,
    down_bias,
    norm_gain,
    norm_bias,
    offsets,
    terminal,
    cotangent,
):
    nz, no = place.nz, place.no
    length, width = tokens.shape
    head = width // HEADS
    rows = heads_weight.shape[0]
    hidden_rows = down_weight.shape[0]
    part = width // GROUP
    hidden_part = up_weight.shape[1] // GROUP
    number = place.dp * place.nf + place.z * CORES + place.c
    tables = turn_tables(length, head, 128)
    pieces = [columns(place, heads_weight, up_weight, m) for m in range(GROUP)]
    pieces = jnp.concatenate([pieces[0]] + [place.swap_t(pieces[m], m) for m in range(1, GROUP)])
    layout = [(rows, GROUP)]
    (heads,) = plain_assemble(place, plain_gather(place, pieces[:, : 3 * part]), layout)
    (up,) = plain_assemble(place, plain_gather(place, pieces[:, 3 * part :]), layout)
    block = jnp.concatenate([down_weight, merge_weight])
    layout = [(hidden_rows, 1), (rows, 1)]
    down, merge = plain_assemble(place, plain_gather(place, block), layout)
    small, up_shift, ends = small_gather(
        place, norm_gain, norm_bias, down_bias, up_bias, offsets, terminal
    )
    up_shift = jnp.pad(up_shift, ((0, 4), (0, width - hidden_part)))
    small = jnp.concatenate([small, up_shift])
    ends = jnp.stack([jnp.floor(ends / 16.0), ends % 16.0], axis=-1).reshape(GROUP, 1, 4)
    ends = jnp.pad(ends, ((0, 0), (4, 11), (0, 124))).reshape(16 * GROUP, 128)
    windows = gather_windows(place, tokens)
    grads = gather_windows(place, cotangent)

    saved = [attend(w, ends, windows[w], heads, small, tables, head)[0] for w in range(GROUP)]
    acts, normed, attended, qkv, lse = zip(*saved)
    activated, slope = zip(*(hidden_units([a], up, small)[0][0] for a in acts))
    outs = [out_terms([activated[w]], [attended[w]], down, merge)[0][0] for w in range(GROUP)]
    block_output, _ = finish(finish_out_kernel, [tokens, small], *sum_windows(place, outs))
    (hidden_grad, attended_grad, joined_sums), _ = joined_grad(grads, down, merge, slope)
    mixed_grad, terms, acts_sums = [], [], []
    for w in range(GROUP):
        mixed = attend_back(w, ends, qkv[w], attended_grad[w], lse[w], tables, head)[0][0]
        halves, sums, _ = acts_grad(heads, up, [mixed], [hidden_grad[w]], [normed[w]])
        mixed_grad.append(mixed)
        terms += halves
        acts_sums += sums
    grad_tokens, _ = finish(
        finish_grad_kernel, [tokens, cotangent, small], *sum_windows(place, terms)
    )

    def product(left, right):
        left, right = jnp.concatenate(left), jnp.concatenate(right)
        return dot(left, right, ((0,), (0,))).astype(bf16)

    def by_place(terms):
        terms = terms.reshape(no, GROUP, nz, CORES, rows, terms.shape[1])
        return terms.transpose(0, 2, 3, 1, 4, 5)

    def by_t(summed):
        blocks = [
            lax.dynamic_index_in_dim(summed, place.t ^ m, 0, keepdims=False) for m in range(GROUP)
        ]
        arrived = [blocks[0]] + [place.swap_t(blocks[m].astype(bf16), m) for m in range(1, GROUP)]
        arrived = [a.astype(f32) for a in arrived]
        return [lax.select_n(t ^ place.t, *arrived) for t in range(GROUP)]

    flat = [h for pair in grads for h in pair]
    down_terms = product(activated, flat).reshape(no, nz, CORES, hidden_rows, width)
    merge_terms = product(attended, flat).reshape(no, nz, CORES, rows, width)
    row_total = plain_sum(place, jnp.concatenate([down_terms, merge_terms], axis=3))
    heads_by_t = by_t(plain_sum(place, by_place(product(acts, mixed_grad))))
    up_by_t = by_t(plain_sum(place, by_place(product(acts, hidden_grad))))
    grad_heads = jnp.concatenate(
        [h[:, k * part : (k + 1) * part] for k in range(3) for h in heads_by_t], axis=1
    )
    group_sums = jnp.concatenate([sum(acts_sums)[:2], sum(joined_sums)[:2, :width]])
    group_sums = group_sums + place.swap_core(group_sums)
    group_sums = lax.psum(group_sums, "dp", axis_index_groups=place.outer_groups)
    group_sums = sum((place.shift_z(group_sums, s) for s in range(1, nz)), group_sums)
    all_sums = sum((place.swap_t(group_sums, m) for m in range(1, GROUP)), group_sums)
    grad_gain, grad_bias = (
        lax.dynamic_slice_in_dim(all_sums[k], number * rows, rows) for k in range(2)
    )
    at = (place.dp // GROUP * place.nf + place.z * CORES + place.c) * hidden_rows
    return (
        block_output,
        grad_tokens,
        grad_heads,
        row_total[hidden_rows:],
        jnp.concatenate(up_by_t, axis=1),
        lax.dynamic_slice_in_dim(group_sums[3], at, hidden_rows),
        row_total[:hidden_rows],
        lax.dynamic_slice_in_dim(group_sums[2], number * rows, rows),
        grad_gain,
        grad_bias,
    )


def paced_shards(
    place,
    tokens,
    heads_weight,
    merge_weight,
    up_weight,
    up_bias,
    down_weight,
    down_bias,
    norm_gain,
    norm_bias,
    offsets,
    terminal,
    cotangent,
):
    nz = place.nz
    length, width = tokens.shape
    head = width // HEADS
    rows = heads_weight.shape[0]
    hidden_rows = down_weight.shape[0]
    part = width // GROUP
    hidden_part = up_weight.shape[1] // GROUP
    number = place.dp * place.nf + place.z * CORES + place.c
    where = jnp.stack([place.t, place.z, place.c, number % (128 // rows)]).astype(jnp.int32)
    tables = turn_tables(length, head, 128)
    send, shift, swap = place.swap_t, place.shift_z, place.swap_core

    vectors, at = 0.0, 0
    for v in (norm_gain, norm_bias, down_bias, up_bias):
        v = v.astype(f32)
        at = at if v.shape[0] < 128 else 128
        vectors += jnp.pad(v, (at, 256 - at - v.shape[0]))
        at += v.shape[0]
    *pieces, row_block = prepare(
        where,
        jnp.concatenate([offsets, terminal]),
        vectors.reshape(2, 128),
        heads_weight,
        up_weight,
        down_weight,
        merge_weight,
    )
    joint = 3 * part + 128
    arrived = [send(pieces[m], m) for m in range(1, GROUP)]
    pieces = [pieces[0]] + arrived
    joint_block = jnp.concatenate([p[:, :joint] for p in pieces])
    up_block = jnp.concatenate([p[:, joint:] for p in pieces])

    joint_blocks, up_blocks, row_blocks = [joint_block], [up_block], [row_block]
    joint_blocks.append(shift(joint_block))
    tokens_one = send(later(tokens, *arrived), 1)
    tokens_two = send(later(tokens, *arrived), 2)
    joint_blocks.append(shift(joint_blocks[1]))
    early, _ = stack(*joint_blocks[:2])
    early = swap(early)
    up_blocks.append(shift(later(up_block, joint_blocks[1])))
    joint_blocks.append(shift(joint_blocks[2]))
    (three_low, three_high), cut_done = cut(tokens_one, tokens_two, [joint_blocks[2]])
    up_blocks.append(shift(later(up_blocks[1], joint_blocks[3])))
    third, fourth = swap(joint_blocks[2]), swap(later(joint_blocks[3], cut_done))
    three_low, three_high = send(three_low, 2), send(three_high, 1)
    sources = [(0, None), (4, 0), (1, None), (4, 1), (2, None), (5, 0), (3, None), (5, 1)]
    split = [*sources[:5], (5, None), (3, None), (6, None)]
    layout = [(rows, GROUP)]
    (heads, small), done = assemble(
        place, where, [*joint_blocks, early, third, fourth], split, layout, True, [cut_done]
    )

    def attended_window(window, parts, *after):
        return attend(window, joint_block, parts, heads, small, tables, head, after)

    saved, units = [None] * GROUP, [None] * GROUP
    row_blocks.append(shift(later(row_block, joint_blocks[3])))
    grad_one, grad_two = send(later(cotangent, done), 1), send(later(cotangent, done), 2)
    saved[0], done = attended_window(0, [tokens], done, three_low, three_high)
    saved[1], done = attended_window(1, [tokens_one], done)
    up_blocks.append(shift(later(up_blocks[2], done)))
    saved[2], done = attended_window(2, [tokens_two], done)
    saved[3], done = attended_window(3, [three_low, three_high], done)
    early, done = stack(*up_blocks[:2], after=[done, row_blocks[1]])
    late, done = stack(*up_blocks[2:], after=[done])
    early, late = swap(early), swap(late)
    row_blocks.append(shift(later(row_blocks[1], done)))
    (up,), done = assemble(
        place, where, [*up_blocks, early, late], sources, layout, after=[done]
    )
    units[0:1], done = hidden_units([saved[0][0]], up, small, [done])
    (grad_low, grad_high), done = cut(grad_one, grad_two, [done])
    grad_low, grad_high = send(grad_low, 2), send(grad_high, 1)
    units[1:3], done = hidden_units([saved[1][0], saved[2][0]], up, small, [done])
    row_blocks.append(shift(later(row_blocks[2], done)))
    units[3:4], done = hidden_units([saved[3][0]], up, small, [done])
    acts, normed, attended, qkv, lse = zip(*saved)
    activated, slope = zip(*units)
    grads = [[cotangent], [grad_one], [grad_two], [grad_low, grad_high]]

    flat = [h for parts in grads for h in parts]
    early, done = stack(*row_blocks[:2], after=[done])
    early = swap(early)
    (*theirs, mine), done = row_grads(where, nz, rows, activated, attended, flat, [done])
    late, done = stack(*row_blocks[2:], after=[done])
    late = swap(late)
    row_sum = RingSum(place, where, theirs, mine, done)
    (down, merge), done = assemble(
        place,
        where,
        [*row_blocks, early, late],
        sources,
        [(hidden_rows, 1), (rows, 1)],
        after=[done],
    )

    def out_of(windows, *after):
        picked = [activated[w] for w in windows], [attended[w] for w in windows]
        return out_terms(*picked, down, merge, after)

    outs = [None] * GROUP
    outs[3:4], done = out_of([3], done)
    out_low, out_high = send(outs[3][0], 2), send(outs[3][1], 1)
    done = row_sum.begin(done)
    outs[1:3], done = out_of([1, 2], done)
    (hidden_grad, attended_grad, joined_sums), done = joined_grad(grads, down, merge, slope, [done])

    mixed_grad, terms, acts_sums = [None] * GROUP, [None] * GROUP, [None] * GROUP

    def acts_of(windows, *after):
        picked = [[x[w] for w in windows] for x in (mixed_grad, hidden_grad, normed)]
        return acts_grad(heads, up, *picked, after)

    (*theirs, mine), done = column_grads(where, nz, rows, acts, hidden_grad, [done])
    after = [done, row_sum.moving]
    (out_one, out_two), done = add_halves(outs[1], outs[2], out_low, out_high, after)
    out_one, out_two = send(out_one, 1), send(out_two, 2)
    up_sum = RingSum(place, where, theirs, mine, done)
    done = up_sum.begin(done)

    def back(w, *after):
        (mixed_grad[w],), done = attend_back(
            w, joint_block, qkv[w], attended_grad[w], lse[w], tables, head, after
        )
        return done

    done = back(3, done)
    done = row_sum.step(done)
    done = back(1, done)
    done = back(2, done)
    done = up_sum.step(done)
    terms[3:4], acts_sums[3:4], done = acts_of([3], done)
    low, high = send(terms[3][0], 2), send(terms[3][1], 1)
    done = back(0, done)
    terms[0:3], acts_sums[0:3], done = acts_of([0, 1, 2], done, out_one, out_two)
    done = up_sum.step(done)
    sums = [*acts_sums, *joined_sums]
    (*theirs, mine), done = column_grads(where, nz, rows, acts, mixed_grad, [done], sums)
    heads_sum = PairSum(place, where, theirs, mine, done)
    last_rows, done = row_sum.next(done)
    after = [done, up_sum.moving]
    (one, two), done = add_halves(terms[1], terms[2], low, high, after)
    one, two = send(one, 1), send(two, 2)
    done = heads_sum.begin(done)
    outs[0:1], done = out_of([0], done)
    block_output, done = finish(
        finish_out_kernel, [tokens, small], outs[0], out_one, out_two, [done]
    )
    done = heads_sum.step(done)
    row_sum.pass_on(later(last_rows, heads_sum.back))
    columns = hidden_part + 3 * part + 128
    blocks, done = call(
        functools.partial(ring_columns_kernel, len(up_sum.terms())),
        [where, *up_sum.terms(), *heads_sum.terms()],
        [shape16(rows, columns)] * GROUP,
        4,
        [done, heads_sum.back, one, two],
    )
    blocks = [blocks[0]] + [send(blocks[m], m) for m in range(1, GROUP)]
    grad_tokens, done = finish(
        finish_grad_kernel, [tokens, cotangent, small], terms[0], one, two, [done]
    )
    both = [jax.ShapeDtypeStruct((n, width), f32) for n in (hidden_rows, rows)]
    (grad_down, grad_merge), done = call(
        ring_rows_kernel, [where, *row_sum.terms()], both, 4, [done]
    )
    grad_heads, grad_up, narrow = columns_out(where, blocks, hidden_part)
    grad_gain, grad_bias, grad_down_bias = (narrow[k, :rows] for k in range(3))
    return (
        block_output,
        grad_tokens,
        grad_heads,
        grad_merge,
        grad_up,
        narrow[3, :hidden_rows],
        grad_down,
        grad_down_bias,
        grad_gain,
        grad_bias,
    )


def shards(sizes, tokens, *arrays):
    *weights, cotangent = arrays
    place = Place(sizes)
    rows, hidden_rows, part = weights[0].shape[0], weights[4].shape[0], tokens.shape[2] // GROUP
    paced = (
        (place.no, place.nz) == (1, 4)
        and rows % 16 == 0
        and 128 % rows == 0
        and hidden_rows == 128
        and part % 128 == 0
    )
    run = paced_shards if paced else plain_shards
    block_output, grad_tokens, *grads = run(place, tokens[0], *weights, cotangent[0])
    return (block_output[None], grad_tokens[None], *grads)


def solution(mesh):
    whole = P(AXES)
    return jax.shard_map(
        functools.partial(shards, dict(mesh.shape)),
        mesh=mesh,
        in_specs=(whole,) * 12,
        out_specs=(whole,) * 10,
        check_vma=False,
    )
```

```python
import functools

import jax
import jax.numpy as jnp
import numpy as np
from jax import lax
from jax.experimental import pallas as pl
from jax.experimental.pallas import tpu as pltpu
from jax.sharding import PartitionSpec as P

HEADS = 16
ROT = 32
CORES = 2
GROUP = 4
AXES = ("dp", "fsdp")

eps = 1e-05
big_negative = -1e30
gelu_scale = 0.7978845608028654
gelu_cubic = 0.044715

bf16 = jnp.bfloat16
f32 = jnp.float32


def turn_tables(length, head, lanes):
    position = np.arange(length, dtype=np.float32)
    exponent = np.arange(0, ROT, 2, dtype=np.float32) / np.float32(ROT)
    rate = (np.float32(1.0) / np.power(np.float32(10000.0), exponent)).astype(np.float32)
    phase = (position[:, None] * rate[None, :]).astype(np.float32)
    cosine = np.ones((length, head), np.float32)
    sine = np.zeros((length, head), np.float32)
    cosine[:, :ROT] = np.repeat(np.cos(phase), 2, axis=1)
    sine[:, :ROT] = np.repeat(np.sin(phase), 2, axis=1)
    sine[:, 0:ROT:2] *= -1.0
    copies = lanes // head
    return np.tile(cosine, (1, copies)), np.tile(sine, (1, copies))


def turned(values, cosine, sine):
    lanes = values.shape[1]
    even = lax.broadcasted_iota(jnp.int32, values.shape, 1) % 2 == 0
    other = jnp.where(even, pltpu.roll(values, lanes - 1, 1), pltpu.roll(values, 1, 1))
    return values * cosine + other * sine


def dot(a, b, dims=((1,), (0,))):
    return lax.dot_general(a, b, (dims, ((), ())), preferred_element_type=f32)


def allowed_pairs(ends, length):
    offset = (16.0 * ends[:, 0:1] + ends[:, 1:2]).astype(jnp.int32)
    end = (16.0 * ends[:, 2:3] + ends[:, 3:4]).astype(jnp.int32)
    key = lax.broadcasted_iota(jnp.int32, (length, 1), 0)
    query = lax.broadcasted_iota(jnp.int32, (1, length), 1)
    key_part = (key >= offset).astype(jnp.int32) + (key > end).astype(jnp.int32)
    query_part = (query >= offset).astype(jnp.int32) + (query > end).astype(jnp.int32)
    return (key_part == query_part) & (query >= key)


def spec(space):
    return pl.BlockSpec(memory_space=space)


def settings(mebibytes):
    return {
        "compiler_params": pltpu.CompilerParams(vmem_limit_bytes=mebibytes * 2**20),
        "cost_estimate": pl.CostEstimate(flops=1, bytes_accessed=1, transcendentals=0),
    }


TICK = jax.ShapeDtypeStruct((8, 128), jnp.float32)


def tick(ref):
    ref[...] = jnp.zeros_like(ref)


def call(kernel, ins, outs, mebibytes, after=(), scratch=()):
    many = len(ins)

    def body(*refs):
        rest = refs[many + len(after) :]
        tick(rest[len(outs)])
        kernel(*refs[:many], *rest[: len(outs)], *rest[len(outs) + 1 :])

    result = pl.pallas_call(
        body,
        in_specs=[spec(pltpu.SMEM if x.dtype == jnp.int32 else pltpu.VMEM) for x in ins]
        + [spec(pl.ANY)] * len(after),
        out_specs=[spec(pltpu.VMEM)] * (len(outs) + 1),
        out_shape=[*outs, TICK],
        scratch_shapes=list(scratch),
        **settings(mebibytes),
    )(*ins, *after)
    return result[:-1], result[-1]


def shape16(*dims):
    return jax.ShapeDtypeStruct(dims, bf16)


def stacked(refs):
    return jnp.concatenate([r[...] for r in refs])


def normalised(values):
    mean = jnp.mean(values, axis=-1, keepdims=True)
    centered = values - mean
    inverse_std = lax.rsqrt(jnp.mean(centered * centered, axis=-1, keepdims=True) + eps)
    return centered * inverse_std, inverse_std


def gelu_and_slope(h):
    square = h * h
    tanh_value = jnp.tanh(h * (gelu_scale + gelu_scale * gelu_cubic * square))
    half = 0.5 + 0.5 * tanh_value
    value = h * half
    factor = 2.0 * gelu_scale + 6.0 * gelu_scale * gelu_cubic * square
    return value, half + (value - value * half) * factor


def ends_of(window, ends_ref):
    rows, width = ends_ref.shape
    at = rows // GROUP * window
    return ends_ref[at : at + 16, width - 128 :].astype(f32)[4:5]


def attend_kernel(head, window, ends_ref, heads_ref, small_ref, cos_ref, sin_ref, *refs):
    tokens = refs[:-5]
    acts_ref, normed_ref, attended_ref, qkv_ref, lse_ref = refs[-5:]
    length, part = attended_ref.shape
    lanes = cos_ref.shape[1]
    normed, _ = normalised(stacked(tokens).astype(f32))
    normed_ref[...] = normed.astype(bf16)
    acts_ref[...] = (normed * small_ref[0:1, :] + small_ref[1:2, :]).astype(bf16)
    acts = acts_ref[...]
    query_all, keys_all, values_all = (
        dot(acts, heads_ref[:, k * part : (k + 1) * part]) for k in range(3)
    )
    allowed = allowed_pairs(ends_of(window, ends_ref), length)
    cosine, sine = cos_ref[...], sin_ref[...]
    lane = lax.broadcasted_iota(jnp.int32, (1, lanes), 1)
    heads_of = [(at, sub) for at in range(0, part, lanes) for sub in range(lanes // head)]
    queries, scores, values_turned = {}, [], {}
    for at in range(0, part, lanes):
        query = (turned(query_all[:, at : at + lanes], cosine, sine) * head ** (-0.5)).astype(bf16)
        keys = turned(keys_all[:, at : at + lanes], cosine, sine).astype(bf16)
        values = values_all[:, at : at + lanes]
        qkv_ref[:, at : at + lanes] = query
        qkv_ref[:, part + at : part + at + lanes] = keys
        qkv_ref[:, 2 * part + at : 2 * part + at + lanes] = values.astype(bf16)
        values_turned[at] = values.T.astype(bf16)
        for sub in range(lanes // head):
            mine = (lane >= sub * head) & (lane < (sub + 1) * head)
            scores.append(dot(jnp.where(mine, keys, 0), query, ((1,), (1,))))
    probs = []
    for number, score in enumerate(scores):
        score = jnp.where(allowed, score, big_negative)
        top = jnp.max(score, axis=0, keepdims=True)
        expo = jnp.exp(score - top)
        total = jnp.sum(expo, axis=0, keepdims=True)
        probs.append((expo * (1.0 / total)).astype(bf16))
        lse_ref[number : number + 1, :] = top + jnp.log(total)
    outs = [
        dot(values_turned[at][sub * head : (sub + 1) * head, :], prob)
        for (at, sub), prob in zip(heads_of, probs)
    ]
    attended_ref[...] = jnp.concatenate(outs, axis=0).T.astype(bf16)


def attend(window, ends, tokens, heads, small, tables, head, after=()):
    length, width = sum(t.shape[0] for t in tokens), tokens[0].shape[1]
    part = heads.shape[1] // 3
    outs = [shape16(length, w) for w in (width, width, part, 3 * part)]
    outs.append(jax.ShapeDtypeStruct((max(8, part // head), length), f32))
    kernel = functools.partial(attend_kernel, head, window)
    return call(kernel, [ends, heads, small, *tables, *tokens], outs, 6, after)


def hidden_kernel(up_ref, small_ref, *refs):
    count = len(refs) // 3
    acts = stacked(refs[:count])
    length, hidden_part = refs[count].shape
    step = min(256, hidden_part)
    for at in range(0, hidden_part, step):
        here = slice(at, at + step)
        hidden = dot(acts, up_ref[:, here])
        value, slope = gelu_and_slope(hidden + small_ref[3:4, here])
        for w in range(count):
            rows = slice(w * length, (w + 1) * length)
            refs[count + w][:, here] = value[rows].astype(bf16)
            refs[2 * count + w][:, here] = slope[rows].astype(bf16)


def hidden_units(acts, up, small, after=()):
    outs = [shape16(acts[0].shape[0], up.shape[1])] * (2 * len(acts))
    outs, done = call(hidden_kernel, [up, small, *acts], outs, 8, after)
    return list(zip(outs[: len(acts)], outs[len(acts) :])), done


def out_kernel(down_ref, merge_ref, *refs):
    count = len(refs) // 4
    activated, attended = stacked(refs[:count]), stacked(refs[count : 2 * count])
    halves = refs[2 * count :]
    half, width = halves[0].shape
    step = min(256, width)
    for at in range(0, width, step):
        here = slice(at, at + step)
        term = dot(activated, down_ref[:, here])
        term = (term + dot(attended, merge_ref[:, here])).astype(bf16)
        for i, ref in enumerate(halves):
            ref[:, here] = term[i * half : (i + 1) * half]


def out_terms(activated, attended, down, merge, after=()):
    outs = [shape16(activated[0].shape[0] // 2, down.shape[1])] * (2 * len(activated))
    outs, done = call(out_kernel, [down, merge, *activated, *attended], outs, 8, after)
    return list(zip(outs[::2], outs[1::2])), done


def joined_grad_kernel(count, down_ref, merge_ref, *refs):
    slopes, grads, outs = refs[:count], refs[count : -3 * count], refs[-3 * count :]
    hiddens, attendeds, sums = outs[:count], outs[count : 2 * count], outs[2 * count :]
    length, hidden_part = hiddens[0].shape
    grad = stacked(grads)
    windows = [slice(w * length, (w + 1) * length) for w in range(count)]
    for ref, rows in zip(sums, windows):
        ref[...] = jnp.zeros_like(ref)
        ref[0:1, :] = jnp.sum(grad[rows].astype(f32), axis=0, keepdims=True)
    step = min(256, hidden_part)
    for at in range(0, hidden_part, step):
        here = slice(at, at + step)
        terms = dot(grad, down_ref[here, :], ((1,), (1,)))
        for w, rows in enumerate(windows):
            term = (terms[rows] * slopes[w][:, here].astype(f32)).astype(bf16)
            hiddens[w][:, here] = term
            sums[w][1:2, here] = jnp.sum(term.astype(f32), axis=0, keepdims=True)
    terms = dot(grad, merge_ref[...], ((1,), (1,))).astype(bf16)
    for ref, rows in zip(attendeds, windows):
        ref[...] = terms[rows]


def joined_grad(grads, down, merge, slopes, after=()):
    count = len(slopes)
    length, hidden_part = slopes[0].shape
    outs = [shape16(length, hidden_part)] * count + [shape16(length, merge.shape[0])] * count
    outs += [jax.ShapeDtypeStruct((8, max(down.shape)), f32)] * count
    flat = [part for parts in grads for part in parts]
    kernel = functools.partial(joined_grad_kernel, count)
    outs, done = call(kernel, [down, merge, *slopes, *flat], outs, 16, after)
    return [outs[k * count : (k + 1) * count] for k in range(3)], done


def attend_back_kernel(
    head, window, ends_ref, cos_ref, sin_ref, qkv_ref, grad_ref, lse_ref, mixed_ref
):
    length = qkv_ref.shape[0]
    part = qkv_ref.shape[1] // 3
    lanes = cos_ref.shape[1]
    allowed = allowed_pairs(ends_of(window, ends_ref), length)
    cosine, sine = cos_ref[...], -sin_ref[...]
    lane = lax.broadcasted_iota(jnp.int32, (1, lanes), 1)
    for group in range(part // lanes):
        at = group * lanes
        query = qkv_ref[:, at : at + lanes]
        keys = qkv_ref[:, part + at : part + at + lanes]
        values = qkv_ref[:, 2 * part + at : 2 * part + at + lanes]
        grad = grad_ref[:, at : at + lanes]
        keys_turned = keys.astype(f32).T.astype(bf16)
        subs = range(lanes // head)
        mines = [(lane >= sub * head) & (lane < (sub + 1) * head) for sub in subs]
        scores = [dot(jnp.where(m, keys, 0), query, ((1,), (1,))) for m in mines]
        probs_grads = [dot(jnp.where(m, values, 0), grad, ((1,), (1,))) for m in mines]
        probs, scores_grads = [], []
        for sub in subs:
            number = group * (lanes // head) + sub
            prob = jnp.exp(
                jnp.where(allowed, scores[sub], big_negative) - lse_ref[number : number + 1, :]
            )
            weighted = jnp.sum(prob * probs_grads[sub], axis=0, keepdims=True)
            scores_grads.append((prob * (probs_grads[sub] - weighted)).astype(bf16))
            probs.append(prob.astype(bf16))
        values_grad = jnp.concatenate(
            [dot(p, grad)[:, sub * head : (sub + 1) * head] for sub, p in enumerate(probs)], axis=1
        )
        keys_grad = jnp.concatenate(
            [dot(x, query)[:, sub * head : (sub + 1) * head] for sub, x in enumerate(scores_grads)],
            axis=1,
        )
        query_grads = [
            dot(keys_turned[sub * head : (sub + 1) * head, :], scores_grads[sub]) for sub in subs
        ]
        query_grad = jnp.concatenate(query_grads, axis=0).T * head ** (-0.5)
        mixed_ref[:, at : at + lanes] = turned(query_grad, cosine, sine).astype(bf16)
        mixed_ref[:, part + at : part + at + lanes] = turned(keys_grad, cosine, sine).astype(bf16)
        mixed_ref[:, 2 * part + at : 2 * part + at + lanes] = values_grad.astype(bf16)


def attend_back(window, ends, qkv, grad, lse, tables, head, after=()):
    kernel = functools.partial(attend_back_kernel, head, window)
    return call(kernel, [ends, *tables, qkv, grad, lse], [shape16(*qkv.shape)], 6, after)


def acts_grad_kernel(count, heads_ref, up_ref, *refs):
    mixed, hidden = stacked(refs[:count]), stacked(refs[count : 2 * count])
    normed = refs[2 * count : 3 * count]
    halves, sums = refs[3 * count : 5 * count], refs[5 * count :]
    half, width = halves[0].shape
    for ref in sums:
        ref[...] = jnp.zeros_like(ref)
    step = min(256, width)
    for at in range(0, width, step):
        here = slice(at, at + step)
        terms = dot(mixed, heads_ref[here, :], ((1,), (1,)))
        terms += dot(hidden, up_ref[here, :], ((1,), (1,)))
        for w, ref in enumerate(sums):
            term = terms[2 * w * half : 2 * (w + 1) * half]
            ref[0:1, here] = jnp.sum(
                term * normed[w][:, here].astype(f32), axis=0, keepdims=True
            )
            ref[1:2, here] = jnp.sum(term, axis=0, keepdims=True)
        for i, ref in enumerate(halves):
            ref[:, here] = terms[i * half : (i + 1) * half].astype(bf16)


def acts_grad(heads, up, mixed, hidden, normed, after=()):
    count = len(mixed)
    length, width = normed[0].shape
    outs = [shape16(length // 2, width)] * (2 * count)
    outs += [jax.ShapeDtypeStruct((8, width), f32)] * count
    kernel = functools.partial(acts_grad_kernel, count)
    outs, done = call(kernel, [heads, up, *mixed, *hidden, *normed], outs, 10, after)
    return list(zip(outs[0 : 2 * count : 2], outs[1 : 2 * count : 2])), outs[2 * count :], done


def joined_windows(refs, scratch):
    at = 0
    for ref in refs:
        rows = ref.shape[0]
        scratch[at : at + rows, :] = ref[...]
        at += rows


def halved(shape):
    return [shape16(shape.shape[0] // 2, *shape.shape[1:])] * 2


def row_grads_kernel(rows, place_ref, *refs):
    activated, attended, grads = refs[:GROUP], refs[GROUP : 2 * GROUP], refs[2 * GROUP : -6]
    *theirs, mine_ref, a_ref, b_ref, g_ref = refs[-6:]
    joined_windows(activated, a_ref)
    joined_windows(attended, b_ref)
    joined_windows(grads, g_ref)
    first = place_ref[2] == 0
    grad = g_ref[...]
    at = 0
    for ref, size in ((a_ref, mine_ref.shape[1] - rows), (b_ref, rows)):
        step = min(256, ref.shape[1])
        for start in range(0, ref.shape[1], step):
            term = dot(ref[:, start : start + step], grad, ((0,), (0,))).astype(bf16)
            for pair in range(step // (CORES * size)):
                z = start // (CORES * size) + pair
                zero = term[pair * 2 * size : (pair * 2 + 1) * size]
                one = term[(pair * 2 + 1) * size : (pair * 2 + 2) * size]
                mine_ref[z, at : at + size, :] = jnp.where(first, zero, one)
                theirs[z // 2][z % 2, at : at + size, :] = jnp.where(first, one, zero)
        at += size


def row_grads(where, steps, rows, activated, attended, grads, after=()):
    length, hidden_part = activated[0].shape
    part = attended[0].shape[1]
    width = grads[0].shape[1]
    out = shape16(steps, hidden_part // (steps * CORES) + rows, width)
    scratch = [pltpu.VMEM((GROUP * length, w), bf16) for w in (hidden_part, part, width)]
    ins = [where, *activated, *attended, *grads]
    kernel = functools.partial(row_grads_kernel, rows)
    return call(kernel, ins, [*halved(out), out], 12, after, scratch)


def column_grads_kernel(rows, sums, place_ref, *refs):
    *theirs, mine_ref, a_ref, b_ref = refs[-5:]
    steps = mine_ref.shape[0]
    columns = b_ref.shape[1]
    joined_windows(refs[:GROUP], a_ref)
    joined_windows(refs[GROUP : 2 * GROUP], b_ref)
    first = place_ref[2] == 0
    grad = b_ref[...]
    step = steps * CORES * rows
    if sums:
        refs = refs[2 * GROUP :]
        acts_sums = sum((r[0:2, :] for r in refs[1:GROUP]), refs[0][0:2, :])
        joined_sums = sum((r[0:2, :] for r in refs[GROUP + 1 : 2 * GROUP]), refs[GROUP][0:2, :])
        row = lax.broadcasted_iota(jnp.int32, (rows, 128), 0)

        def tiles(t, z, c):
            number = (t * steps + z) * CORES + c
            at, up = number * rows // 128 * 128, (z * CORES + c) * 128
            value = jnp.zeros((rows, 128), f32)
            for k, line in enumerate(
                (
                    acts_sums[0:1, at : at + 128],
                    acts_sums[1:2, at : at + 128],
                    joined_sums[0:1, at : at + 128],
                    joined_sums[1:2, up : up + 128],
                )
            ):
                value = jnp.where(row == k, line, value)
            return value.astype(bf16)

    for t in range(GROUP):
        term = dot(a_ref[:, t * step : (t + 1) * step], grad, ((0,), (0,))).astype(bf16)
        here = slice(t * rows, (t + 1) * rows)
        for z in range(steps):
            zero = term[z * 2 * rows : (z * 2 + 1) * rows]
            one = term[(z * 2 + 1) * rows : (z * 2 + 2) * rows]
            mine_ref[z, here, :columns] = jnp.where(first, zero, one)
            theirs[z // 2][z % 2, here, :columns] = jnp.where(first, one, zero)
            if sums:
                zero, one = tiles(t, z, 0), tiles(t, z, 1)
                mine_ref[z, here, columns:] = jnp.where(first, zero, one)
                theirs[z // 2][z % 2, here, columns:] = jnp.where(first, one, zero)


def column_grads(where, steps, rows, acts, grads, after=(), sums=()):
    length, width = acts[0].shape
    columns = grads[0].shape[1]
    out = shape16(steps, GROUP * rows, columns + (128 if sums else 0))
    scratch = [pltpu.VMEM((GROUP * length, w), bf16) for w in (width, columns)]
    kernel = functools.partial(column_grads_kernel, rows, bool(sums))
    return call(kernel, [where, *acts, *grads, *sums], [*halved(out), out], 12, after, scratch)


def ring_begin_kernel(steps_on, place_ref, mine_ref, low_ref, high_ref, chip_ref, *firsts):
    steps = mine_ref.shape[0]
    for z in range(steps):
        got = (low_ref, high_ref)[z // 2][z % 2]
        chip_ref[z] = (mine_ref[z].astype(f32) + got.astype(f32)).astype(bf16)
    for on, ref in zip(steps_on, firsts):
        ref[...] = chip_ref[lax.rem(place_ref[1] + on, steps)]


def ring_add_kernel(on, place_ref, chip_ref, moving_ref, out_ref):
    at = lax.rem(place_ref[1] + on, chip_ref.shape[0])
    out_ref[...] = (chip_ref[at].astype(f32) + moving_ref[...].astype(f32)).astype(bf16)


def ring_rows_kernel(place_ref, chip_ref, *refs):
    down_ref, merge_ref = refs[-2:]
    total = chip_ref[place_ref[1]].astype(f32)
    for other in refs[:-2]:
        total += other[...].astype(f32)
    size = down_ref.shape[0]
    down_ref[...] = total[:size]
    merge_ref[...] = total[size:]


def ring_columns_kernel(count, place_ref, *refs):
    outs = refs[-GROUP:]
    rows = outs[0].shape[0]
    for mask in range(GROUP):
        t = jnp.bitwise_xor(place_ref[0], mask)
        at = pl.ds(pl.multiple_of(t * rows, rows), rows)
        column = 0
        for chip, *others in (refs[:count], refs[count:-GROUP]):
            total = chip[place_ref[1], at, :].astype(f32)
            for other in others:
                total += other[at, :].astype(f32)
            width = total.shape[1]
            outs[mask][:, column : column + width] = total.astype(bf16)
            column += width


def add_halves_kernel(*refs):
    one, two, low, high, one_ref, two_ref = refs[0:2], refs[2:4], *refs[4:]
    half = low.shape[0]
    one_ref[:half] = (one[0][...].astype(f32) + low[...].astype(f32)).astype(bf16)
    one_ref[half:] = one[1][...]
    two_ref[:half] = two[0][...]
    two_ref[half:] = (two[1][...].astype(f32) + high[...].astype(f32)).astype(bf16)


def add_halves(one, two, low, high, after=()):
    outs = [shape16(2 * low.shape[0], low.shape[1])] * 2
    return call(add_halves_kernel, [*one, *two, low, high], outs, 4, after)


def summed(own, one, two):
    return stacked(own).astype(f32) + one[...].astype(f32) + two[...].astype(f32)


def finish_out_kernel(tokens_ref, small_ref, low_ref, high_ref, one_ref, two_ref, out_ref):
    total = summed([low_ref, high_ref], one_ref, two_ref)
    out_ref[...] = (tokens_ref[...].astype(f32) + total + small_ref[2:3, :]).astype(bf16)


def finish_grad_kernel(
    tokens_ref, grad_ref, small_ref, low_ref, high_ref, one_ref, two_ref, out_ref
):
    normed, inverse_std = normalised(tokens_ref[...].astype(f32))
    normed_grad = summed([low_ref, high_ref], one_ref, two_ref) * small_ref[0:1, :]
    mean = jnp.mean(normed_grad, axis=-1, keepdims=True)
    along = jnp.mean(normed_grad * normed, axis=-1, keepdims=True)
    grad = grad_ref[...].astype(f32)
    out_ref[...] = (grad + inverse_std * (normed_grad - mean - normed * along)).astype(bf16)


def finish(kernel, arrays, own, one, two, after=()):
    (out,), done = call(kernel, [*arrays, *own, one, two], [shape16(*one.shape)], 10, after)
    return out, done


def prepare_kernel(
    place_ref, ends_ref, small_ref, heads_ref, up_ref, down_ref, merge_ref, *refs
):
    outs, sem = refs[: GROUP + 1], refs[-1]
    rows = heads_ref.shape[0]
    part = heads_ref.shape[1] // 3 // GROUP
    hidden_part = up_ref.shape[1] // GROUP
    hidden_rows = down_ref.shape[0]
    copies = []

    def copy(src, dst):
        copies.append(pltpu.make_async_copy(src, dst, sem.at[len(copies)]))

    for mask in range(GROUP):
        to = jnp.bitwise_xor(place_ref[0], mask)
        for k in range(3):
            at = pl.multiple_of((k * GROUP + to) * part, part)
            copy(heads_ref.at[:, pl.ds(at, part)], outs[mask].at[:, pl.ds(k * part, part)])
        at = pl.multiple_of(to * hidden_part, hidden_part)
        copy(
            up_ref.at[:, pl.ds(at, hidden_part)],
            outs[mask].at[:, pl.ds(3 * part + 128, hidden_part)],
        )
    copy(down_ref, outs[GROUP].at[pl.ds(0, hidden_rows)])
    copy(merge_ref, outs[GROUP].at[pl.ds(hidden_rows, rows)])
    for each in copies:
        each.start()
    quarter = place_ref[3]
    row = lax.broadcasted_iota(jnp.int32, (rows, 128), 0)
    lane = lax.broadcasted_iota(jnp.int32, (rows, 128), 1)
    first = jnp.broadcast_to(small_ref[0:1, :], (rows, 128))
    extra = jnp.zeros((rows, 128), f32)
    for k in range(3):
        moved = pltpu.roll(first, lax.rem(quarter * rows + (128 - k * rows), 128), 1)
        here = (row == k) & (lane >= quarter * rows) & (lane < (quarter + 1) * rows)
        extra = jnp.where(here, moved, extra)
    extra = jnp.where(row == 3, small_ref[1:2, :], extra)
    for k in range(2):
        value = ends_ref[k]
        for i, piece in enumerate((value // 16, value % 16)):
            extra = jnp.where((row == 4) & (lane == 2 * k + i), piece.astype(f32), extra)
    extra = extra.astype(bf16)
    for mask in range(GROUP):
        outs[mask][:, 3 * part : 3 * part + 128] = extra
    for each in copies:
        each.wait()


def prepare(where, ends, small, heads_weight, up_weight, down_weight, merge_weight):
    rows, width3 = heads_weight.shape
    columns = width3 // GROUP + up_weight.shape[1] // GROUP + 128
    block = (down_weight.shape[0] + merge_weight.shape[0], down_weight.shape[1])
    far = [heads_weight, up_weight, down_weight, merge_weight]
    far = [pltpu.with_memory_space_constraint(x, pltpu.HBM) for x in far]
    return pl.pallas_call(
        prepare_kernel,
        in_specs=[spec(pltpu.SMEM)] * 2 + [spec(pltpu.VMEM)] + [spec(pltpu.HBM)] * len(far),
        out_specs=[spec(pltpu.VMEM)] * (GROUP + 1),
        out_shape=[shape16(rows, columns)] * GROUP + [shape16(*block)],
        scratch_shapes=[pltpu.SemaphoreType.DMA((4 * GROUP + 2,))],
        **settings(2),
    )(where, ends, small, *far)


def small_rows_kernel(count, place_ref, extra_ref, small_ref):
    total = extra_ref.shape[0]
    rows = total // (count * GROUP)
    row = lax.broadcasted_iota(jnp.int32, (8, 128), 0)
    per = 128 // rows
    for tile in range(small_ref.shape[1] // 128):
        value = jnp.zeros((8, 128), f32)
        for i in range(per):
            at = (tile * per + i) * rows
            value += extra_ref[at : at + 16, :].astype(f32)[:8]
        if tile < count:
            at = pl.multiple_of((place_ref[0] * count + tile) * rows, rows)
            value = jnp.where(row == 3, extra_ref[pl.ds(at, 16), :].astype(f32)[:8], value)
        small_ref[:, tile * 128 : (tile + 1) * 128] = value


def assemble_kernel(layout, steps, with_small, sources, place_ref, *refs):
    count = steps * CORES
    extra_ref = refs[-1]
    outs = refs[-1 - len(layout) - with_small : -1]
    for number, (source, part) in enumerate(sources):
        piece = refs[source] if part is None else refs[source].at[part]
        z = place_ref[1] - number // CORES
        z = jnp.where(z < 0, z + steps, z)
        c = jnp.bitwise_xor(place_ref[2], number % CORES)
        row = 0
        for (rows, masks), out in zip(layout, outs):
            width = out.shape[1]
            for mask in range(masks):
                d = jnp.bitwise_xor(place_ref[0], mask) if masks > 1 else 0
                to = pl.ds(pl.multiple_of(((d * steps + z) * CORES + c) * rows, rows), rows)
                out[to, :] = piece[row : row + rows, :width]
                if with_small:
                    extra_ref[to, :] = piece[row : row + rows, width:]
                row += rows
    if with_small:
        small_rows_kernel(count, place_ref, extra_ref, outs[-1])


def assemble(place, where, arrays, sources, layout, with_small=False, after=()):
    width = arrays[0].shape[1] - (128 if with_small else 0)
    totals = [len(sources) * r * masks for r, masks in layout]
    outs = [shape16(total, width) for total in totals]
    if with_small:
        outs.append(jax.ShapeDtypeStruct((8, totals[0]), f32))
    kernel = functools.partial(assemble_kernel, layout, place.nz, with_small, sources)
    scratch = [pltpu.VMEM((totals[0], 128), bf16)]
    return call(kernel, [where, *arrays], outs, 2, after, scratch)


def stack_kernel(*refs):
    for i, ref in enumerate(refs[:-1]):
        refs[-1][i] = ref[...]


def stack(*arrays, after=()):
    (out,), done = call(stack_kernel, list(arrays), [shape16(len(arrays), *arrays[0].shape)], 2, after)
    return out, done


def halves_kernel(x_ref, low_ref, high_ref):
    half = low_ref.shape[0]
    low_ref[...] = x_ref[:half]
    high_ref[...] = x_ref[half:]


def halves(x, after=()):
    outs = [shape16(x.shape[0] // 2, x.shape[1])] * 2
    return call(halves_kernel, [x], outs, 3, after)


def cut_kernel(one_ref, two_ref, low_ref, high_ref):
    half = low_ref.shape[0]
    low_ref[...] = one_ref[:half]
    high_ref[...] = two_ref[half:]


def cut(one, two, after=()):
    outs = [shape16(one.shape[0] // 2, one.shape[1])] * 2
    return call(cut_kernel, [one, two], outs, 2, after)


def plain_assemble(place, pieces, layout):
    steps = place.nz
    flat = [piece for pair in pieces for piece in pair]
    width = flat[0].shape[1]
    stacked_pieces = jnp.stack(flat).reshape(steps, CORES, place.no, -1, width)
    stacked_pieces = jnp.take(stacked_pieces, (place.z - np.arange(steps)) % steps, axis=0)
    stacked_pieces = jnp.take(stacked_pieces, np.arange(CORES) ^ place.c, axis=1)
    outs, row = [], 0
    for r, masks in layout:
        part = stacked_pieces[:, :, :, row : row + r * masks]
        part = part.reshape(steps, CORES, place.no, masks, r, width)
        if masks > 1:
            part = jnp.take(part, np.arange(masks) ^ place.t, axis=3)
        outs.append(part.transpose(2, 3, 0, 1, 4, 5).reshape(-1, width))
        row += r * masks
    return outs


def columns_out_kernel(place_ref, *refs):
    blocks = refs[:GROUP]
    heads_out_ref, up_out_ref, *moved_refs, hidden_ref = refs[GROUP:]
    rows = blocks[0].shape[0]
    hidden_part = up_out_ref.shape[1] // GROUP
    part = heads_out_ref.shape[1] // GROUP // 3
    total = jnp.zeros((16, 128), f32)
    for mask in range(GROUP):
        to = jnp.bitwise_xor(place_ref[0], mask)
        at = pl.multiple_of(to * hidden_part, hidden_part)
        up_out_ref[:, pl.ds(at, hidden_part)] = blocks[mask][:, :hidden_part].astype(f32)
        for k in range(3):
            at = pl.multiple_of((k * GROUP + to) * part, part)
            start = hidden_part + k * part
            heads_out_ref[:, pl.ds(at, part)] = blocks[mask][:, start : start + part].astype(f32)
        total += blocks[mask][:16, hidden_part + 3 * part :].astype(f32)
    own = blocks[0][:16, hidden_part + 3 * part :].astype(f32)
    row = lax.broadcasted_iota(jnp.int32, (16, 128), 0)
    value = jnp.where(row < 2, total, own)
    moved = pltpu.roll(value, lax.rem(128 - place_ref[3] * rows, 128), 1)
    for k, ref in enumerate(moved_refs):
        ref[...] = moved[k : k + 1, :rows]
    hidden_ref[...] = value[3:4]


def columns_out(where, blocks, hidden_part):
    rows, columns = blocks[0].shape
    outs = [
        jax.ShapeDtypeStruct((rows, GROUP * (columns - 128 - hidden_part)), f32),
        jax.ShapeDtypeStruct((rows, GROUP * hidden_part), f32),
    ] + [jax.ShapeDtypeStruct((1, n), f32) for n in (rows, rows, rows, 128)]
    return call(columns_out_kernel, [where, *blocks], outs, 4)[0]


class Place:
    def __init__(self, sizes):
        self.ndp = sizes["dp"]
        self.no = self.ndp // GROUP
        self.nf = sizes["fsdp"]
        self.nz = self.nf // CORES
        fsdp = lax.axis_index("fsdp")
        self.dp = lax.axis_index("dp")
        self.t = self.dp % GROUP
        self.z = fsdp // CORES
        self.c = fsdp % CORES
        self.outer_groups = [[o * GROUP + t for o in range(self.no)] for t in range(GROUP)]

    def send(self, x, to):
        pairs = []
        for d in range(self.ndp):
            for z in range(self.nz):
                for c in range(CORES):
                    d2, z2, c2 = to(d, z, c)
                    pairs.append(
                        (d * self.nf + z * CORES + c, d2 * self.nf + z2 * CORES + c2)
                    )
        return lax.ppermute(x, AXES, pairs)

    def swap_t(self, x, mask):
        return self.send(x, lambda d, z, c: (d ^ mask, z, c))

    def shift_z(self, x, step=1):
        return self.send(x, lambda d, z, c: (d, (z + step) % self.nz, c))

    def swap_core(self, x):
        return self.send(x, lambda d, z, c: (d, z, CORES - 1 - c))


def later(x, *after):
    return lax.optimization_barrier((x,) + after)[0]


def add(a, b):
    return a.astype(f32) + b.astype(f32)


class RingSum:
    def __init__(self, place, where, theirs, mine, *after):
        self.place, self.where, self.mine = place, where, mine
        self.got = [place.swap_core(later(x, *after)) for x in theirs]

    def run(self, kernel, arrays, outs, after):
        return call(kernel, [self.where, *arrays], outs, 6, after)

    def first(self, steps_on, after):
        block = shape16(*self.mine.shape[1:])
        outs = [shape16(*self.mine.shape)] + [block] * len(steps_on)
        kernel = functools.partial(ring_begin_kernel, steps_on)
        (self.chip, *firsts), done = self.run(kernel, [self.mine, *self.got], outs, after)
        return firsts, done

    def added(self, on, after):
        outs = [shape16(*self.moving.shape)]
        kernel = functools.partial(ring_add_kernel, on)
        (out,), done = self.run(kernel, [self.chip, self.moving], outs, after)
        return out, done

    def begin(self, *after):
        (first,), done = self.first((3,), after)
        self.moving, self.on = self.place.shift_z(first), 3
        return done

    def pass_on(self, out):
        self.moving = self.place.shift_z(out)

    def next(self, *after):
        self.on -= 1
        return self.added(self.on, after)

    def step(self, *after):
        out, done = self.next(*after)
        self.pass_on(out)
        return done

    def terms(self):
        return [self.chip, self.moving]


class PairSum(RingSum):
    def begin(self, *after):
        (far, back), done = self.first((2, 3), after)
        self.moving, self.back = self.place.shift_z(far), self.place.shift_z(back, -1)
        return done

    def step(self, *after):
        out, done = self.added(1, after)
        self.moving = self.place.shift_z(out)
        return done

    def terms(self):
        return [self.chip, self.back, self.moving]


def plain_sum(place, terms):
    terms = lax.psum_scatter(terms, "dp", scatter_dimension=0, axis_index_groups=place.outer_groups)
    theirs = lax.dynamic_index_in_dim(terms, 1 - place.c, 1, keepdims=False)
    chip = lax.dynamic_index_in_dim(terms, place.c, 1, keepdims=False)
    chip = add(chip, place.swap_core(theirs)).astype(bf16)
    moving = None
    for step in range(1, place.nz + 1):
        own = lax.dynamic_index_in_dim(chip, (place.z - step) % place.nz, 0, keepdims=False)
        moving = own if moving is None else add(place.shift_z(moving), own).astype(bf16)
    return moving.astype(f32)


def plain_gather(place, block):
    block = lax.all_gather(block, "dp", axis_index_groups=place.outer_groups, tiled=True)
    blocks = [block]
    for _ in range(place.nz - 1):
        blocks.append(place.shift_z(blocks[-1]))
    return [(b, place.swap_core(b)) for b in blocks]


def gather_windows(place, own):
    half = own.shape[0] // 2
    one, two = place.swap_t(own, 1), place.swap_t(own, 2)
    three = [place.swap_t(one[:half], 2), place.swap_t(two[half:], 1)]
    return [[own], [one], [two], three]


def sum_windows(place, terms):
    low, high = place.swap_t(terms[3][0], 2), place.swap_t(terms[3][1], 1)
    (one, two), _ = add_halves(terms[1], terms[2], low, high)
    return terms[0], place.swap_t(one, 1), place.swap_t(two, 2)


def columns(place, heads_weight, up_weight, mask):
    rows, width3 = heads_weight.shape
    part = width3 // 3 // GROUP
    hidden_part = up_weight.shape[1] // GROUP
    to = place.t ^ mask
    joint = [
        lax.dynamic_slice_in_dim(heads_weight, (k * GROUP + to) * part, part, axis=1)
        for k in range(3)
    ]
    up = lax.dynamic_slice_in_dim(up_weight, to * hidden_part, hidden_part, axis=1)
    return jnp.concatenate(joint + [up], axis=1)


def spread(vector, at, count):
    n = vector.shape[0]
    row = jnp.tile(vector.astype(f32).reshape(1, n), (1, count))
    lane = lax.broadcasted_iota(jnp.int32, row.shape, 1)
    return jnp.where(lane // n == at, row, 0.0)


def small_gather(place, norm_gain, norm_bias, down_bias, up_bias, offsets, terminal):
    here = ((place.dp * place.nz) + place.z) * CORES + place.c
    count = place.ndp * place.nf
    rows = jnp.concatenate([spread(v, here, count) for v in (norm_gain, norm_bias, down_bias)])
    fsdp = (place.dp // GROUP * place.nz + place.z) * CORES + place.c
    own = spread(up_bias, fsdp, place.no * place.nf)
    lanes = rows.shape[1]
    both = jnp.concatenate([rows, jnp.pad(own, ((0, 0), (0, lanes - own.shape[1])))])
    if place.no > 1:
        both = lax.psum(both, "dp", axis_index_groups=place.outer_groups)
    shifted = [place.shift_z(both, s) for s in range(1, place.nz)]
    both = sum(shifted, both)
    both = both + place.swap_core(both)
    ends = jnp.concatenate([offsets, terminal]).astype(f32).reshape(1, -1)
    ends = jnp.pad(ends, ((0, 0), (0, lanes - ends.shape[1])))
    group = jnp.concatenate([both[:3], ends])
    others = [place.swap_t(group, m) for m in range(1, GROUP)]
    rows = sum((o[:3] for o in others), group[:3])
    windows = offsets.shape[0]
    ends = jnp.concatenate([g[3:4, : 2 * windows] for g in [group] + others])
    return rows, both[3:4, : own.shape[1]], ends


def plain_shards(
    place,
    tokens,
    heads_weight,
    merge_weight,
    up_weight,
    up_bias,
    down_weight,
    down_bias,
    norm_gain,
    norm_bias,
    offsets,
    terminal,
    cotangent,
):
    nz, no = place.nz, place.no
    length, width = tokens.shape
    head = width // HEADS
    rows = heads_weight.shape[0]
    hidden_rows = down_weight.shape[0]
    part = width // GROUP
    hidden_part = up_weight.shape[1] // GROUP
    number = place.dp * place.nf + place.z * CORES + place.c
    tables = turn_tables(length, head, 128)
    pieces = [columns(place, heads_weight, up_weight, m) for m in range(GROUP)]
    pieces = jnp.concatenate([pieces[0]] + [place.swap_t(pieces[m], m) for m in range(1, GROUP)])
    layout = [(rows, GROUP)]
    (heads,) = plain_assemble(place, plain_gather(place, pieces[:, : 3 * part]), layout)
    (up,) = plain_assemble(place, plain_gather(place, pieces[:, 3 * part :]), layout)
    block = jnp.concatenate([down_weight, merge_weight])
    layout = [(hidden_rows, 1), (rows, 1)]
    down, merge = plain_assemble(place, plain_gather(place, block), layout)
    small, up_shift, ends = small_gather(
        place, norm_gain, norm_bias, down_bias, up_bias, offsets, terminal
    )
    up_shift = jnp.pad(up_shift, ((0, 4), (0, width - hidden_part)))
    small = jnp.concatenate([small, up_shift])
    ends = jnp.stack([jnp.floor(ends / 16.0), ends % 16.0], axis=-1).reshape(GROUP, 1, 4)
    ends = jnp.pad(ends, ((0, 0), (4, 11), (0, 124))).reshape(16 * GROUP, 128)
    windows = gather_windows(place, tokens)
    grads = gather_windows(place, cotangent)

    saved = [attend(w, ends, windows[w], heads, small, tables, head)[0] for w in range(GROUP)]
    acts, normed, attended, qkv, lse = zip(*saved)
    activated, slope = zip(*(hidden_units([a], up, small)[0][0] for a in acts))
    outs = [out_terms([activated[w]], [attended[w]], down, merge)[0][0] for w in range(GROUP)]
    block_output, _ = finish(finish_out_kernel, [tokens, small], *sum_windows(place, outs))
    (hidden_grad, attended_grad, joined_sums), _ = joined_grad(grads, down, merge, slope)
    mixed_grad, terms, acts_sums = [], [], []
    for w in range(GROUP):
        mixed = attend_back(w, ends, qkv[w], attended_grad[w], lse[w], tables, head)[0][0]
        halves, sums, _ = acts_grad(heads, up, [mixed], [hidden_grad[w]], [normed[w]])
        mixed_grad.append(mixed)
        terms += halves
        acts_sums += sums
    grad_tokens, _ = finish(
        finish_grad_kernel, [tokens, cotangent, small], *sum_windows(place, terms)
    )

    def product(left, right):
        left, right = jnp.concatenate(left), jnp.concatenate(right)
        return dot(left, right, ((0,), (0,))).astype(bf16)

    def by_place(terms):
        terms = terms.reshape(no, GROUP, nz, CORES, rows, terms.shape[1])
        return terms.transpose(0, 2, 3, 1, 4, 5)

    def by_t(summed):
        blocks = [
            lax.dynamic_index_in_dim(summed, place.t ^ m, 0, keepdims=False) for m in range(GROUP)
        ]
        arrived = [blocks[0]] + [place.swap_t(blocks[m].astype(bf16), m) for m in range(1, GROUP)]
        arrived = [a.astype(f32) for a in arrived]
        return [lax.select_n(t ^ place.t, *arrived) for t in range(GROUP)]

    flat = [h for pair in grads for h in pair]
    down_terms = product(activated, flat).reshape(no, nz, CORES, hidden_rows, width)
    merge_terms = product(attended, flat).reshape(no, nz, CORES, rows, width)
    row_total = plain_sum(place, jnp.concatenate([down_terms, merge_terms], axis=3))
    heads_by_t = by_t(plain_sum(place, by_place(product(acts, mixed_grad))))
    up_by_t = by_t(plain_sum(place, by_place(product(acts, hidden_grad))))
    grad_heads = jnp.concatenate(
        [h[:, k * part : (k + 1) * part] for k in range(3) for h in heads_by_t], axis=1
    )
    group_sums = jnp.concatenate([sum(acts_sums)[:2], sum(joined_sums)[:2, :width]])
    group_sums = group_sums + place.swap_core(group_sums)
    group_sums = lax.psum(group_sums, "dp", axis_index_groups=place.outer_groups)
    group_sums = sum((place.shift_z(group_sums, s) for s in range(1, nz)), group_sums)
    all_sums = sum((place.swap_t(group_sums, m) for m in range(1, GROUP)), group_sums)
    grad_gain, grad_bias = (
        lax.dynamic_slice_in_dim(all_sums[k], number * rows, rows) for k in range(2)
    )
    at = (place.dp // GROUP * place.nf + place.z * CORES + place.c) * hidden_rows
    return (
        block_output,
        grad_tokens,
        grad_heads,
        row_total[hidden_rows:],
        jnp.concatenate(up_by_t, axis=1),
        lax.dynamic_slice_in_dim(group_sums[3], at, hidden_rows),
        row_total[:hidden_rows],
        lax.dynamic_slice_in_dim(group_sums[2], number * rows, rows),
        grad_gain,
        grad_bias,
    )


def paced_shards(
    place,
    tokens,
    heads_weight,
    merge_weight,
    up_weight,
    up_bias,
    down_weight,
    down_bias,
    norm_gain,
    norm_bias,
    offsets,
    terminal,
    cotangent,
):
    nz = place.nz
    length, width = tokens.shape
    head = width // HEADS
    rows = heads_weight.shape[0]
    hidden_rows = down_weight.shape[0]
    part = width // GROUP
    hidden_part = up_weight.shape[1] // GROUP
    number = place.dp * place.nf + place.z * CORES + place.c
    where = jnp.stack([place.t, place.z, place.c, number % (128 // rows)]).astype(jnp.int32)
    tables = turn_tables(length, head, 128)
    send, shift, swap = place.swap_t, place.shift_z, place.swap_core

    vectors, at = 0.0, 0
    for v in (norm_gain, norm_bias, down_bias, up_bias):
        v = v.astype(f32)
        at = at if v.shape[0] < 128 else 128
        vectors += jnp.pad(v, (at, 256 - at - v.shape[0]))
        at += v.shape[0]
    *pieces, row_block = prepare(
        where,
        jnp.concatenate([offsets, terminal]),
        vectors.reshape(2, 128),
        heads_weight,
        up_weight,
        down_weight,
        merge_weight,
    )
    joint = 3 * part + 128
    arrived = [send(pieces[m], m) for m in range(1, GROUP)]
    pieces = [pieces[0]] + arrived
    joint_block = jnp.concatenate([p[:, :joint] for p in pieces])
    up_block = jnp.concatenate([p[:, joint:] for p in pieces])

    joint_blocks, up_blocks, row_blocks = [joint_block], [up_block], [row_block]
    joint_blocks.append(shift(joint_block))
    tokens_one = send(later(tokens, *arrived), 1)
    tokens_two = send(later(tokens, *arrived), 2)
    joint_blocks.append(shift(joint_blocks[1]))
    early, _ = stack(*joint_blocks[:2])
    early = swap(early)
    up_blocks.append(shift(later(up_block, joint_blocks[1])))
    joint_blocks.append(shift(joint_blocks[2]))
    (three_low, three_high), cut_done = cut(tokens_one, tokens_two, [joint_blocks[2]])
    up_blocks.append(shift(later(up_blocks[1], joint_blocks[3])))
    third, fourth = swap(joint_blocks[2]), swap(later(joint_blocks[3], cut_done))
    three_low, three_high = send(three_low, 2), send(three_high, 1)
    sources = [(0, None), (4, 0), (1, None), (4, 1), (2, None), (5, 0), (3, None), (5, 1)]
    split = [*sources[:5], (5, None), (3, None), (6, None)]
    layout = [(rows, GROUP)]
    (heads, small), done = assemble(
        place, where, [*joint_blocks, early, third, fourth], split, layout, True, [cut_done]
    )

    def attended_window(window, parts, *after):
        return attend(window, joint_block, parts, heads, small, tables, head, after)

    saved, units = [None] * GROUP, [None] * GROUP
    row_blocks.append(shift(later(row_block, joint_blocks[3])))
    grad_one, grad_two = send(later(cotangent, done), 1), send(later(cotangent, done), 2)
    saved[0], done = attended_window(0, [tokens], done, three_low, three_high)
    saved[1], done = attended_window(1, [tokens_one], done)
    up_blocks.append(shift(later(up_blocks[2], done)))
    saved[2], done = attended_window(2, [tokens_two], done)
    saved[3], done = attended_window(3, [three_low, three_high], done)
    early, done = stack(*up_blocks[:2], after=[done, row_blocks[1]])
    late, done = stack(*up_blocks[2:], after=[done])
    early, late = swap(early), swap(late)
    row_blocks.append(shift(later(row_blocks[1], done)))
    (up,), done = assemble(
        place, where, [*up_blocks, early, late], sources, layout, after=[done]
    )
    units[0:1], done = hidden_units([saved[0][0]], up, small, [done])
    (grad_low, grad_high), done = cut(grad_one, grad_two, [done])
    grad_low, grad_high = send(grad_low, 2), send(grad_high, 1)
    units[1:3], done = hidden_units([saved[1][0], saved[2][0]], up, small, [done])
    row_blocks.append(shift(later(row_blocks[2], done)))
    units[3:4], done = hidden_units([saved[3][0]], up, small, [done])
    acts, normed, attended, qkv, lse = zip(*saved)
    activated, slope = zip(*units)
    grads = [[cotangent], [grad_one], [grad_two], [grad_low, grad_high]]

    flat = [h for parts in grads for h in parts]
    early, done = stack(*row_blocks[:2], after=[done])
    early = swap(early)
    (*theirs, mine), done = row_grads(where, nz, rows, activated, attended, flat, [done])
    late, done = stack(*row_blocks[2:], after=[done])
    late = swap(late)
    row_sum = RingSum(place, where, theirs, mine, done)
    (down, merge), done = assemble(
        place,
        where,
        [*row_blocks, early, late],
        sources,
        [(hidden_rows, 1), (rows, 1)],
        after=[done],
    )

    def out_of(windows, *after):
        picked = [activated[w] for w in windows], [attended[w] for w in windows]
        return out_terms(*picked, down, merge, after)

    outs = [None] * GROUP
    outs[3:4], done = out_of([3], done)
    out_low, out_high = send(outs[3][0], 2), send(outs[3][1], 1)
    done = row_sum.begin(done)
    outs[1:3], done = out_of([1, 2], done)
    (hidden_grad, attended_grad, joined_sums), done = joined_grad(grads, down, merge, slope, [done])

    mixed_grad, terms, acts_sums = [None] * GROUP, [None] * GROUP, [None] * GROUP

    def acts_of(windows, *after):
        picked = [[x[w] for w in windows] for x in (mixed_grad, hidden_grad, normed)]
        return acts_grad(heads, up, *picked, after)

    (*theirs, mine), done = column_grads(where, nz, rows, acts, hidden_grad, [done])
    after = [done, row_sum.moving]
    (out_one, out_two), done = add_halves(outs[1], outs[2], out_low, out_high, after)
    out_one, out_two = send(out_one, 1), send(out_two, 2)
    up_sum = RingSum(place, where, theirs, mine, done)
    done = up_sum.begin(done)

    def back(w, *after):
        (mixed_grad[w],), done = attend_back(
            w, joint_block, qkv[w], attended_grad[w], lse[w], tables, head, after
        )
        return done

    done = back(3, done)
    done = row_sum.step(done)
    done = back(1, done)
    done = back(2, done)
    done = up_sum.step(done)
    terms[3:4], acts_sums[3:4], done = acts_of([3], done)
    low, high = send(terms[3][0], 2), send(terms[3][1], 1)
    done = back(0, done)
    terms[0:3], acts_sums[0:3], done = acts_of([0, 1, 2], done, out_one, out_two)
    done = up_sum.step(done)
    sums = [*acts_sums, *joined_sums]
    (*theirs, mine), done = column_grads(where, nz, rows, acts, mixed_grad, [done], sums)
    heads_sum = PairSum(place, where, theirs, mine, done)
    last_rows, done = row_sum.next(done)
    after = [done, up_sum.moving]
    (one, two), done = add_halves(terms[1], terms[2], low, high, after)
    one, two = send(one, 1), send(two, 2)
    done = heads_sum.begin(done)
    outs[0:1], done = out_of([0], done)
    block_output, done = finish(
        finish_out_kernel, [tokens, small], outs[0], out_one, out_two, [done]
    )
    done = heads_sum.step(done)
    row_sum.pass_on(later(last_rows, heads_sum.back))
    columns = hidden_part + 3 * part + 128
    blocks, done = call(
        functools.partial(ring_columns_kernel, len(up_sum.terms())),
        [where, *up_sum.terms(), *heads_sum.terms()],
        [shape16(rows, columns)] * GROUP,
        4,
        [done, heads_sum.back, one, two],
    )
    blocks = [blocks[0]] + [send(blocks[m], m) for m in range(1, GROUP)]
    grad_tokens, done = finish(
        finish_grad_kernel, [tokens, cotangent, small], terms[0], one, two, [done]
    )
    both = [jax.ShapeDtypeStruct((n, width), f32) for n in (hidden_rows, rows)]
    (grad_down, grad_merge), done = call(
        ring_rows_kernel, [where, *row_sum.terms()], both, 4, [done]
    )
    grad_heads, grad_up, *narrow = columns_out(where, blocks, hidden_part)
    grad_gain, grad_bias, grad_down_bias, grad_up_bias = (x.reshape(-1) for x in narrow)
    return (
        block_output,
        grad_tokens,
        grad_heads,
        grad_merge,
        grad_up,
        grad_up_bias,
        grad_down,
        grad_down_bias,
        grad_gain,
        grad_bias,
    )


def shards(sizes, tokens, *arrays):
    *weights, cotangent = arrays
    place = Place(sizes)
    rows, hidden_rows, part = weights[0].shape[0], weights[4].shape[0], tokens.shape[2] // GROUP
    paced = (
        (place.no, place.nz) == (1, 4)
        and rows % 16 == 0
        and 128 % rows == 0
        and hidden_rows == 128
        and part % 128 == 0
    )
    run = paced_shards if paced else plain_shards
    block_output, grad_tokens, *grads = run(place, tokens[0], *weights, cotangent[0])
    return (block_output[None], grad_tokens[None], *grads)


def solution(mesh):
    whole = P(AXES)
    return jax.shard_map(
        functools.partial(shards, dict(mesh.shape)),
        mesh=mesh,
        in_specs=(whole,) * 12,
        out_specs=(whole,) * 10,
        check_vma=False,
    )
```

```python
import functools

import jax
import jax.numpy as jnp
import numpy as np
from jax import lax
from jax.experimental import pallas as pl
from jax.experimental.pallas import tpu as pltpu
from jax.sharding import PartitionSpec as P

HEADS = 16
ROT = 32
CORES = 2
GROUP = 4
AXES = ("dp", "fsdp")

eps = 1e-05
big_negative = -1e30
gelu_scale = 0.7978845608028654
gelu_cubic = 0.044715

bf16 = jnp.bfloat16
f32 = jnp.float32


def turn_tables(length, head, lanes):
    position = np.arange(length, dtype=np.float32)
    exponent = np.arange(0, ROT, 2, dtype=np.float32) / np.float32(ROT)
    rate = (np.float32(1.0) / np.power(np.float32(10000.0), exponent)).astype(np.float32)
    phase = (position[:, None] * rate[None, :]).astype(np.float32)
    cosine = np.ones((length, head), np.float32)
    sine = np.zeros((length, head), np.float32)
    cosine[:, :ROT] = np.repeat(np.cos(phase), 2, axis=1)
    sine[:, :ROT] = np.repeat(np.sin(phase), 2, axis=1)
    sine[:, 0:ROT:2] *= -1.0
    copies = lanes // head
    return np.tile(cosine, (1, copies)), np.tile(sine, (1, copies))


def turned(values, cosine, sine):
    lanes = values.shape[1]
    even = lax.broadcasted_iota(jnp.int32, values.shape, 1) % 2 == 0
    other = jnp.where(even, pltpu.roll(values, lanes - 1, 1), pltpu.roll(values, 1, 1))
    return values * cosine + other * sine


def dot(a, b, dims=((1,), (0,))):
    return lax.dot_general(a, b, (dims, ((), ())), preferred_element_type=f32)


def allowed_pairs(ends, length):
    offset = (16.0 * ends[:, 0:1] + ends[:, 1:2]).astype(jnp.int32)
    end = (16.0 * ends[:, 2:3] + ends[:, 3:4]).astype(jnp.int32)
    key = lax.broadcasted_iota(jnp.int32, (length, 1), 0)
    query = lax.broadcasted_iota(jnp.int32, (1, length), 1)
    key_part = (key >= offset).astype(jnp.int32) + (key > end).astype(jnp.int32)
    query_part = (query >= offset).astype(jnp.int32) + (query > end).astype(jnp.int32)
    return (key_part == query_part) & (query >= key)


def spec(space):
    return pl.BlockSpec(memory_space=space)


def settings(mebibytes):
    return {
        "compiler_params": pltpu.CompilerParams(vmem_limit_bytes=mebibytes * 2**20),
        "cost_estimate": pl.CostEstimate(flops=1, bytes_accessed=1, transcendentals=0),
    }


TICK = jax.ShapeDtypeStruct((8, 128), jnp.float32)


def tick(ref):
    ref[...] = jnp.zeros_like(ref)


def call(kernel, ins, outs, mebibytes, after=(), scratch=()):
    many = len(ins)

    def body(*refs):
        rest = refs[many + len(after) :]
        tick(rest[len(outs)])
        kernel(*refs[:many], *rest[: len(outs)], *rest[len(outs) + 1 :])

    result = pl.pallas_call(
        body,
        in_specs=[spec(pltpu.SMEM if x.dtype == jnp.int32 else pltpu.VMEM) for x in ins]
        + [spec(pl.ANY)] * len(after),
        out_specs=[spec(pltpu.VMEM)] * (len(outs) + 1),
        out_shape=[*outs, TICK],
        scratch_shapes=list(scratch),
        **settings(mebibytes),
    )(*ins, *after)
    return result[:-1], result[-1]


def shape16(*dims):
    return jax.ShapeDtypeStruct(dims, bf16)


def stacked(refs):
    return jnp.concatenate([r[...] for r in refs])


def normalised(values):
    mean = jnp.mean(values, axis=-1, keepdims=True)
    centered = values - mean
    inverse_std = lax.rsqrt(jnp.mean(centered * centered, axis=-1, keepdims=True) + eps)
    return centered * inverse_std, inverse_std


def gelu_and_slope(h):
    square = h * h
    tanh_value = jnp.tanh(h * (gelu_scale + gelu_scale * gelu_cubic * square))
    half = 0.5 + 0.5 * tanh_value
    value = h * half
    factor = 2.0 * gelu_scale + 6.0 * gelu_scale * gelu_cubic * square
    return value, half + (value - value * half) * factor


def ends_of(window, ends_ref):
    rows, width = ends_ref.shape
    at = rows // GROUP * window
    return ends_ref[at : at + 16, width - 128 :].astype(f32)[4:5]


def attend_kernel(head, window, ends_ref, heads_ref, small_ref, cos_ref, sin_ref, *refs):
    tokens = refs[:-5]
    acts_ref, normed_ref, attended_ref, qkv_ref, lse_ref = refs[-5:]
    length, part = attended_ref.shape
    lanes = cos_ref.shape[1]
    normed, _ = normalised(stacked(tokens).astype(f32))
    normed_ref[...] = normed.astype(bf16)
    acts_ref[...] = (normed * small_ref[0:1, :] + small_ref[1:2, :]).astype(bf16)
    acts = acts_ref[...]
    query_all, keys_all, values_all = (
        dot(acts, heads_ref[:, k * part : (k + 1) * part]) for k in range(3)
    )
    allowed = allowed_pairs(ends_of(window, ends_ref), length)
    cosine, sine = cos_ref[...], sin_ref[...]
    lane = lax.broadcasted_iota(jnp.int32, (1, lanes), 1)
    heads_of = [(at, sub) for at in range(0, part, lanes) for sub in range(lanes // head)]
    queries, scores, values_turned = {}, [], {}
    for at in range(0, part, lanes):
        query = (turned(query_all[:, at : at + lanes], cosine, sine) * head ** (-0.5)).astype(bf16)
        keys = turned(keys_all[:, at : at + lanes], cosine, sine).astype(bf16)
        values = values_all[:, at : at + lanes]
        qkv_ref[:, at : at + lanes] = query
        qkv_ref[:, part + at : part + at + lanes] = keys
        qkv_ref[:, 2 * part + at : 2 * part + at + lanes] = values.astype(bf16)
        values_turned[at] = values.T.astype(bf16)
        for sub in range(lanes // head):
            mine = (lane >= sub * head) & (lane < (sub + 1) * head)
            scores.append(dot(jnp.where(mine, keys, 0), query, ((1,), (1,))))
    probs = []
    for number, score in enumerate(scores):
        score = jnp.where(allowed, score, big_negative)
        top = jnp.max(score, axis=0, keepdims=True)
        expo = jnp.exp(score - top)
        total = jnp.sum(expo, axis=0, keepdims=True)
        probs.append((expo * (1.0 / total)).astype(bf16))
        lse_ref[number : number + 1, :] = top + jnp.log(total)
    outs = [
        dot(values_turned[at][sub * head : (sub + 1) * head, :], prob)
        for (at, sub), prob in zip(heads_of, probs)
    ]
    attended_ref[...] = jnp.concatenate(outs, axis=0).T.astype(bf16)


def attend(window, ends, tokens, heads, small, tables, head, after=()):
    length, width = sum(t.shape[0] for t in tokens), tokens[0].shape[1]
    part = heads.shape[1] // 3
    outs = [shape16(length, w) for w in (width, width, part, 3 * part)]
    outs.append(jax.ShapeDtypeStruct((max(8, part // head), length), f32))
    kernel = functools.partial(attend_kernel, head, window)
    return call(kernel, [ends, heads, small, *tables, *tokens], outs, 6, after)


def hidden_kernel(up_ref, small_ref, *refs):
    count = len(refs) // 3
    acts = stacked(refs[:count])
    length, hidden_part = refs[count].shape
    step = min(256, hidden_part)
    for at in range(0, hidden_part, step):
        here = slice(at, at + step)
        hidden = dot(acts, up_ref[:, here])
        value, slope = gelu_and_slope(hidden + small_ref[3:4, here])
        for w in range(count):
            rows = slice(w * length, (w + 1) * length)
            refs[count + w][:, here] = value[rows].astype(bf16)
            refs[2 * count + w][:, here] = slope[rows].astype(bf16)


def hidden_units(acts, up, small, after=()):
    outs = [shape16(acts[0].shape[0], up.shape[1])] * (2 * len(acts))
    outs, done = call(hidden_kernel, [up, small, *acts], outs, 8, after)
    return list(zip(outs[: len(acts)], outs[len(acts) :])), done


def out_kernel(down_ref, merge_ref, *refs):
    count = len(refs) // 4
    activated, attended = stacked(refs[:count]), stacked(refs[count : 2 * count])
    halves = refs[2 * count :]
    half, width = halves[0].shape
    step = min(256, width)
    for at in range(0, width, step):
        here = slice(at, at + step)
        term = dot(activated, down_ref[:, here])
        term = (term + dot(attended, merge_ref[:, here])).astype(bf16)
        for i, ref in enumerate(halves):
            ref[:, here] = term[i * half : (i + 1) * half]


def out_terms(activated, attended, down, merge, after=()):
    outs = [shape16(activated[0].shape[0] // 2, down.shape[1])] * (2 * len(activated))
    outs, done = call(out_kernel, [down, merge, *activated, *attended], outs, 8, after)
    return list(zip(outs[::2], outs[1::2])), done


def joined_grad_kernel(count, down_ref, merge_ref, *refs):
    slopes, grads, outs = refs[:count], refs[count : -3 * count], refs[-3 * count :]
    hiddens, attendeds, sums = outs[:count], outs[count : 2 * count], outs[2 * count :]
    length, hidden_part = hiddens[0].shape
    grad = stacked(grads)
    windows = [slice(w * length, (w + 1) * length) for w in range(count)]
    for ref, rows in zip(sums, windows):
        ref[...] = jnp.zeros_like(ref)
        ref[0:1, :] = jnp.sum(grad[rows].astype(f32), axis=0, keepdims=True)
    step = min(256, hidden_part)
    for at in range(0, hidden_part, step):
        here = slice(at, at + step)
        terms = dot(grad, down_ref[here, :], ((1,), (1,)))
        for w, rows in enumerate(windows):
            term = (terms[rows] * slopes[w][:, here].astype(f32)).astype(bf16)
            hiddens[w][:, here] = term
            sums[w][1:2, here] = jnp.sum(term.astype(f32), axis=0, keepdims=True)
    terms = dot(grad, merge_ref[...], ((1,), (1,))).astype(bf16)
    for ref, rows in zip(attendeds, windows):
        ref[...] = terms[rows]


def joined_grad(grads, down, merge, slopes, after=()):
    count = len(slopes)
    length, hidden_part = slopes[0].shape
    outs = [shape16(length, hidden_part)] * count + [shape16(length, merge.shape[0])] * count
    outs += [jax.ShapeDtypeStruct((8, max(down.shape)), f32)] * count
    flat = [part for parts in grads for part in parts]
    kernel = functools.partial(joined_grad_kernel, count)
    outs, done = call(kernel, [down, merge, *slopes, *flat], outs, 16, after)
    return [outs[k * count : (k + 1) * count] for k in range(3)], done


def attend_back_kernel(
    head, window, ends_ref, cos_ref, sin_ref, qkv_ref, grad_ref, lse_ref, mixed_ref
):
    length = qkv_ref.shape[0]
    part = qkv_ref.shape[1] // 3
    lanes = cos_ref.shape[1]
    allowed = allowed_pairs(ends_of(window, ends_ref), length)
    cosine, sine = cos_ref[...], -sin_ref[...]
    lane = lax.broadcasted_iota(jnp.int32, (1, lanes), 1)
    for group in range(part // lanes):
        at = group * lanes
        query = qkv_ref[:, at : at + lanes]
        keys = qkv_ref[:, part + at : part + at + lanes]
        values = qkv_ref[:, 2 * part + at : 2 * part + at + lanes]
        grad = grad_ref[:, at : at + lanes]
        keys_turned = keys.astype(f32).T.astype(bf16)
        subs = range(lanes // head)
        mines = [(lane >= sub * head) & (lane < (sub + 1) * head) for sub in subs]
        scores = [dot(jnp.where(m, keys, 0), query, ((1,), (1,))) for m in mines]
        probs_grads = [dot(jnp.where(m, values, 0), grad, ((1,), (1,))) for m in mines]
        probs, scores_grads = [], []
        for sub in subs:
            number = group * (lanes // head) + sub
            prob = jnp.exp(
                jnp.where(allowed, scores[sub], big_negative) - lse_ref[number : number + 1, :]
            )
            weighted = jnp.sum(prob * probs_grads[sub], axis=0, keepdims=True)
            scores_grads.append((prob * (probs_grads[sub] - weighted)).astype(bf16))
            probs.append(prob.astype(bf16))
        values_grad = jnp.concatenate(
            [dot(p, grad)[:, sub * head : (sub + 1) * head] for sub, p in enumerate(probs)], axis=1
        )
        keys_grad = jnp.concatenate(
            [dot(x, query)[:, sub * head : (sub + 1) * head] for sub, x in enumerate(scores_grads)],
            axis=1,
        )
        query_grads = [
            dot(keys_turned[sub * head : (sub + 1) * head, :], scores_grads[sub]) for sub in subs
        ]
        query_grad = jnp.concatenate(query_grads, axis=0).T * head ** (-0.5)
        mixed_ref[:, at : at + lanes] = turned(query_grad, cosine, sine).astype(bf16)
        mixed_ref[:, part + at : part + at + lanes] = turned(keys_grad, cosine, sine).astype(bf16)
        mixed_ref[:, 2 * part + at : 2 * part + at + lanes] = values_grad.astype(bf16)


def attend_back(window, ends, qkv, grad, lse, tables, head, after=()):
    kernel = functools.partial(attend_back_kernel, head, window)
    return call(kernel, [ends, *tables, qkv, grad, lse], [shape16(*qkv.shape)], 6, after)


def acts_grad_kernel(count, heads_ref, up_ref, *refs):
    mixed, hidden = stacked(refs[:count]), stacked(refs[count : 2 * count])
    normed = refs[2 * count : 3 * count]
    halves, sums = refs[3 * count : 5 * count], refs[5 * count :]
    half, width = halves[0].shape
    for ref in sums:
        ref[...] = jnp.zeros_like(ref)
    step = min(256, width)
    for at in range(0, width, step):
        here = slice(at, at + step)
        terms = dot(mixed, heads_ref[here, :], ((1,), (1,)))
        terms += dot(hidden, up_ref[here, :], ((1,), (1,)))
        for w, ref in enumerate(sums):
            term = terms[2 * w * half : 2 * (w + 1) * half]
            ref[0:1, here] = jnp.sum(
                term * normed[w][:, here].astype(f32), axis=0, keepdims=True
            )
            ref[1:2, here] = jnp.sum(term, axis=0, keepdims=True)
        for i, ref in enumerate(halves):
            ref[:, here] = terms[i * half : (i + 1) * half].astype(bf16)


def acts_grad(heads, up, mixed, hidden, normed, after=()):
    count = len(mixed)
    length, width = normed[0].shape
    outs = [shape16(length // 2, width)] * (2 * count)
    outs += [jax.ShapeDtypeStruct((8, width), f32)] * count
    kernel = functools.partial(acts_grad_kernel, count)
    outs, done = call(kernel, [heads, up, *mixed, *hidden, *normed], outs, 10, after)
    return list(zip(outs[0 : 2 * count : 2], outs[1 : 2 * count : 2])), outs[2 * count :], done


def joined_windows(refs, scratch):
    at = 0
    for ref in refs:
        rows = ref.shape[0]
        scratch[at : at + rows, :] = ref[...]
        at += rows


def halved(shape):
    return [shape16(shape.shape[0] // 2, *shape.shape[1:])] * 2


def row_grads_kernel(rows, place_ref, *refs):
    activated, attended, grads = refs[:GROUP], refs[GROUP : 2 * GROUP], refs[2 * GROUP : -6]
    *theirs, mine_ref, a_ref, b_ref, g_ref = refs[-6:]
    joined_windows(activated, a_ref)
    joined_windows(attended, b_ref)
    joined_windows(grads, g_ref)
    first = place_ref[2] == 0
    grad = g_ref[...]
    at = 0
    for ref, size in ((a_ref, mine_ref.shape[1] - rows), (b_ref, rows)):
        step = min(256, ref.shape[1])
        for start in range(0, ref.shape[1], step):
            term = dot(ref[:, start : start + step], grad, ((0,), (0,))).astype(bf16)
            for pair in range(step // (CORES * size)):
                z = start // (CORES * size) + pair
                zero = term[pair * 2 * size : (pair * 2 + 1) * size]
                one = term[(pair * 2 + 1) * size : (pair * 2 + 2) * size]
                mine_ref[z, at : at + size, :] = jnp.where(first, zero, one)
                theirs[z // 2][z % 2, at : at + size, :] = jnp.where(first, one, zero)
        at += size


def row_grads(where, steps, rows, activated, attended, grads, after=()):
    length, hidden_part = activated[0].shape
    part = attended[0].shape[1]
    width = grads[0].shape[1]
    out = shape16(steps, hidden_part // (steps * CORES) + rows, width)
    scratch = [pltpu.VMEM((GROUP * length, w), bf16) for w in (hidden_part, part, width)]
    ins = [where, *activated, *attended, *grads]
    kernel = functools.partial(row_grads_kernel, rows)
    return call(kernel, ins, [*halved(out), out], 12, after, scratch)


def column_grads_kernel(rows, sums, place_ref, *refs):
    *theirs, mine_ref, a_ref, b_ref = refs[-5:]
    steps = mine_ref.shape[0]
    columns = b_ref.shape[1]
    joined_windows(refs[:GROUP], a_ref)
    joined_windows(refs[GROUP : 2 * GROUP], b_ref)
    first = place_ref[2] == 0
    grad = b_ref[...]
    step = steps * CORES * rows
    if sums:
        refs = refs[2 * GROUP :]
        acts_sums = sum((r[0:2, :] for r in refs[1:GROUP]), refs[0][0:2, :])
        joined_sums = sum((r[0:2, :] for r in refs[GROUP + 1 : 2 * GROUP]), refs[GROUP][0:2, :])
        row = lax.broadcasted_iota(jnp.int32, (rows, 128), 0)

        def tiles(t, z, c):
            number = (t * steps + z) * CORES + c
            at, up = number * rows // 128 * 128, (z * CORES + c) * 128
            value = jnp.zeros((rows, 128), f32)
            for k, line in enumerate(
                (
                    acts_sums[0:1, at : at + 128],
                    acts_sums[1:2, at : at + 128],
                    joined_sums[0:1, at : at + 128],
                    joined_sums[1:2, up : up + 128],
                )
            ):
                value = jnp.where(row == k, line, value)
            return value.astype(bf16)

    for t in range(GROUP):
        term = dot(a_ref[:, t * step : (t + 1) * step], grad, ((0,), (0,))).astype(bf16)
        here = slice(t * rows, (t + 1) * rows)
        for z in range(steps):
            zero = term[z * 2 * rows : (z * 2 + 1) * rows]
            one = term[(z * 2 + 1) * rows : (z * 2 + 2) * rows]
            mine_ref[z, here, :columns] = jnp.where(first, zero, one)
            theirs[z // 2][z % 2, here, :columns] = jnp.where(first, one, zero)
            if sums:
                zero, one = tiles(t, z, 0), tiles(t, z, 1)
                mine_ref[z, here, columns:] = jnp.where(first, zero, one)
                theirs[z // 2][z % 2, here, columns:] = jnp.where(first, one, zero)


def column_grads(where, steps, rows, acts, grads, after=(), sums=()):
    length, width = acts[0].shape
    columns = grads[0].shape[1]
    out = shape16(steps, GROUP * rows, columns + (128 if sums else 0))
    scratch = [pltpu.VMEM((GROUP * length, w), bf16) for w in (width, columns)]
    kernel = functools.partial(column_grads_kernel, rows, bool(sums))
    return call(kernel, [where, *acts, *grads, *sums], [*halved(out), out], 12, after, scratch)


def ring_begin_kernel(steps_on, place_ref, mine_ref, low_ref, high_ref, chip_ref, *firsts):
    steps = mine_ref.shape[0]
    for z in range(steps):
        got = (low_ref, high_ref)[z // 2][z % 2]
        chip_ref[z] = (mine_ref[z].astype(f32) + got.astype(f32)).astype(bf16)
    for on, ref in zip(steps_on, firsts):
        ref[...] = chip_ref[lax.rem(place_ref[1] + on, steps)]


def ring_add_kernel(on, place_ref, chip_ref, moving_ref, out_ref):
    at = lax.rem(place_ref[1] + on, chip_ref.shape[0])
    out_ref[...] = (chip_ref[at].astype(f32) + moving_ref[...].astype(f32)).astype(bf16)


def ring_rows_kernel(place_ref, chip_ref, *refs):
    down_ref, merge_ref = refs[-2:]
    total = chip_ref[place_ref[1]].astype(f32)
    for other in refs[:-2]:
        total += other[...].astype(f32)
    size = down_ref.shape[0]
    down_ref[...] = total[:size]
    merge_ref[...] = total[size:]


def ring_columns_kernel(count, place_ref, *refs):
    outs = refs[-GROUP:]
    rows = outs[0].shape[0]
    for mask in range(GROUP):
        t = jnp.bitwise_xor(place_ref[0], mask)
        at = pl.ds(pl.multiple_of(t * rows, rows), rows)
        column = 0
        for chip, *others in (refs[:count], refs[count:-GROUP]):
            total = chip[place_ref[1], at, :].astype(f32)
            for other in others:
                total += other[at, :].astype(f32)
            width = total.shape[1]
            outs[mask][:, column : column + width] = total.astype(bf16)
            column += width


def add_halves_kernel(*refs):
    one, two, low, high, one_ref, two_ref = refs[0:2], refs[2:4], *refs[4:]
    half = low.shape[0]
    one_ref[:half] = (one[0][...].astype(f32) + low[...].astype(f32)).astype(bf16)
    one_ref[half:] = one[1][...]
    two_ref[:half] = two[0][...]
    two_ref[half:] = (two[1][...].astype(f32) + high[...].astype(f32)).astype(bf16)


def add_halves(one, two, low, high, after=()):
    outs = [shape16(2 * low.shape[0], low.shape[1])] * 2
    return call(add_halves_kernel, [*one, *two, low, high], outs, 4, after)


def summed(own, one, two):
    return stacked(own).astype(f32) + one[...].astype(f32) + two[...].astype(f32)


def finish_out_kernel(tokens_ref, small_ref, low_ref, high_ref, one_ref, two_ref, out_ref):
    total = summed([low_ref, high_ref], one_ref, two_ref)
    out_ref[...] = (tokens_ref[...].astype(f32) + total + small_ref[2:3, :]).astype(bf16)


def finish_grad_kernel(
    tokens_ref, grad_ref, small_ref, low_ref, high_ref, one_ref, two_ref, out_ref
):
    normed, inverse_std = normalised(tokens_ref[...].astype(f32))
    normed_grad = summed([low_ref, high_ref], one_ref, two_ref) * small_ref[0:1, :]
    mean = jnp.mean(normed_grad, axis=-1, keepdims=True)
    along = jnp.mean(normed_grad * normed, axis=-1, keepdims=True)
    grad = grad_ref[...].astype(f32)
    out_ref[...] = (grad + inverse_std * (normed_grad - mean - normed * along)).astype(bf16)


def finish(kernel, arrays, own, one, two, after=()):
    (out,), done = call(kernel, [*arrays, *own, one, two], [shape16(*one.shape)], 10, after)
    return out, done


def prepare_kernel(
    place_ref, ends_ref, small_ref, heads_ref, up_ref, down_ref, merge_ref, *refs
):
    outs, sem = refs[: GROUP + 1], refs[-1]
    rows = heads_ref.shape[0]
    part = heads_ref.shape[1] // 3 // GROUP
    hidden_part = up_ref.shape[1] // GROUP
    hidden_rows = down_ref.shape[0]
    copies = []

    def copy(src, dst):
        copies.append(pltpu.make_async_copy(src, dst, sem.at[len(copies)]))

    for mask in range(GROUP):
        to = jnp.bitwise_xor(place_ref[0], mask)
        for k in range(3):
            at = pl.multiple_of((k * GROUP + to) * part, part)
            copy(heads_ref.at[:, pl.ds(at, part)], outs[mask].at[:, pl.ds(k * part, part)])
        at = pl.multiple_of(to * hidden_part, hidden_part)
        copy(
            up_ref.at[:, pl.ds(at, hidden_part)],
            outs[mask].at[:, pl.ds(3 * part + 128, hidden_part)],
        )
    copy(down_ref, outs[GROUP].at[pl.ds(0, hidden_rows)])
    copy(merge_ref, outs[GROUP].at[pl.ds(hidden_rows, rows)])
    for each in copies:
        each.start()
    quarter = place_ref[3]
    row = lax.broadcasted_iota(jnp.int32, (rows, 128), 0)
    lane = lax.broadcasted_iota(jnp.int32, (rows, 128), 1)
    first = jnp.broadcast_to(small_ref[0:1, :], (rows, 128))
    extra = jnp.zeros((rows, 128), f32)
    for k in range(3):
        moved = pltpu.roll(first, lax.rem(quarter * rows + (128 - k * rows), 128), 1)
        here = (row == k) & (lane >= quarter * rows) & (lane < (quarter + 1) * rows)
        extra = jnp.where(here, moved, extra)
    extra = jnp.where(row == 3, small_ref[1:2, :], extra)
    for k in range(2):
        value = ends_ref[k]
        for i, piece in enumerate((value // 16, value % 16)):
            extra = jnp.where((row == 4) & (lane == 2 * k + i), piece.astype(f32), extra)
    extra = extra.astype(bf16)
    for mask in range(GROUP):
        outs[mask][:, 3 * part : 3 * part + 128] = extra
    for each in copies:
        each.wait()


def prepare(where, ends, small, heads_weight, up_weight, down_weight, merge_weight):
    rows, width3 = heads_weight.shape
    columns = width3 // GROUP + up_weight.shape[1] // GROUP + 128
    block = (down_weight.shape[0] + merge_weight.shape[0], down_weight.shape[1])
    far = [heads_weight, up_weight, down_weight, merge_weight]
    far = [pltpu.with_memory_space_constraint(x, pltpu.HBM) for x in far]
    return pl.pallas_call(
        prepare_kernel,
        in_specs=[spec(pltpu.SMEM)] * 2 + [spec(pltpu.VMEM)] + [spec(pltpu.HBM)] * len(far),
        out_specs=[spec(pltpu.VMEM)] * (GROUP + 1),
        out_shape=[shape16(rows, columns)] * GROUP + [shape16(*block)],
        scratch_shapes=[pltpu.SemaphoreType.DMA((4 * GROUP + 2,))],
        **settings(2),
    )(where, ends, small, *far)


def small_rows_kernel(count, place_ref, extra_ref, small_ref):
    total = extra_ref.shape[0]
    rows = total // (count * GROUP)
    row = lax.broadcasted_iota(jnp.int32, (8, 128), 0)
    per = 128 // rows
    for tile in range(small_ref.shape[1] // 128):
        value = jnp.zeros((8, 128), f32)
        for i in range(per):
            at = (tile * per + i) * rows
            value += extra_ref[at : at + 16, :].astype(f32)[:8]
        if tile < count:
            at = pl.multiple_of((place_ref[0] * count + tile) * rows, rows)
            value = jnp.where(row == 3, extra_ref[pl.ds(at, 16), :].astype(f32)[:8], value)
        small_ref[:, tile * 128 : (tile + 1) * 128] = value


def assemble_kernel(layout, steps, with_small, sources, place_ref, *refs):
    count = steps * CORES
    extra_ref = refs[-1]
    outs = refs[-1 - len(layout) - with_small : -1]
    for number, (source, part) in enumerate(sources):
        piece = refs[source] if part is None else refs[source].at[part]
        z = place_ref[1] - number // CORES
        z = jnp.where(z < 0, z + steps, z)
        c = jnp.bitwise_xor(place_ref[2], number % CORES)
        row = 0
        for (rows, masks), out in zip(layout, outs):
            width = out.shape[1]
            for mask in range(masks):
                d = jnp.bitwise_xor(place_ref[0], mask) if masks > 1 else 0
                to = pl.ds(pl.multiple_of(((d * steps + z) * CORES + c) * rows, rows), rows)
                out[to, :] = piece[row : row + rows, :width]
                if with_small:
                    extra_ref[to, :] = piece[row : row + rows, width:]
                row += rows
    if with_small:
        small_rows_kernel(count, place_ref, extra_ref, outs[-1])


def assemble(place, where, arrays, sources, layout, with_small=False, after=()):
    width = arrays[0].shape[1] - (128 if with_small else 0)
    totals = [len(sources) * r * masks for r, masks in layout]
    outs = [shape16(total, width) for total in totals]
    if with_small:
        outs.append(jax.ShapeDtypeStruct((8, totals[0]), f32))
    kernel = functools.partial(assemble_kernel, layout, place.nz, with_small, sources)
    scratch = [pltpu.VMEM((totals[0], 128), bf16)]
    return call(kernel, [where, *arrays], outs, 2, after, scratch)


def stack_kernel(*refs):
    for i, ref in enumerate(refs[:-1]):
        refs[-1][i] = ref[...]


def stack(*arrays, after=()):
    (out,), done = call(stack_kernel, list(arrays), [shape16(len(arrays), *arrays[0].shape)], 2, after)
    return out, done


def halves_kernel(x_ref, low_ref, high_ref):
    half = low_ref.shape[0]
    low_ref[...] = x_ref[:half]
    high_ref[...] = x_ref[half:]


def halves(x, after=()):
    outs = [shape16(x.shape[0] // 2, x.shape[1])] * 2
    return call(halves_kernel, [x], outs, 3, after)


def cut_kernel(one_ref, two_ref, low_ref, high_ref):
    half = low_ref.shape[0]
    low_ref[...] = one_ref[:half]
    high_ref[...] = two_ref[half:]


def cut(one, two, after=()):
    outs = [shape16(one.shape[0] // 2, one.shape[1])] * 2
    return call(cut_kernel, [one, two], outs, 2, after)


def plain_assemble(place, pieces, layout):
    steps = place.nz
    flat = [piece for pair in pieces for piece in pair]
    width = flat[0].shape[1]
    stacked_pieces = jnp.stack(flat).reshape(steps, CORES, place.no, -1, width)
    stacked_pieces = jnp.take(stacked_pieces, (place.z - np.arange(steps)) % steps, axis=0)
    stacked_pieces = jnp.take(stacked_pieces, np.arange(CORES) ^ place.c, axis=1)
    outs, row = [], 0
    for r, masks in layout:
        part = stacked_pieces[:, :, :, row : row + r * masks]
        part = part.reshape(steps, CORES, place.no, masks, r, width)
        if masks > 1:
            part = jnp.take(part, np.arange(masks) ^ place.t, axis=3)
        outs.append(part.transpose(2, 3, 0, 1, 4, 5).reshape(-1, width))
        row += r * masks
    return outs


def columns_out_kernel(place_ref, *refs):
    blocks = refs[:GROUP]
    heads_out_ref, up_out_ref, *moved_refs, hidden_ref = refs[GROUP:]
    rows = blocks[0].shape[0]
    hidden_part = up_out_ref.shape[1] // GROUP
    part = heads_out_ref.shape[1] // GROUP // 3
    total = jnp.zeros((16, 128), f32)
    for mask in range(GROUP):
        to = jnp.bitwise_xor(place_ref[0], mask)
        at = pl.multiple_of(to * hidden_part, hidden_part)
        up_out_ref[:, pl.ds(at, hidden_part)] = blocks[mask][:, :hidden_part].astype(f32)
        for k in range(3):
            at = pl.multiple_of((k * GROUP + to) * part, part)
            start = hidden_part + k * part
            heads_out_ref[:, pl.ds(at, part)] = blocks[mask][:, start : start + part].astype(f32)
        total += blocks[mask][:16, hidden_part + 3 * part :].astype(f32)
    own = blocks[0][:16, hidden_part + 3 * part :].astype(f32)
    row = lax.broadcasted_iota(jnp.int32, (16, 128), 0)
    value = jnp.where(row < 2, total, own)
    moved = pltpu.roll(value, lax.rem(128 - place_ref[3] * rows, 128), 1)
    for k, ref in enumerate(moved_refs):
        ref[...] = moved[k : k + 1, :rows]
    hidden_ref[...] = value[3:4]


def columns_out(where, blocks, hidden_part):
    rows, columns = blocks[0].shape
    outs = [
        jax.ShapeDtypeStruct((rows, GROUP * (columns - 128 - hidden_part)), f32),
        jax.ShapeDtypeStruct((rows, GROUP * hidden_part), f32),
    ] + [jax.ShapeDtypeStruct((1, n), f32) for n in (rows, rows, rows, 128)]
    return call(columns_out_kernel, [where, *blocks], outs, 4)[0]


class Place:
    def __init__(self, sizes):
        self.ndp = sizes["dp"]
        self.no = self.ndp // GROUP
        self.nf = sizes["fsdp"]
        self.nz = self.nf // CORES
        fsdp = lax.axis_index("fsdp")
        self.dp = lax.axis_index("dp")
        self.t = self.dp % GROUP
        self.z = fsdp // CORES
        self.c = fsdp % CORES
        self.outer_groups = [[o * GROUP + t for o in range(self.no)] for t in range(GROUP)]

    def send(self, x, to):
        pairs = []
        for d in range(self.ndp):
            for z in range(self.nz):
                for c in range(CORES):
                    d2, z2, c2 = to(d, z, c)
                    pairs.append(
                        (d * self.nf + z * CORES + c, d2 * self.nf + z2 * CORES + c2)
                    )
        return lax.ppermute(x, AXES, pairs)

    def swap_t(self, x, mask):
        return self.send(x, lambda d, z, c: (d ^ mask, z, c))

    def shift_z(self, x, step=1):
        return self.send(x, lambda d, z, c: (d, (z + step) % self.nz, c))

    def swap_core(self, x):
        return self.send(x, lambda d, z, c: (d, z, CORES - 1 - c))


def later(x, *after):
    return lax.optimization_barrier((x,) + after)[0]


def add(a, b):
    return a.astype(f32) + b.astype(f32)


class RingSum:
    def __init__(self, place, where, theirs, mine, *after):
        self.place, self.where, self.mine = place, where, mine
        self.got = [place.swap_core(later(x, *after)) for x in theirs]

    def run(self, kernel, arrays, outs, after):
        return call(kernel, [self.where, *arrays], outs, 6, after)

    def first(self, steps_on, after):
        block = shape16(*self.mine.shape[1:])
        outs = [shape16(*self.mine.shape)] + [block] * len(steps_on)
        kernel = functools.partial(ring_begin_kernel, steps_on)
        (self.chip, *firsts), done = self.run(kernel, [self.mine, *self.got], outs, after)
        return firsts, done

    def added(self, on, after):
        outs = [shape16(*self.moving.shape)]
        kernel = functools.partial(ring_add_kernel, on)
        (out,), done = self.run(kernel, [self.chip, self.moving], outs, after)
        return out, done

    def begin(self, *after):
        (first,), done = self.first((3,), after)
        self.moving, self.on = self.place.shift_z(first), 3
        return done

    def pass_on(self, out):
        self.moving = self.place.shift_z(out)

    def next(self, *after):
        self.on -= 1
        return self.added(self.on, after)

    def step(self, *after):
        out, done = self.next(*after)
        self.pass_on(out)
        return done

    def terms(self):
        return [self.chip, self.moving]


class PairSum(RingSum):
    def begin(self, *after):
        (far, back), done = self.first((2, 3), after)
        self.moving, self.back = self.place.shift_z(far), self.place.shift_z(back, -1)
        return done

    def step(self, *after):
        out, done = self.added(1, after)
        self.moving = self.place.shift_z(out)
        return done

    def terms(self):
        return [self.chip, self.back, self.moving]


def plain_sum(place, terms):
    terms = lax.psum_scatter(terms, "dp", scatter_dimension=0, axis_index_groups=place.outer_groups)
    theirs = lax.dynamic_index_in_dim(terms, 1 - place.c, 1, keepdims=False)
    chip = lax.dynamic_index_in_dim(terms, place.c, 1, keepdims=False)
    chip = add(chip, place.swap_core(theirs)).astype(bf16)
    moving = None
    for step in range(1, place.nz + 1):
        own = lax.dynamic_index_in_dim(chip, (place.z - step) % place.nz, 0, keepdims=False)
        moving = own if moving is None else add(place.shift_z(moving), own).astype(bf16)
    return moving.astype(f32)


def plain_gather(place, block):
    block = lax.all_gather(block, "dp", axis_index_groups=place.outer_groups, tiled=True)
    blocks = [block]
    for _ in range(place.nz - 1):
        blocks.append(place.shift_z(blocks[-1]))
    return [(b, place.swap_core(b)) for b in blocks]


def gather_windows(place, own):
    half = own.shape[0] // 2
    one, two = place.swap_t(own, 1), place.swap_t(own, 2)
    three = [place.swap_t(one[:half], 2), place.swap_t(two[half:], 1)]
    return [[own], [one], [two], three]


def sum_windows(place, terms):
    low, high = place.swap_t(terms[3][0], 2), place.swap_t(terms[3][1], 1)
    (one, two), _ = add_halves(terms[1], terms[2], low, high)
    return terms[0], place.swap_t(one, 1), place.swap_t(two, 2)


def columns(place, heads_weight, up_weight, mask):
    rows, width3 = heads_weight.shape
    part = width3 // 3 // GROUP
    hidden_part = up_weight.shape[1] // GROUP
    to = place.t ^ mask
    joint = [
        lax.dynamic_slice_in_dim(heads_weight, (k * GROUP + to) * part, part, axis=1)
        for k in range(3)
    ]
    up = lax.dynamic_slice_in_dim(up_weight, to * hidden_part, hidden_part, axis=1)
    return jnp.concatenate(joint + [up], axis=1)


def spread(vector, at, count):
    n = vector.shape[0]
    row = jnp.tile(vector.astype(f32).reshape(1, n), (1, count))
    lane = lax.broadcasted_iota(jnp.int32, row.shape, 1)
    return jnp.where(lane // n == at, row, 0.0)


def small_gather(place, norm_gain, norm_bias, down_bias, up_bias, offsets, terminal):
    here = ((place.dp * place.nz) + place.z) * CORES + place.c
    count = place.ndp * place.nf
    rows = jnp.concatenate([spread(v, here, count) for v in (norm_gain, norm_bias, down_bias)])
    fsdp = (place.dp // GROUP * place.nz + place.z) * CORES + place.c
    own = spread(up_bias, fsdp, place.no * place.nf)
    lanes = rows.shape[1]
    both = jnp.concatenate([rows, jnp.pad(own, ((0, 0), (0, lanes - own.shape[1])))])
    if place.no > 1:
        both = lax.psum(both, "dp", axis_index_groups=place.outer_groups)
    shifted = [place.shift_z(both, s) for s in range(1, place.nz)]
    both = sum(shifted, both)
    both = both + place.swap_core(both)
    ends = jnp.concatenate([offsets, terminal]).astype(f32).reshape(1, -1)
    ends = jnp.pad(ends, ((0, 0), (0, lanes - ends.shape[1])))
    group = jnp.concatenate([both[:3], ends])
    others = [place.swap_t(group, m) for m in range(1, GROUP)]
    rows = sum((o[:3] for o in others), group[:3])
    windows = offsets.shape[0]
    ends = jnp.concatenate([g[3:4, : 2 * windows] for g in [group] + others])
    return rows, both[3:4, : own.shape[1]], ends


def plain_shards(
    place,
    tokens,
    heads_weight,
    merge_weight,
    up_weight,
    up_bias,
    down_weight,
    down_bias,
    norm_gain,
    norm_bias,
    offsets,
    terminal,
    cotangent,
):
    nz, no = place.nz, place.no
    length, width = tokens.shape
    head = width // HEADS
    rows = heads_weight.shape[0]
    hidden_rows = down_weight.shape[0]
    part = width // GROUP
    hidden_part = up_weight.shape[1] // GROUP
    number = place.dp * place.nf + place.z * CORES + place.c
    tables = turn_tables(length, head, 128)
    pieces = [columns(place, heads_weight, up_weight, m) for m in range(GROUP)]
    pieces = jnp.concatenate([pieces[0]] + [place.swap_t(pieces[m], m) for m in range(1, GROUP)])
    layout = [(rows, GROUP)]
    (heads,) = plain_assemble(place, plain_gather(place, pieces[:, : 3 * part]), layout)
    (up,) = plain_assemble(place, plain_gather(place, pieces[:, 3 * part :]), layout)
    block = jnp.concatenate([down_weight, merge_weight])
    layout = [(hidden_rows, 1), (rows, 1)]
    down, merge = plain_assemble(place, plain_gather(place, block), layout)
    small, up_shift, ends = small_gather(
        place, norm_gain, norm_bias, down_bias, up_bias, offsets, terminal
    )
    up_shift = jnp.pad(up_shift, ((0, 4), (0, width - hidden_part)))
    small = jnp.concatenate([small, up_shift])
    ends = jnp.stack([jnp.floor(ends / 16.0), ends % 16.0], axis=-1).reshape(GROUP, 1, 4)
    ends = jnp.pad(ends, ((0, 0), (4, 11), (0, 124))).reshape(16 * GROUP, 128)
    windows = gather_windows(place, tokens)
    grads = gather_windows(place, cotangent)

    saved = [attend(w, ends, windows[w], heads, small, tables, head)[0] for w in range(GROUP)]
    acts, normed, attended, qkv, lse = zip(*saved)
    activated, slope = zip(*(hidden_units([a], up, small)[0][0] for a in acts))
    outs = [out_terms([activated[w]], [attended[w]], down, merge)[0][0] for w in range(GROUP)]
    block_output, _ = finish(finish_out_kernel, [tokens, small], *sum_windows(place, outs))
    (hidden_grad, attended_grad, joined_sums), _ = joined_grad(grads, down, merge, slope)
    mixed_grad, terms, acts_sums = [], [], []
    for w in range(GROUP):
        mixed = attend_back(w, ends, qkv[w], attended_grad[w], lse[w], tables, head)[0][0]
        halves, sums, _ = acts_grad(heads, up, [mixed], [hidden_grad[w]], [normed[w]])
        mixed_grad.append(mixed)
        terms += halves
        acts_sums += sums
    grad_tokens, _ = finish(
        finish_grad_kernel, [tokens, cotangent, small], *sum_windows(place, terms)
    )

    def product(left, right):
        left, right = jnp.concatenate(left), jnp.concatenate(right)
        return dot(left, right, ((0,), (0,))).astype(bf16)

    def by_place(terms):
        terms = terms.reshape(no, GROUP, nz, CORES, rows, terms.shape[1])
        return terms.transpose(0, 2, 3, 1, 4, 5)

    def by_t(summed):
        blocks = [
            lax.dynamic_index_in_dim(summed, place.t ^ m, 0, keepdims=False) for m in range(GROUP)
        ]
        arrived = [blocks[0]] + [place.swap_t(blocks[m].astype(bf16), m) for m in range(1, GROUP)]
        arrived = [a.astype(f32) for a in arrived]
        return [lax.select_n(t ^ place.t, *arrived) for t in range(GROUP)]

    flat = [h for pair in grads for h in pair]
    down_terms = product(activated, flat).reshape(no, nz, CORES, hidden_rows, width)
    merge_terms = product(attended, flat).reshape(no, nz, CORES, rows, width)
    row_total = plain_sum(place, jnp.concatenate([down_terms, merge_terms], axis=3))
    heads_by_t = by_t(plain_sum(place, by_place(product(acts, mixed_grad))))
    up_by_t = by_t(plain_sum(place, by_place(product(acts, hidden_grad))))
    grad_heads = jnp.concatenate(
        [h[:, k * part : (k + 1) * part] for k in range(3) for h in heads_by_t], axis=1
    )
    group_sums = jnp.concatenate([sum(acts_sums)[:2], sum(joined_sums)[:2, :width]])
    group_sums = group_sums + place.swap_core(group_sums)
    group_sums = lax.psum(group_sums, "dp", axis_index_groups=place.outer_groups)
    group_sums = sum((place.shift_z(group_sums, s) for s in range(1, nz)), group_sums)
    all_sums = sum((place.swap_t(group_sums, m) for m in range(1, GROUP)), group_sums)
    grad_gain, grad_bias = (
        lax.dynamic_slice_in_dim(all_sums[k], number * rows, rows) for k in range(2)
    )
    at = (place.dp // GROUP * place.nf + place.z * CORES + place.c) * hidden_rows
    return (
        block_output,
        grad_tokens,
        grad_heads,
        row_total[hidden_rows:],
        jnp.concatenate(up_by_t, axis=1),
        lax.dynamic_slice_in_dim(group_sums[3], at, hidden_rows),
        row_total[:hidden_rows],
        lax.dynamic_slice_in_dim(group_sums[2], number * rows, rows),
        grad_gain,
        grad_bias,
    )


def paced_shards(
    place,
    tokens,
    heads_weight,
    merge_weight,
    up_weight,
    up_bias,
    down_weight,
    down_bias,
    norm_gain,
    norm_bias,
    offsets,
    terminal,
    cotangent,
):
    nz = place.nz
    length, width = tokens.shape
    head = width // HEADS
    rows = heads_weight.shape[0]
    hidden_rows = down_weight.shape[0]
    part = width // GROUP
    hidden_part = up_weight.shape[1] // GROUP
    number = place.dp * place.nf + place.z * CORES + place.c
    where = jnp.stack([place.t, place.z, place.c, number % (128 // rows)]).astype(jnp.int32)
    tables = turn_tables(length, head, 128)
    send, shift, swap = place.swap_t, place.shift_z, place.swap_core

    vectors, at = 0.0, 0
    for v in (norm_gain, norm_bias, down_bias, up_bias):
        v = v.astype(f32)
        at = at if v.shape[0] < 128 else 128
        vectors += jnp.pad(v, (at, 256 - at - v.shape[0]))
        at += v.shape[0]
    *pieces, row_block = prepare(
        where,
        jnp.concatenate([offsets, terminal]),
        vectors.reshape(2, 128),
        heads_weight,
        up_weight,
        down_weight,
        merge_weight,
    )
    joint = 3 * part + 128
    arrived = [send(pieces[m], m) for m in range(1, GROUP)]
    pieces = [pieces[0]] + arrived
    joint_block = jnp.concatenate([p[:, :joint] for p in pieces])
    up_block = jnp.concatenate([p[:, joint:] for p in pieces])

    joint_blocks, up_blocks, row_blocks = [joint_block], [up_block], [row_block]
    joint_blocks.append(shift(joint_block))
    tokens_one = send(later(tokens, *arrived), 1)
    tokens_two = send(later(tokens, *arrived), 2)
    joint_blocks.append(shift(joint_blocks[1]))
    early, _ = stack(*joint_blocks[:2])
    early = swap(early)
    up_blocks.append(shift(later(up_block, joint_blocks[1])))
    joint_blocks.append(shift(joint_blocks[2]))
    (three_low, three_high), cut_done = cut(tokens_one, tokens_two, [joint_blocks[2]])
    up_blocks.append(shift(later(up_blocks[1], joint_blocks[3])))
    third, fourth = swap(joint_blocks[2]), swap(later(joint_blocks[3], cut_done))
    three_low, three_high = send(three_low, 2), send(three_high, 1)
    sources = [(0, None), (4, 0), (1, None), (4, 1), (2, None), (5, 0), (3, None), (5, 1)]
    split = [*sources[:5], (5, None), (3, None), (6, None)]
    layout = [(rows, GROUP)]
    (heads, small), done = assemble(
        place, where, [*joint_blocks, early, third, fourth], split, layout, True, [cut_done]
    )

    def attended_window(window, parts, *after):
        return attend(window, joint_block, parts, heads, small, tables, head, after)

    saved, units = [None] * GROUP, [None] * GROUP
    row_blocks.append(shift(later(row_block, joint_blocks[3])))
    grad_one, grad_two = send(later(cotangent, done), 1), send(later(cotangent, done), 2)
    saved[0], done = attended_window(0, [tokens], done, three_low, three_high)
    saved[1], done = attended_window(1, [tokens_one], done)
    up_blocks.append(shift(later(up_blocks[2], done)))
    saved[2], done = attended_window(2, [tokens_two], done)
    saved[3], done = attended_window(3, [three_low, three_high], done)
    early, done = stack(*up_blocks[:2], after=[done, row_blocks[1]])
    late, done = stack(*up_blocks[2:], after=[done])
    early, late = swap(early), swap(late)
    row_blocks.append(shift(later(row_blocks[1], done)))
    (up,), done = assemble(
        place, where, [*up_blocks, early, late], sources, layout, after=[done]
    )
    units[0:1], done = hidden_units([saved[0][0]], up, small, [done])
    (grad_low, grad_high), done = cut(grad_one, grad_two, [done])
    grad_low, grad_high = send(grad_low, 2), send(grad_high, 1)
    units[1:3], done = hidden_units([saved[1][0], saved[2][0]], up, small, [done])
    row_blocks.append(shift(later(row_blocks[2], done)))
    units[3:4], done = hidden_units([saved[3][0]], up, small, [done])
    acts, normed, attended, qkv, lse = zip(*saved)
    activated, slope = zip(*units)
    grads = [[cotangent], [grad_one], [grad_two], [grad_low, grad_high]]

    flat = [h for parts in grads for h in parts]
    early, done = stack(*row_blocks[:2], after=[done])
    early = swap(early)
    (*theirs, mine), done = row_grads(where, nz, rows, activated, attended, flat, [done])
    late, done = stack(*row_blocks[2:], after=[done])
    late = swap(late)
    row_sum = RingSum(place, where, theirs, mine, done)
    (down, merge), done = assemble(
        place,
        where,
        [*row_blocks, early, late],
        sources,
        [(hidden_rows, 1), (rows, 1)],
        after=[done],
    )

    def out_of(windows, *after):
        picked = [activated[w] for w in windows], [attended[w] for w in windows]
        return out_terms(*picked, down, merge, after)

    outs = [None] * GROUP
    outs[3:4], done = out_of([3], done)
    out_low, out_high = send(outs[3][0], 2), send(outs[3][1], 1)
    done = row_sum.begin(done)
    outs[1:3], done = out_of([1, 2], done)
    (hidden_grad, attended_grad, joined_sums), done = joined_grad(grads, down, merge, slope, [done])

    mixed_grad, terms, acts_sums = [None] * GROUP, [None] * GROUP, [None] * GROUP

    def acts_of(windows, *after):
        picked = [[x[w] for w in windows] for x in (mixed_grad, hidden_grad, normed)]
        return acts_grad(heads, up, *picked, after)

    (*theirs, mine), done = column_grads(where, nz, rows, acts, hidden_grad, [done])
    after = [done, row_sum.moving]
    (out_one, out_two), done = add_halves(outs[1], outs[2], out_low, out_high, after)
    out_one, out_two = send(out_one, 1), send(out_two, 2)
    up_sum = RingSum(place, where, theirs, mine, done)
    done = up_sum.begin(done)

    def back(w, *after):
        (mixed_grad[w],), done = attend_back(
            w, joint_block, qkv[w], attended_grad[w], lse[w], tables, head, after
        )
        return done

    done = back(3, done)
    done = row_sum.step(done)
    done = back(1, done)
    done = back(2, done)
    done = up_sum.step(done)
    terms[3:4], acts_sums[3:4], done = acts_of([3], done)
    low, high = send(terms[3][0], 2), send(terms[3][1], 1)
    done = back(0, done)
    terms[0:3], acts_sums[0:3], done = acts_of([0, 1, 2], done, out_one, out_two)
    done = up_sum.step(done)
    sums = [*acts_sums, *joined_sums]
    (*theirs, mine), done = column_grads(where, nz, rows, acts, mixed_grad, [done], sums)
    heads_sum = PairSum(place, where, theirs, mine, done)
    after = [done, row_sum.moving, up_sum.moving]
    (one, two), done = add_halves(terms[1], terms[2], low, high, after)
    one, two = send(one, 1), send(two, 2)
    done = heads_sum.begin(done)
    last_rows, done = row_sum.next(done)
    outs[0:1], done = out_of([0], done)
    block_output, done = finish(
        finish_out_kernel, [tokens, small], outs[0], out_one, out_two, [done]
    )
    done = heads_sum.step(done)
    row_sum.pass_on(later(last_rows, heads_sum.back))
    columns = hidden_part + 3 * part + 128
    blocks, done = call(
        functools.partial(ring_columns_kernel, len(up_sum.terms())),
        [where, *up_sum.terms(), *heads_sum.terms()],
        [shape16(rows, columns)] * GROUP,
        4,
        [done, heads_sum.back, one, two],
    )
    blocks = [blocks[0]] + [send(blocks[m], m) for m in range(1, GROUP)]
    grad_tokens, done = finish(
        finish_grad_kernel, [tokens, cotangent, small], terms[0], one, two, [done]
    )
    both = [jax.ShapeDtypeStruct((n, width), f32) for n in (hidden_rows, rows)]
    (grad_down, grad_merge), done = call(
        ring_rows_kernel, [where, *row_sum.terms()], both, 4, [done]
    )
    grad_heads, grad_up, *narrow = columns_out(where, blocks, hidden_part)
    grad_gain, grad_bias, grad_down_bias, grad_up_bias = (x.reshape(-1) for x in narrow)
    return (
        block_output,
        grad_tokens,
        grad_heads,
        grad_merge,
        grad_up,
        grad_up_bias,
        grad_down,
        grad_down_bias,
        grad_gain,
        grad_bias,
    )


def shards(sizes, tokens, *arrays):
    *weights, cotangent = arrays
    place = Place(sizes)
    rows, hidden_rows, part = weights[0].shape[0], weights[4].shape[0], tokens.shape[2] // GROUP
    paced = (
        (place.no, place.nz) == (1, 4)
        and rows % 16 == 0
        and 128 % rows == 0
        and hidden_rows == 128
        and part % 128 == 0
    )
    run = paced_shards if paced else plain_shards
    block_output, grad_tokens, *grads = run(place, tokens[0], *weights, cotangent[0])
    return (block_output[None], grad_tokens[None], *grads)


def solution(mesh):
    whole = P(AXES)
    return jax.shard_map(
        functools.partial(shards, dict(mesh.shape)),
        mesh=mesh,
        in_specs=(whole,) * 12,
        out_specs=(whole,) * 10,
        check_vma=False,
    )
```
